512 devices in a mesh: dp: 128 (over z, x, core), rep: 4 (over y).
Axes of the slice: x: 4, y: 4, z: 16, core: 2. Of those that a mesh axis runs over, the one named last changes fastest.
Arguments:
- hot_ids: int32 [131072, 2], P(('dp', 'rep')), may hold values from 0 to 1023
- cold_owner: int32 [262144, 1], P(('dp', 'rep')), may hold values from 0 to 127; in each aligned block of 512 rows (0 to 511, 512 to 1023, ...) at most 8 rows name the same one
- cold_offset: int32 [262144], P(('dp', 'rep')), may hold values from 0 to 511
- labels: int32 [131072], P(('dp', 'rep')), may hold values 0 or 1
- top_weight: bfloat16 [512, 1024], replicated, may hold values from -0.25 to 0.25
- out_weight: float32 [1024], replicated, may hold values from -0.5 to 0.5
- cold_table: float32 [65536, 128], P('dp'), may hold values from -6 to 6
- cold_accum: float32 [65536, 128], P('dp'), may hold values from 0.0001 to 0.01
- hot_cache: float32 [1024, 128], replicated, may hold values from -6 to 6
- hot_accum: float32 [1024, 128], replicated, may hold values from 0.01 to 1
- pending: float32 [524288, 128], P(('dp', 'rep')), may hold values from -0.3 to 0.3
- refresh_blocks: int32 [3], replicated, may hold values from 0 to 7, as said below
- block_clock: int32 [8], replicated, may hold values from 0 to 8
Outputs:
- cold_table_new: float32 [65536, 128], P('dp')
- cold_accum_new: float32 [65536, 128], P('dp')
- hot_cache_new: float32 [1024, 128], replicated
- hot_accum_new: float32 [1024, 128], replicated
- pending_new: float32 [524288, 128], P(('dp', 'rep'))
- top_grad: float32 [512, 1024], P(('dp', 'rep'))
- out_grad: float32 [1024], replicated
The draws below stay inside these ranges and needn't reach their ends.
Inputs may be any that keep to these rules, and one draw needn't show every extreme that they name: `cold_owner`: within the lookups of one device (512 rows), no owner is named more than 8 times. `refresh_blocks`: the block numbers are distinct.
All inputs are finite; a program needn't handle non-finite values. No bound on the sum of `labels` on one device may be relied on, other than what follows from the above.
Results may differ from the reference program's by a relative error of at most 0.00165.
The reference program's roundings to bfloat16 on the way (of `hot_rows`, `cold_rows`, `inputs`, `hidden`, `dhidden` and `dinputs`) count: a program that leaves them out, or rounds other values in their place, can miss the bound.
Values may be sent and summed in bfloat16 or wider, within the bound.
No kernel may reach another device: no remote copies, remote signals or barrier semaphores. Data moves between devices by JAX's collectives and lax.ppermute only.
A program may use at most 64 MiB of HBM per device.

```python
import math
import jax
import jax.numpy as jnp
import numpy as np
from jax import lax

E = 128
H = 1024
FH = 2
FC = 2
B_DEV = 256
OWN_ROWS = 512
BLOCK = 128
HBLK = 8
NREF = 3
HOT = 1024
CAP = 8
SAMPLES = 131072
N_DP = 128
N_REP = 4


def draw_refresh_blocks(key, part):
    shuffled = jax.random.permutation(jax.random.fold_in(key, 41), HBLK)
    return shuffled[:NREF].astype(jnp.int32)


def place_ends(drawn, own_key, smallest, high):
    dims = drawn.shape
    spot = [jax.random.randint(jax.random.fold_in(own_key, axis), (), 0, dims[axis]) for axis in range(len(dims))]
    drawn = drawn.at[tuple(spot)].set(smallest)
    longest = dims.index(max(dims))
    spot[longest] = (spot[longest] + 1) % dims[longest]
    return drawn.at[tuple(spot)].set(high)


def level_of(rng, shape, cuts, low, high):
    factor_of = 1.0
    for dim, parts in cuts:
        heights = jax.random.uniform(jax.random.fold_in(jax.random.fold_in(rng, 6), dim), (parts,), jnp.float32, low / len(cuts), high / len(cuts))
        factor_of = factor_of * jnp.repeat(jnp.exp(heights), shape[dim] // parts).reshape((-1,) + (1,) * (len(shape) - 1 - dim))
    return factor_of


def rank_bounds(number_of, skew):
    weights = [(1 << 20) // math.isqrt(standing ** skew) + 1 for standing in range(1, number_of + 1)]
    spread = 1 + sum(weights) // (1 << 30)
    return np.cumsum(np.array([max(1, weight // spread) for weight in weights]))


def ranked_ids(rng, shape, count, skew):
    table = rank_bounds(count, skew)
    pick = jax.random.randint(jax.random.fold_in(rng, 1), shape, 0, int(table[count - 1]))
    grade = jnp.searchsorted(jnp.asarray(table, jnp.int32), pick, side="right")
    return jax.random.permutation(jax.random.fold_in(rng, 2), count)[grade].astype(jnp.int32)


def shared_out(rng, own, number, rows, count, top, most, skew):
    ranking = jax.random.permutation(rng, count)
    crowded, usual = shares(count, rows * top, most, skew, True), shares(count, rows * top, most, skew, False)
    places = jnp.arange(count)

    def named(tallies, offset_by):
        used = int((tallies > 0).sum())
        fixed = max(1, used // 4)
        passed = fixed + (places - fixed + offset_by * (used - fixed)) % max(1, count - fixed)
        return jnp.zeros((count,), jnp.int32).at[ranking[jnp.where(places < fixed, places, passed)]].set(jnp.asarray(tallies, jnp.int32))

    tallies = jnp.where(number % 4 == 0, named(crowded, number // 4), named(usual, number - number // 4 - 1))
    mixed = jax.random.permutation(jax.random.fold_in(own, 3), count)
    giver, receiver = mixed[0:count // 2 * 2:2], mixed[1:count // 2 * 2:2]
    margin = jnp.minimum(tallies[giver] - 1, most - tallies[receiver]) // 2
    margin = jnp.where((giver == ranking[0]) | (receiver == ranking[0]) | (tallies[receiver] == 0), 0, jnp.maximum(margin, 0))
    passed = jax.random.randint(jax.random.fold_in(own, 4), (count // 2,), 0, 1 << 20) % (margin + 1)
    tallies = tallies.at[giver].add(-passed).at[receiver].add(passed)
    items = jnp.searchsorted(jnp.cumsum(tallies), jnp.arange(rows * top), side="right").astype(jnp.int32)
    listing = items.reshape(top, rows).T
    listing = listing[jax.random.permutation(jax.random.fold_in(own, 1), rows)]
    offset_by = jax.random.randint(jax.random.fold_in(own, 2), (rows, 1), 0, top)
    return jnp.take_along_axis(listing, (jnp.arange(top)[None, :] + offset_by) % top, axis=1)


def shares(count, total, reach, skew, full):
    loads = [(1 << 20) // math.isqrt(rank ** skew) + 1 for rank in range(1, count + 1)]
    largest = reach if full else min(reach, max(-(-total // count), total * loads[0] // sum(loads)))
    least = 1 if total - largest >= count - 1 else 0
    holding, surplus = [largest] + [least] * (count - 1), total - largest - least * (count - 1)
    while surplus > 0:
        free = [i for i in range(1, count) if holding[i] < largest] or [i for i in range(1, count) if holding[i] < reach]
        pool, remaining = sum([loads[i] for i in free]), surplus
        for i in free:
            extra = min(reach - holding[i], max(1, remaining * loads[i] // pool), surplus)
            holding[i] = holding[i] + extra
            surplus = surplus - extra
    return np.array(holding)


def normal_values(own_key, dims, scale, limit, cuts=(), kind=jnp.bfloat16):
    factor_of = level_of(own_key, dims, cuts, -0.22, 0.18) if cuts else 1.0
    array = jax.random.normal(own_key, dims, jnp.float32) * scale * factor_of
    return jnp.minimum(jnp.maximum(array, -limit), limit).astype(kind)


def setup_inputs(seed: int = 0) -> dict:
    key_of = jax.random.split(jax.random.key(seed), 14)
    hot_ids = place_ends(ranked_ids(key_of[0], (SAMPLES, FH), HOT, 2), jax.random.fold_in(key_of[0], 3), 0, HOT - 1).astype(jnp.int32)
    cold_owner_keys = jax.random.split(jax.random.fold_in(key_of[1], 1), (SAMPLES * FC) // (B_DEV * FC))
    cold_owner_turns = jax.random.permutation(jax.random.fold_in(key_of[1], 3), (SAMPLES * FC) // (B_DEV * FC))
    cold_owner = jax.vmap(lambda own, number: shared_out(jax.random.fold_in(key_of[1], 2), own, number, B_DEV * FC, N_DP, 1, CAP, 2))(cold_owner_keys, cold_owner_turns).reshape((SAMPLES * FC, 1))
    cold_offset = place_ends(jax.random.randint(key_of[2], (SAMPLES * FC,), 0, OWN_ROWS), jax.random.fold_in(key_of[2], 1), 0, OWN_ROWS - 1).astype(jnp.int32)
    labels = place_ends((jax.random.randint(key_of[3], (SAMPLES,), 0, 2) < 1).astype(jnp.int32), jax.random.fold_in(key_of[3], 1), 0, 1)
    top_weight = normal_values(key_of[4], ((FH + FC) * E, H), ((FH + FC) * E) ** -0.5, 0.25)
    out_weight = normal_values(key_of[5], (H,), (H // 8) ** -0.5, 0.5, (), jnp.float32)
    cold_table = normal_values(key_of[6], (N_DP * OWN_ROWS, E), 1.0, 6.0, ((0, 128),), jnp.float32)
    cold_accum = jnp.clip(jnp.exp(math.log(0.01) - 4.6051702 * jax.random.uniform(key_of[7], (N_DP * OWN_ROWS, E), jnp.float32) ** level_of(key_of[7], (N_DP * OWN_ROWS, E), ((0, 128),), -0.2, 0.2)), 0.0001, 0.01)
    hot_cache = normal_values(key_of[8], (HOT, E), 1.0, 6.0, (), jnp.float32)
    hot_accum = jnp.clip(jnp.exp(jax.random.uniform(key_of[9], (HOT, E), jnp.float32, math.log(0.01), math.log(1.0))), 0.01, 1.0)
    pending = normal_values(key_of[10], (N_DP * N_REP * HOT, E), 0.05, 0.3, ((0, 512),), jnp.float32)
    refresh_blocks = draw_refresh_blocks(jax.random.fold_in(key_of[13], 71), 0)
    block_clock = place_ends(jax.random.randint(key_of[12], (HBLK,), 0, 9), jax.random.fold_in(key_of[12], 1), 0, 8).astype(jnp.int32)
    return dict(hot_ids=hot_ids, cold_owner=cold_owner, cold_offset=cold_offset, labels=labels, top_weight=top_weight, out_weight=out_weight, cold_table=cold_table, cold_accum=cold_accum, hot_cache=hot_cache, hot_accum=hot_accum, pending=pending, refresh_blocks=refresh_blocks, block_clock=block_clock)


step_size = 0.5
epsilon = 1e-08

def adagrad(table_rows, accum_rows, gradient):
    accum_next = accum_rows + gradient * gradient
    return (table_rows - step_size * gradient / (jnp.sqrt(accum_next) + epsilon), accum_next)

def reference(hot_ids, cold_owner, cold_offset, labels, top_weight, out_weight, cold_table, cold_accum, hot_cache, hot_accum, pending, refresh_blocks, block_clock):
    devices = N_DP * N_REP
    samples = hot_ids.shape[0]
    width = hot_cache.shape[1]
    hot_rows = hot_cache[hot_ids].astype(jnp.bfloat16)
    global_rows = (cold_owner[:, 0] * OWN_ROWS + cold_offset).astype(jnp.int32)
    cold_rows = cold_table[global_rows].astype(jnp.bfloat16).reshape(samples, FC, width)
    inputs = jnp.concatenate([hot_rows, cold_rows], axis=1).reshape(samples, (FH + FC) * width)
    groups = N_DP
    inputs_grouped = inputs.reshape(groups, samples // groups, (FH + FC) * width)
    labels_grouped = labels.reshape(groups, samples // groups).astype(jnp.float32)

    def per_group(carry, pieces):
        block_inputs, block_labels = pieces
        preact = jnp.dot(block_inputs, top_weight, preferred_element_type=jnp.float32)
        hidden = jax.nn.silu(preact).astype(jnp.bfloat16)
        hidden_wide = hidden.astype(jnp.float32)
        logits = jnp.dot(hidden_wide, out_weight, precision=lax.Precision.HIGHEST)
        errors = jax.nn.sigmoid(logits) - block_labels
        gates = jax.nn.sigmoid(preact)
        slope = gates * (1.0 + preact * (1.0 - gates))
        dhidden = (errors[:, None] * out_weight[None, :] * slope).astype(jnp.bfloat16)
        weight_term = lax.dot_general(block_inputs, dhidden, (((0,), (0,)), ((), ())), preferred_element_type=jnp.float32)
        head_term = jnp.dot(errors, hidden_wide, precision=lax.Precision.HIGHEST)
        dinputs = lax.dot_general(dhidden, top_weight, (((1,), (1,)), ((), ())), preferred_element_type=jnp.float32).astype(jnp.bfloat16)
        return ((carry[0] + weight_term, carry[1] + head_term), dinputs)
    start = (jnp.zeros(top_weight.shape, jnp.float32), jnp.zeros(out_weight.shape, jnp.float32))
    totals, dinputs = lax.scan(per_group, start, (inputs_grouped, labels_grouped))
    top_grad, out_grad = totals
    dinputs = dinputs.reshape(samples, FH + FC, width)
    hot_dx = dinputs[:, :FH].reshape(samples * FH, width).astype(jnp.float32)
    cold_dx = dinputs[:, FH:].reshape(samples * FC, width).astype(jnp.float32)
    cold_grad = jnp.zeros(cold_table.shape, jnp.float32).at[global_rows].add(cold_dx)
    cold_table_new, cold_accum_new = adagrad(cold_table, cold_accum, cold_grad)
    device_of = (jnp.arange(samples) // (samples // devices)).astype(jnp.int32)
    hot_index = (device_of[:, None] * HOT + hot_ids).astype(jnp.int32).reshape(-1)
    hot_grad = jnp.zeros(pending.shape, jnp.float32).at[hot_index].add(hot_dx)
    carried = (pending + hot_grad).reshape(devices, HBLK, BLOCK, width)
    picked = lax.optimization_barrier(jnp.sum(carried[:, refresh_blocks], axis=0))
    divisors = 1.0 + block_clock[refresh_blocks].astype(jnp.float32)
    flush = picked / divisors[:, None, None]
    cache_blocks = hot_cache.reshape(HBLK, BLOCK, width)
    accum_blocks = hot_accum.reshape(HBLK, BLOCK, width)
    cache_part, accum_part = adagrad(cache_blocks[refresh_blocks], accum_blocks[refresh_blocks], flush)
    hot_cache_new = cache_blocks.at[refresh_blocks].set(cache_part).reshape(HOT, width)
    hot_accum_new = accum_blocks.at[refresh_blocks].set(accum_part).reshape(HOT, width)
    pending_new = carried.at[:, refresh_blocks].set(0.0).reshape(devices * HOT, width)
    return (cold_table_new, cold_accum_new, hot_cache_new, hot_accum_new, pending_new, top_grad, out_grad)
```

```python
import jax
import jax.numpy as jnp
from jax import lax
from jax.experimental import pallas as pl
from jax.experimental.pallas import tpu as pltpu
from jax.sharding import Mesh
from jax.sharding import PartitionSpec as P

BLOCK = 128
SLOTS = 8
DP = ("dp_0", "dp_1", "dp_2")
DP_REP = ("dp_0", "dp_1", "dp_2", "rep")
PLANE = ("dp_2", "rep", "dp_1")

step_size = 0.5
epsilon = 1e-08

F32 = jnp.float32
BF16 = jnp.bfloat16
EXACT = lax.Precision.HIGHEST
VMEM = pl.BlockSpec(memory_space=pltpu.VMEM)
SMEM = pl.BlockSpec(memory_space=pltpu.SMEM)


def call(kernel, outs, args, smem=0, scratch=(), flops=10**8, moved=10**6):
    shapes = [jax.ShapeDtypeStruct(s, d) for s, d in outs]
    return pl.pallas_call(
        kernel,
        out_shape=shapes,
        in_specs=[SMEM] * smem + [VMEM] * (len(args) - smem),
        out_specs=[VMEM] * len(outs),
        scratch_shapes=[pltpu.VMEM(s, d) for s, d in scratch],
        compiler_params=pltpu.CompilerParams(vmem_limit_bytes=40 * 2**20),
        cost_estimate=pl.CostEstimate(flops=flops, bytes_accessed=moved, transcendentals=0),
    )(*args)


def iota(shape, dim):
    return lax.broadcasted_iota(jnp.int32, shape, dim)


def iota_f(shape, dim):
    return iota(shape, dim).astype(F32)


def ones_where(mask):
    return jnp.where(mask, 1.0, 0.0).astype(BF16)


def column_of(row, eye):
    return jnp.sum(jnp.where(eye, row, 0.0), axis=1, keepdims=True)


def dot(a, b, precision=None):
    return jnp.dot(a, b, preferred_element_type=F32, precision=precision)


def dot_t(a, b):
    return lax.dot_general(a, b, (((1,), (1,)), ((), ())), preferred_element_type=F32)


def requests_kernel(owner_ref, offset_ref, request_ref, target_ref):
    square = (BLOCK, BLOCK)
    eye = iota(square, 0) == iota(square, 1)
    groups = owner_ref.shape[0]
    lookups = groups * BLOCK
    owner = owner_ref[...].astype(F32)
    offset = offset_ref[...].astype(F32)
    rows = [owner[s : s + 1, :] for s in range(groups)]
    owner_col = jnp.concatenate([column_of(row, eye) for row in rows], axis=0)
    offset_col = jnp.concatenate([column_of(offset[s : s + 1, :], eye) for s in range(groups)], axis=0)
    lane = iota_f((lookups, BLOCK), 1)
    named = owner_col == lane
    before = ones_where(iota((lookups, lookups), 0) > iota((lookups, lookups), 1))
    earlier = dot(before, ones_where(named))
    rank = jnp.sum(jnp.where(named, earlier, 0.0), axis=1, keepdims=True)
    target_ref[...] = jnp.broadcast_to(owner_col * SLOTS + rank, (lookups, BLOCK))
    placed = jnp.where(rank == lane, offset_col, 0.0)
    sublane = iota_f(square, 0)
    named_t = jnp.concatenate([jnp.where(sublane == row, 1.0, 0.0) for row in rows], axis=1)
    request_ref[...] = dot(named_t, placed, EXACT)


def rows_kernel(asked_ref, table_ref, rows_ref):
    count = rows_ref.shape[0]
    row, lane = iota((count, BLOCK), 0), iota((count, BLOCK), 1)
    spread = dot(jnp.where(row // SLOTS == lane, 1.0, 0.0), asked_ref[...], EXACT)
    wanted = jnp.sum(jnp.where(row % SLOTS == lane, spread, 0.0), axis=1, keepdims=True)
    chosen = ones_where(wanted == iota_f((count, table_ref.shape[0]), 1))
    rows_ref[...] = dot(chosen, table_ref[...].astype(BF16)).astype(BF16)


def masks_kernel(target_ref, hot_ref, cache_ref, asked_ref, take_ref, put_ref, hot_in_ref, hot_put_ref, owned_ref):
    square = (BLOCK, BLOCK)
    eye = iota(square, 0) == iota(square, 1)
    slots, lookups = put_ref.shape
    feats = hot_ref.shape[0]
    samples = hot_ref.shape[1]
    lane = iota_f((samples, BLOCK), 1)
    slot = iota_f((slots, BLOCK), 0)
    for k in range(feats):
        mine = target_ref[pl.ds(k, samples, stride=feats), :]
        for b in range(slots // BLOCK):
            take_ref[k * samples : (k + 1) * samples, b * BLOCK : (b + 1) * BLOCK] = ones_where(
                mine == lane + float(b * BLOCK)
            )
        for h in range(samples // BLOCK):
            at = k * samples + h * BLOCK
            row = jnp.sum(jnp.where(eye, mine[h * BLOCK : (h + 1) * BLOCK, :], 0.0), axis=0, keepdims=True)
            put_ref[:, at : at + BLOCK] = ones_where(slot == row)
    cache = cache_ref[...].astype(BF16)
    hot = hot_ref[...].astype(F32)
    hot_count = cache.shape[0]
    hot_row = iota_f((hot_count, BLOCK), 0)
    hot_lane = iota_f((BLOCK, hot_count), 1)
    for k in range(feats):
        for h in range(samples // BLOCK):
            at = k * samples + h * BLOCK
            row = hot[k : k + 1, h * BLOCK : (h + 1) * BLOCK]
            hot_put_ref[:, at : at + BLOCK] = ones_where(hot_row == row)
            chosen = ones_where(column_of(row, eye) == hot_lane)
            hot_in_ref[h * BLOCK : (h + 1) * BLOCK, k * BLOCK : (k + 1) * BLOCK] = dot(chosen, cache).astype(BF16)
    source, line = iota((BLOCK, slots), 0), iota((BLOCK, slots), 1)
    spread = dot(asked_ref[...], jnp.where(source == line % SLOTS, 1.0, 0.0), EXACT)
    wanted = jnp.sum(jnp.where(source == line // SLOTS, spread, 0.0), axis=0, keepdims=True)
    owned_ref[...] = ones_where(iota_f(owned_ref.shape, 0) == wanted)


def layer_kernel(
    returned_ref, take_ref, put_ref, hot_in_ref, weight_ref, out_weight_ref, labels_ref,
    outgoing_ref, inputs_ref, dhidden_ref, hot_dx_ref, head_ref,
):
    square = (BLOCK, BLOCK)
    eye = iota(square, 0) == iota(square, 1)
    samples = hot_in_ref.shape[0]
    width = BLOCK
    cold = dot(take_ref[...], returned_ref[...]).astype(BF16)
    inputs = jnp.concatenate([hot_in_ref[...], cold[:samples], cold[samples:]], axis=1)
    inputs_ref[...] = inputs
    weight = weight_ref[...]
    out_weight = out_weight_ref[...]
    preact = dot(inputs, weight)
    gates = jax.nn.sigmoid(preact)
    hidden = (preact * gates).astype(BF16).astype(F32)
    logits = jnp.sum(hidden * out_weight, axis=1, keepdims=True)
    labels = labels_ref[...].astype(F32)
    label = jnp.concatenate([column_of(labels[h : h + 1, :], eye) for h in range(samples // BLOCK)], axis=0)
    errors = jax.nn.sigmoid(logits) - label
    slope = gates * (1.0 + preact * (1.0 - gates))
    dhidden = (errors * out_weight * slope).astype(BF16)
    dhidden_ref[...] = dhidden
    dinputs = dot_t(dhidden, weight).astype(BF16)
    cold_dx = jnp.concatenate([dinputs[:, 2 * width : 3 * width], dinputs[:, 3 * width :]], axis=0)
    outgoing_ref[...] = dot(put_ref[...], cold_dx).astype(BF16)
    hot_dx_ref[:samples, :] = dinputs[:, :width]
    hot_dx_ref[samples:, :] = dinputs[:, width : 2 * width]
    head = jnp.sum(errors * hidden, axis=0, keepdims=True)
    for b in range(head_ref.shape[0]):
        head_ref[b : b + 1, :] = head[:, b * BLOCK : (b + 1) * BLOCK]


def half_of_top(core, inputs, dhidden):
    shape = (inputs.shape[1] // 2, inputs.shape[1])
    line = iota(shape, 0)
    row = (line & 15) * 32 + ((line >> 4) & 3) * 8 + core * 4 + (line >> 6)
    ordered = dot_t(ones_where(row == iota(shape, 1)), inputs).astype(BF16)
    return dot(ordered, dhidden)


def send_kernel(
    core_ref, refresh_ref, inputs_ref, dhidden_ref, hot_put_ref, hot_dx_ref, head_ref, pending_ref,
    send_ref, picked_ref, pending_new_ref,
):
    pending_new_ref[...] = pending_ref[...] + dot(hot_put_ref[...], hot_dx_ref[...])
    count = refresh_ref.shape[0]
    blocks = [pl.ds(pl.multiple_of(refresh_ref[i] * BLOCK, BLOCK), BLOCK) for i in range(count)]
    for i, at in enumerate(blocks):
        picked_ref[i * BLOCK : (i + 1) * BLOCK, :] = pending_new_ref[at, :]
    end = count * BLOCK
    picked_ref[end : end + 8, :] = head_ref[...]
    picked_ref[end + 8 :, :] = jnp.zeros((picked_ref.shape[0] - end - 8, BLOCK), F32)
    for at in blocks:
        pending_new_ref[at, :] = jnp.zeros((BLOCK, BLOCK), F32)
    other = 1 - core_ref[0]
    wide = dhidden_ref.shape[1]
    half = send_ref.shape[0]
    send_ref[:, :wide] = half_of_top(other, inputs_ref[...], dhidden_ref[...])
    send_ref[:, wide:] = picked_ref[pl.ds(pl.multiple_of(other * half, half), half), :]


def pair_kernel(core_ref, inputs_ref, dhidden_ref, picked_ref, received_ref, sum_ref):
    mine = core_ref[0]
    wide = dhidden_ref.shape[1]
    half = sum_ref.shape[0]
    sum_ref[:, :wide] = half_of_top(mine, inputs_ref[...], dhidden_ref[...]) + received_ref[:, :wide]
    sum_ref[:, wide:] = picked_ref[pl.ds(pl.multiple_of(mine * half, half), half), :] + received_ref[:, wide:]


def plane_kernel(parts_ref, out_ref):
    total = parts_ref[0]
    for i in range(1, parts_ref.shape[0]):
        total = total + parts_ref[i]
    wide = total.shape[1] - BLOCK
    tall = wide // BLOCK
    for b in range(tall):
        out_ref[:, b, :] = total[:, b * BLOCK : (b + 1) * BLOCK]
    for z in range(out_ref.shape[0]):
        out_ref[z, tall:, :] = total[:, wide:]


def column_kernel(parts_ref, top_ref, copies_ref):
    total = parts_ref[0]
    for i in range(1, parts_ref.shape[0]):
        total = total + parts_ref[i]
    tall = top_ref.shape[0]
    top_ref[...] = total[:tall]
    for i in range(copies_ref.shape[0]):
        copies_ref[i] = total[tall:]


def adagrad(table_rows, accum_rows, gradient):
    accum_next = accum_rows + gradient * gradient
    return (table_rows - step_size * gradient / (jnp.sqrt(accum_next) + epsilon), accum_next)


def hot_kernel(refresh_ref, clock_ref, sums_ref, cache_ref, accum_ref, cache_new_ref, accum_new_ref, out_grad_ref):
    cache_new_ref[...] = cache_ref[...]
    accum_new_ref[...] = accum_ref[...]
    count = refresh_ref.shape[0]
    for i in range(count):
        block = refresh_ref[i]
        at = pl.ds(pl.multiple_of(block * BLOCK, BLOCK), BLOCK)
        flush = sums_ref[i * BLOCK : (i + 1) * BLOCK, :] / (1.0 + clock_ref[block].astype(F32))
        cache_next, accum_next = adagrad(cache_ref[at, :], accum_ref[at, :], flush)
        cache_new_ref[at, :] = cache_next
        accum_new_ref[at, :] = accum_next
    out_grad_ref[...] = sums_ref[count * BLOCK : count * BLOCK + 8, :]


def cold_kernel(owned_ref, incoming_ref, grad_ref):
    grad_ref[...] = dot(owned_ref[...], incoming_ref[...])


def update_kernel(own_ref, one_ref, two_ref, three_ref, table_ref, accum_ref, table_new_ref, accum_new_ref):
    grad = (own_ref[...] + one_ref[...]) + (two_ref[...] + three_ref[...])
    table_next, accum_next = adagrad(table_ref[...], accum_ref[...], grad)
    table_new_ref[...] = table_next
    accum_new_ref[...] = accum_next


def swap(x, axis):
    return lax.all_to_all(x, axis, split_axis=0, concat_axis=0, tiled=True)


def local(
    hot_ids,
    cold_owner,
    cold_offset,
    labels,
    top_weight,
    out_weight,
    cold_table,
    cold_accum,
    hot_cache,
    hot_accum,
    pending,
    refresh_blocks,
    block_clock,
):
    samples, feats = hot_ids.shape
    lookups = cold_offset.shape[0]
    own_rows, width = cold_table.shape
    hot_count = hot_cache.shape[0]
    inputs_width, hidden_width = top_weight.shape
    owners = lax.axis_size(DP)
    slots = owners * SLOTS
    groups = lookups // BLOCK
    core = lax.axis_index("dp_2").astype(jnp.int32).reshape(1)

    request, target = call(
        requests_kernel,
        [((owners, BLOCK), F32), ((lookups, BLOCK), F32)],
        (cold_owner.reshape(groups, BLOCK), cold_offset.reshape(groups, BLOCK)),
    )
    asked = swap(request.reshape(owners, 1, BLOCK), DP).reshape(owners, BLOCK)
    (found,) = call(rows_kernel, [((slots, width), BF16)], (asked, cold_table))
    returned = swap(found.reshape(owners, SLOTS, width), DP).reshape(slots, width)
    take, put, hot_in, hot_put, owned = call(
        masks_kernel,
        [
            ((lookups, slots), BF16),
            ((slots, lookups), BF16),
            ((samples, feats * width), BF16),
            ((hot_count, samples * feats), BF16),
            ((own_rows, slots), BF16),
        ],
        (target, hot_ids.T, hot_cache, asked),
    )
    outgoing, inputs, dhidden, hot_dx, head = call(
        layer_kernel,
        [
            ((slots, width), BF16),
            ((samples, inputs_width), BF16),
            ((samples, hidden_width), BF16),
            ((samples * feats, width), BF16),
            ((8, BLOCK), F32),
        ],
        (returned, take, put, hot_in, top_weight, out_weight.reshape(1, hidden_width), labels.reshape(2, BLOCK)),
    )
    incoming = swap(outgoing.reshape(owners, SLOTS, width), DP).reshape(slots, width)

    half = inputs_width // 2
    broad = hidden_width + BLOCK
    send, picked, pending_new = call(
        send_kernel,
        [((half, broad), F32), ((inputs_width, BLOCK), F32), ((hot_count, width), F32)],
        (core, refresh_blocks, inputs, dhidden, hot_put, hot_dx, head, pending),
        smem=2,
    )
    received = lax.ppermute(send, "dp_2", [(0, 1), (1, 0)])
    (paired,) = call(pair_kernel, [((half, broad), F32)], (core, inputs, dhidden, picked, received), smem=1)
    near = lax.axis_size(("rep", "dp_1"))
    far = lax.axis_size("dp_0")
    plane = swap(paired.reshape(near, far, broad), ("rep", "dp_1"))
    tall = hidden_width // BLOCK
    (columns,) = call(plane_kernel, [((far, tall + far, BLOCK), F32)], (plane,))
    columns = swap(columns, "dp_0")
    top, copies = call(
        column_kernel, [((tall, BLOCK), F32), ((2 * near, far, BLOCK), F32)], (columns,)
    )
    sums = swap(copies, PLANE).reshape(2 * near * far, BLOCK)

    (grad,) = call(cold_kernel, [((own_rows, width), F32)], (owned, incoming))
    others = [lax.ppermute(grad, "rep", [(i, i ^ d) for i in range(4)]) for d in (1, 2, 3)]
    cold_table_new, cold_accum_new = call(
        update_kernel, [((own_rows, width), F32)] * 2, (grad, *others, cold_table, cold_accum)
    )
    hot_cache_new, hot_accum_new, out_grad = call(
        hot_kernel,
        [((hot_count, width), F32)] * 2 + [((8, BLOCK), F32)],
        (refresh_blocks, block_clock, sums, hot_cache, hot_accum),
        smem=2,
    )
    return (
        cold_table_new,
        cold_accum_new,
        hot_cache_new,
        hot_accum_new,
        pending_new,
        top.reshape(1, hidden_width),
        out_grad.reshape(hidden_width),
    )


def solution(mesh):
    split = Mesh(mesh.devices.reshape(16, 4, 2, mesh.shape["rep"]), ("dp_0", "dp_1", "dp_2", "rep"))
    in_specs = (
        P(DP_REP, None),
        P(DP_REP, None),
        P(DP_REP),
        P(DP_REP),
        P(),
        P(),
        P(DP, None),
        P(DP, None),
        P(),
        P(),
        P(DP_REP, None),
        P(),
        P(),
    )
    out_specs = (P(DP, None), P(DP, None), P(), P(), P(DP_REP, None), P(DP_REP, None), P())
    return jax.shard_map(local, mesh=split, in_specs=in_specs, out_specs=out_specs, check_vma=False)
```

```python
import jax
import jax.numpy as jnp
from jax import lax
from jax.experimental import pallas as pl
from jax.experimental.pallas import tpu as pltpu
from jax.sharding import Mesh
from jax.sharding import PartitionSpec as P

BLOCK = 128
SLOTS = 8
DP = ("dp_0", "dp_1", "dp_2")
DP_REP = ("dp_0", "dp_1", "dp_2", "rep")
PLANE = ("dp_2", "rep", "dp_1")

step_size = 0.5
epsilon = 1e-08

F32 = jnp.float32
BF16 = jnp.bfloat16
EXACT = lax.Precision.HIGHEST
VMEM = pl.BlockSpec(memory_space=pltpu.VMEM)
SMEM = pl.BlockSpec(memory_space=pltpu.SMEM)


def call(kernel, outs, args, smem=0, scratch=(), flops=10**8, moved=10**6):
    shapes = [jax.ShapeDtypeStruct(s, d) for s, d in outs]
    return pl.pallas_call(
        kernel,
        out_shape=shapes,
        in_specs=[SMEM] * smem + [VMEM] * (len(args) - smem),
        out_specs=[VMEM] * len(outs),
        scratch_shapes=[pltpu.VMEM(s, d) for s, d in scratch],
        compiler_params=pltpu.CompilerParams(vmem_limit_bytes=16 * 2**20),
        cost_estimate=pl.CostEstimate(flops=flops, bytes_accessed=moved, transcendentals=0),
    )(*args)


def iota(shape, dim):
    return lax.broadcasted_iota(jnp.int32, shape, dim)


def iota_f(shape, dim):
    return iota(shape, dim).astype(F32)


def ones_where(mask):
    return jnp.where(mask, 1.0, 0.0).astype(BF16)


def column_of(row, eye):
    return jnp.sum(jnp.where(eye, row, 0.0), axis=1, keepdims=True)


def dot(a, b, precision=None):
    return jnp.dot(a, b, preferred_element_type=F32, precision=precision)


def dot_t(a, b):
    return lax.dot_general(a, b, (((1,), (1,)), ((), ())), preferred_element_type=F32)


def requests_kernel(owner_ref, offset_ref, request_ref, target_ref):
    square = (BLOCK, BLOCK)
    eye = iota(square, 0) == iota(square, 1)
    groups = owner_ref.shape[0]
    lookups = groups * BLOCK
    owner = owner_ref[...].astype(F32)
    offset = offset_ref[...].astype(F32)
    rows = [owner[s : s + 1, :] for s in range(groups)]
    owner_col = jnp.concatenate([column_of(row, eye) for row in rows], axis=0)
    offset_col = jnp.concatenate([column_of(offset[s : s + 1, :], eye) for s in range(groups)], axis=0)
    lane = iota_f((lookups, BLOCK), 1)
    named = owner_col == lane
    before = ones_where(iota((lookups, lookups), 0) > iota((lookups, lookups), 1))
    earlier = dot(before, ones_where(named))
    rank = jnp.sum(jnp.where(named, earlier, 0.0), axis=1, keepdims=True)
    target_ref[...] = jnp.broadcast_to(owner_col * SLOTS + rank, (lookups, BLOCK))
    placed = jnp.where(rank == lane, offset_col, 0.0)
    sublane = iota_f(square, 0)
    named_t = jnp.concatenate([jnp.where(sublane == row, 1.0, 0.0) for row in rows], axis=1)
    request_ref[...] = dot(named_t, placed, EXACT)


def rows_kernel(asked_ref, table_ref, rows_ref, wide_ref):
    asked = asked_ref[...]
    table = table_ref[...]
    sources = asked.shape[0]
    line = iota_f((sources, table.shape[0]), 1)
    for slot in range(SLOTS):
        chosen = ones_where(asked[:, slot : slot + 1] == line)
        wide_ref[pl.ds(slot, sources, stride=SLOTS), :] = dot(chosen, table)
    rows_ref[...] = wide_ref[...].astype(BF16)


def owned_kernel(asked_ref, owned_ref):
    slots = owned_ref.shape[1]
    source, line = iota((BLOCK, slots), 0), iota((BLOCK, slots), 1)
    spread = dot(asked_ref[...], jnp.where(source == line % SLOTS, 1.0, 0.0), EXACT)
    wanted = jnp.sum(jnp.where(source == line // SLOTS, spread, 0.0), axis=0, keepdims=True)
    owned_ref[...] = ones_where(iota_f(owned_ref.shape, 0) == wanted)


def masks_kernel(target_ref, hot_ref, cache_ref, table_ref, take_ref, put_ref, hot_in_ref, hot_put_ref, narrow_ref):
    square = (BLOCK, BLOCK)
    eye = iota(square, 0) == iota(square, 1)
    slots, lookups = put_ref.shape
    feats = hot_ref.shape[0]
    samples = hot_ref.shape[1]
    lane = iota_f((samples, BLOCK), 1)
    slot = iota_f((slots, BLOCK), 0)
    for k in range(feats):
        mine = target_ref[pl.ds(k, samples, stride=feats), :]
        for b in range(slots // BLOCK):
            take_ref[k * samples : (k + 1) * samples, b * BLOCK : (b + 1) * BLOCK] = ones_where(
                mine == lane + float(b * BLOCK)
            )
        for h in range(samples // BLOCK):
            at = k * samples + h * BLOCK
            row = jnp.sum(jnp.where(eye, mine[h * BLOCK : (h + 1) * BLOCK, :], 0.0), axis=0, keepdims=True)
            put_ref[:, at : at + BLOCK] = ones_where(slot == row)
    cache = cache_ref[...].astype(BF16)
    hot = hot_ref[...].astype(F32)
    hot_count = cache.shape[0]
    hot_row = iota_f((hot_count, BLOCK), 0)
    hot_lane = iota_f((BLOCK, hot_count), 1)
    for k in range(feats):
        for h in range(samples // BLOCK):
            at = k * samples + h * BLOCK
            row = hot[k : k + 1, h * BLOCK : (h + 1) * BLOCK]
            hot_put_ref[:, at : at + BLOCK] = ones_where(hot_row == row)
            chosen = ones_where(column_of(row, eye) == hot_lane)
            hot_in_ref[h * BLOCK : (h + 1) * BLOCK, k * BLOCK : (k + 1) * BLOCK] = dot(chosen, cache).astype(BF16)
    narrow_ref[...] = table_ref[...].astype(BF16)


def layer_kernel(
    returned_ref, take_ref, put_ref, hot_in_ref, weight_ref, out_weight_ref, labels_ref,
    outgoing_ref, inputs_ref, dhidden_ref, hot_dx_ref, head_ref,
):
    square = (BLOCK, BLOCK)
    eye = iota(square, 0) == iota(square, 1)
    samples = hot_in_ref.shape[0]
    width = BLOCK
    cold = dot(take_ref[...], returned_ref[...]).astype(BF16)
    inputs = jnp.concatenate([hot_in_ref[...], cold[:samples], cold[samples:]], axis=1)
    inputs_ref[...] = inputs
    weight = weight_ref[...]
    out_weight = out_weight_ref[...]
    preact = dot(inputs, weight)
    gates = jax.nn.sigmoid(preact)
    hidden = (preact * gates).astype(BF16).astype(F32)
    logits = jnp.sum(hidden * out_weight, axis=1, keepdims=True)
    labels = labels_ref[...].astype(F32)
    label = jnp.concatenate([column_of(labels[h : h + 1, :], eye) for h in range(samples // BLOCK)], axis=0)
    errors = jax.nn.sigmoid(logits) - label
    slope = gates * (1.0 + preact * (1.0 - gates))
    dhidden = (errors * out_weight * slope).astype(BF16)
    dhidden_ref[...] = dhidden
    dinputs = dot_t(dhidden, weight).astype(BF16)
    cold_dx = jnp.concatenate([dinputs[:, 2 * width : 3 * width], dinputs[:, 3 * width :]], axis=0)
    outgoing_ref[...] = dot(put_ref[...], cold_dx).astype(BF16)
    hot_dx_ref[:samples, :] = dinputs[:, :width]
    hot_dx_ref[samples:, :] = dinputs[:, width : 2 * width]
    head = jnp.sum(errors * hidden, axis=0, keepdims=True)
    for b in range(head_ref.shape[0]):
        head_ref[b : b + 1, :] = head[:, b * BLOCK : (b + 1) * BLOCK]


def half_of_top(core, rep, inputs, dhidden):
    shape = (inputs.shape[1] // 2, inputs.shape[1])
    line = iota(shape, 0)
    row = (line & 15) * 32 + ((line >> 4) & 3) * 8 + core * 4 + ((line >> 6) ^ rep)
    ordered = dot_t(ones_where(row == iota(shape, 1)), inputs).astype(BF16)
    return dot(ordered, dhidden)


def hot_rows(picked_ref, core, rep, piece):
    count = picked_ref.shape[0] // 8
    return picked_ref[pl.ds(pl.multiple_of((core * 4 + (rep ^ piece)) * count, count), count), :]


def send_kernel(
    place_ref, refresh_ref, inputs_ref, dhidden_ref, hot_put_ref, hot_dx_ref, head_ref, pending_ref,
    send_ref, picked_ref, pending_new_ref,
):
    pending_new_ref[...] = pending_ref[...] + dot(hot_put_ref[...], hot_dx_ref[...])
    count = refresh_ref.shape[0]
    blocks = [pl.ds(pl.multiple_of(refresh_ref[i] * BLOCK, BLOCK), BLOCK) for i in range(count)]
    for i, at in enumerate(blocks):
        picked_ref[i * BLOCK : (i + 1) * BLOCK, :] = pending_new_ref[at, :]
    end = count * BLOCK
    picked_ref[end : end + 8, :] = head_ref[...]
    picked_ref[end + 8 :, :] = jnp.zeros((picked_ref.shape[0] - end - 8, BLOCK), F32)
    for at in blocks:
        pending_new_ref[at, :] = jnp.zeros((BLOCK, BLOCK), F32)
    core, rep = 1 - place_ref[0], place_ref[1]
    wide = dhidden_ref.shape[1]
    tall = send_ref.shape[0] // 4
    send_ref[:, :wide] = half_of_top(core, rep, inputs_ref[...], dhidden_ref[...])
    for d in range(4):
        send_ref[d * tall : (d + 1) * tall, wide:] = hot_rows(picked_ref, core, rep, d)


def pair_kernel(place_ref, inputs_ref, dhidden_ref, picked_ref, received_ref, *pieces):
    core, rep = place_ref[0], place_ref[1]
    wide = dhidden_ref.shape[1]
    top = half_of_top(core, rep, inputs_ref[...], dhidden_ref[...])
    tall = pieces[0].shape[0]
    for d, piece in enumerate(pieces):
        rows = slice(d * tall, (d + 1) * tall)
        piece[:, :wide] = top[rows] + received_ref[rows, :wide]
        piece[:, wide:] = hot_rows(picked_ref, core, rep, d) + received_ref[rows, wide:]


def four_kernel(own_ref, one_ref, two_ref, three_ref, sum_ref):
    sum_ref[...] = (own_ref[...] + one_ref[...]) + (two_ref[...] + three_ref[...])


def plane_kernel(parts_ref, out_ref):
    total = parts_ref[0]
    for i in range(1, parts_ref.shape[0]):
        total = total + parts_ref[i]
    wide = total.shape[1] - BLOCK
    tall = wide // BLOCK
    for b in range(tall):
        out_ref[:, b, :] = total[:, b * BLOCK : (b + 1) * BLOCK]
    for z in range(out_ref.shape[0]):
        out_ref[z, tall:, :] = total[:, wide:]


def column_kernel(parts_ref, top_ref, copies_ref):
    total = parts_ref[0]
    for i in range(1, parts_ref.shape[0]):
        total = total + parts_ref[i]
    tall = top_ref.shape[0]
    top_ref[...] = total[:tall]
    for i in range(copies_ref.shape[0]):
        copies_ref[i] = total[tall:]


def adagrad(table_rows, accum_rows, gradient):
    accum_next = accum_rows + gradient * gradient
    return (table_rows - step_size * gradient / (jnp.sqrt(accum_next) + epsilon), accum_next)


def hot_kernel(refresh_ref, clock_ref, sums_ref, cache_ref, accum_ref, cache_new_ref, accum_new_ref, out_grad_ref):
    cache_new_ref[...] = cache_ref[...]
    accum_new_ref[...] = accum_ref[...]
    count = refresh_ref.shape[0]
    for i in range(count):
        block = refresh_ref[i]
        at = pl.ds(pl.multiple_of(block * BLOCK, BLOCK), BLOCK)
        flush = sums_ref[i * BLOCK : (i + 1) * BLOCK, :] / (1.0 + clock_ref[block].astype(F32))
        cache_next, accum_next = adagrad(cache_ref[at, :], accum_ref[at, :], flush)
        cache_new_ref[at, :] = cache_next
        accum_new_ref[at, :] = accum_next
    out_grad_ref[...] = sums_ref[count * BLOCK : count * BLOCK + 8, :]


def cold_kernel(owned_ref, incoming_ref, grad_ref):
    grad_ref[...] = dot(owned_ref[...], incoming_ref[...])


def update_kernel(own_ref, one_ref, two_ref, three_ref, table_ref, accum_ref, table_new_ref, accum_new_ref):
    grad = (own_ref[...] + one_ref[...]) + (two_ref[...] + three_ref[...])
    table_next, accum_next = adagrad(table_ref[...], accum_ref[...], grad)
    table_new_ref[...] = table_next
    accum_new_ref[...] = accum_next


def swap(x, axis):
    return lax.all_to_all(x, axis, split_axis=0, concat_axis=0, tiled=True)


def from_others(pieces):
    return [lax.ppermute(p, "rep", [(i, i ^ d) for i in range(4)]) for d, p in enumerate(pieces, 1)]


def local(
    hot_ids,
    cold_owner,
    cold_offset,
    labels,
    top_weight,
    out_weight,
    cold_table,
    cold_accum,
    hot_cache,
    hot_accum,
    pending,
    refresh_blocks,
    block_clock,
):
    samples, feats = hot_ids.shape
    lookups = cold_offset.shape[0]
    own_rows, width = cold_table.shape
    hot_count = hot_cache.shape[0]
    inputs_width, hidden_width = top_weight.shape
    owners = lax.axis_size(DP)
    slots = owners * SLOTS
    groups = lookups // BLOCK
    place = jnp.stack([lax.axis_index("dp_2"), lax.axis_index("rep")]).astype(jnp.int32)

    request, target = call(
        requests_kernel,
        [((owners, BLOCK), F32), ((lookups, BLOCK), F32)],
        (cold_owner.reshape(groups, BLOCK), cold_offset.reshape(groups, BLOCK)),
    )
    asked = swap(request.reshape(owners, 1, BLOCK), DP).reshape(owners, BLOCK)
    take, put, hot_in, hot_put, narrow = call(
        masks_kernel,
        [
            ((lookups, slots), BF16),
            ((slots, lookups), BF16),
            ((samples, feats * width), BF16),
            ((hot_count, samples * feats), BF16),
            ((own_rows, width), BF16),
        ],
        (target, hot_ids.T, hot_cache, cold_table),
    )
    (found,) = call(rows_kernel, [((slots, width), BF16)], (asked, narrow), scratch=[((slots, width), F32)])
    returned = swap(found.reshape(owners, SLOTS, width), DP).reshape(slots, width)
    (owned,) = call(owned_kernel, [((own_rows, slots), BF16)], (asked,))
    outgoing, inputs, dhidden, hot_dx, head = call(
        layer_kernel,
        [
            ((slots, width), BF16),
            ((samples, inputs_width), BF16),
            ((samples, hidden_width), BF16),
            ((samples * feats, width), BF16),
            ((8, BLOCK), F32),
        ],
        (returned, take, put, hot_in, top_weight, out_weight.reshape(1, hidden_width), labels.reshape(2, BLOCK)),
    )
    incoming = swap(outgoing.reshape(owners, SLOTS, width), DP).reshape(slots, width)

    half = inputs_width // 2
    broad = hidden_width + BLOCK
    send, picked, pending_new = call(
        send_kernel,
        [((half, broad), F32), ((inputs_width, BLOCK), F32), ((hot_count, width), F32)],
        (place, refresh_blocks, inputs, dhidden, hot_put, hot_dx, head, pending),
        smem=2,
    )
    received = lax.ppermute(send, "dp_2", [(0, 1), (1, 0)])
    pieces = call(
        pair_kernel, [((half // 4, broad), F32)] * 4, (place, inputs, dhidden, picked, received), smem=1
    )
    (paired,) = call(four_kernel, [((half // 4, broad), F32)], (pieces[0], *from_others(pieces[1:])))
    paired, incoming = lax.optimization_barrier((paired, incoming))
    near = lax.axis_size("dp_1")
    far = lax.axis_size("dp_0")
    plane_size = lax.axis_size(PLANE)
    plane = swap(paired.reshape(near, far, broad), "dp_1")
    tall = hidden_width // BLOCK
    (columns,) = call(plane_kernel, [((far, tall + far, BLOCK), F32)], (plane,))
    columns = swap(columns, "dp_0")
    top, copies = call(
        column_kernel, [((tall, BLOCK), F32), ((plane_size, far, BLOCK), F32)], (columns,)
    )
    sums = swap(copies, PLANE).reshape(plane_size * far, BLOCK)

    (grad,) = call(cold_kernel, [((own_rows, width), F32)], (owned, incoming))
    others = from_others([grad] * 3)
    cold_table_new, cold_accum_new = call(
        update_kernel, [((own_rows, width), F32)] * 2, (grad, *others, cold_table, cold_accum)
    )
    hot_cache_new, hot_accum_new, out_grad = call(
        hot_kernel,
        [((hot_count, width), F32)] * 2 + [((8, BLOCK), F32)],
        (refresh_blocks, block_clock, sums, hot_cache, hot_accum),
        smem=2,
    )
    return (
        cold_table_new,
        cold_accum_new,
        hot_cache_new,
        hot_accum_new,
        pending_new,
        top.reshape(1, hidden_width),
        out_grad.reshape(hidden_width),
    )


def solution(mesh):
    split = Mesh(mesh.devices.reshape(16, 4, 2, mesh.shape["rep"]), ("dp_0", "dp_1", "dp_2", "rep"))
    in_specs = (
        P(DP_REP, None),
        P(DP_REP, None),
        P(DP_REP),
        P(DP_REP),
        P(),
        P(),
        P(DP, None),
        P(DP, None),
        P(),
        P(),
        P(DP_REP, None),
        P(),
        P(),
    )
    out_specs = (P(DP, None), P(DP, None), P(), P(), P(DP_REP, None), P(DP_REP, None), P())
    return jax.shard_map(local, mesh=split, in_specs=in_specs, out_specs=out_specs, check_vma=False)
```

```python
import jax
import jax.numpy as jnp
from jax import lax
from jax.experimental import pallas as pl
from jax.experimental.pallas import tpu as pltpu
from jax.sharding import Mesh
from jax.sharding import PartitionSpec as P

BLOCK = 128
SLOTS = 8
DP = ("dp_0", "dp_1", "dp_2")
DP_REP = ("dp_0", "dp_1", "dp_2", "rep")
PLANE = ("dp_2", "rep", "dp_1")

step_size = 0.5
epsilon = 1e-08

F32 = jnp.float32
BF16 = jnp.bfloat16
I16 = jnp.int16
LN2 = 0.6931471805599453
FINE = 65534.0
EXACT = lax.Precision.HIGHEST
VMEM = pl.BlockSpec(memory_space=pltpu.VMEM)
SMEM = pl.BlockSpec(memory_space=pltpu.SMEM)


def call(kernel, outs, args, smem=0, scratch=(), flops=10**8, moved=10**6):
    shapes = [jax.ShapeDtypeStruct(s, d) for s, d in outs]
    return pl.pallas_call(
        kernel,
        out_shape=shapes,
        in_specs=[SMEM] * smem + [VMEM] * (len(args) - smem),
        out_specs=[VMEM] * len(outs),
        scratch_shapes=[pltpu.VMEM(s, d) for s, d in scratch],
        compiler_params=pltpu.CompilerParams(vmem_limit_bytes=16 * 2**20),
        cost_estimate=pl.CostEstimate(flops=flops, bytes_accessed=moved, transcendentals=0),
    )(*args)


def iota(shape, dim):
    return lax.broadcasted_iota(jnp.int32, shape, dim)


def iota_f(shape, dim):
    return iota(shape, dim).astype(F32)


def ones_where(mask):
    return jnp.where(mask, 1.0, 0.0).astype(BF16)


def column_of(row, eye):
    return jnp.sum(jnp.where(eye, row, 0.0), axis=1, keepdims=True)


def dot(a, b, precision=None):
    return jnp.dot(a, b, preferred_element_type=F32, precision=precision)


def dot_t(a, b):
    return lax.dot_general(a, b, (((1,), (1,)), ((), ())), preferred_element_type=F32)


def power(exponent):
    return jnp.exp(exponent * LN2)


def exponent_of(top):
    return jnp.ceil(jnp.log(jnp.maximum(top, 1e-30)) * (1.0 / LN2) + 0.01) - 15.0


def pack(values, packed_ref):
    wide = values.shape[1] - BLOCK
    top, hot = values[:, :wide], values[:, wide:]
    top_exponent = exponent_of(jnp.max(jnp.abs(top), axis=1, keepdims=True))
    hot_exponent = exponent_of(jnp.max(jnp.abs(hot), axis=1, keepdims=True))
    lane = iota((values.shape[0], BLOCK), 1)
    hot = hot * power(-hot_exponent)
    coarse = jnp.round(hot)
    at = 0
    for part in (
        jnp.round(top * power(-top_exponent)),
        coarse,
        jnp.round((hot - coarse) * FINE),
        jnp.where(lane < BLOCK // 2, top_exponent, hot_exponent),
    ):
        packed_ref[:, at : at + part.shape[1]] = part.astype(jnp.int32).astype(I16)
        at += part.shape[1]


def unpack(packed):
    values = packed.astype(jnp.int32).astype(F32)
    wide = values.shape[1] - 3 * BLOCK
    coarse, fine, exponents = (values[:, wide + i * BLOCK : wide + (i + 1) * BLOCK] for i in range(3))
    top = values[:, :wide] * power(exponents[:, :1])
    hot = (coarse + fine * (1.0 / FINE)) * power(exponents[:, BLOCK - 1 :])
    return jnp.concatenate([top, hot], axis=1)


def requests_kernel(owner_ref, offset_ref, request_ref, target_ref):
    square = (BLOCK, BLOCK)
    eye = iota(square, 0) == iota(square, 1)
    groups = owner_ref.shape[0]
    lookups = groups * BLOCK
    owner = owner_ref[...].astype(F32)
    offset = offset_ref[...].astype(F32)
    rows = [owner[s : s + 1, :] for s in range(groups)]
    owner_col = jnp.concatenate([column_of(row, eye) for row in rows], axis=0)
    offset_col = jnp.concatenate([column_of(offset[s : s + 1, :], eye) for s in range(groups)], axis=0)
    lane = iota_f((lookups, BLOCK), 1)
    named = owner_col == lane
    before = ones_where(iota((lookups, lookups), 0) > iota((lookups, lookups), 1))
    earlier = dot(before, ones_where(named))
    rank = jnp.sum(jnp.where(named, earlier, 0.0), axis=1, keepdims=True)
    target_ref[...] = jnp.broadcast_to(owner_col * SLOTS + rank, (lookups, BLOCK))
    placed = jnp.where(rank == lane, offset_col, 0.0)
    sublane = iota_f(square, 0)
    named_t = jnp.concatenate([jnp.where(sublane == row, 1.0, 0.0) for row in rows], axis=1)
    request_ref[...] = dot(named_t, placed, EXACT)


def rows_kernel(asked_ref, table_ref, rows_ref, wide_ref):
    asked = asked_ref[...]
    table = table_ref[...]
    sources = asked.shape[0]
    line = iota_f((sources, table.shape[0]), 1)
    for slot in range(SLOTS):
        chosen = ones_where(asked[:, slot : slot + 1] == line)
        wide_ref[pl.ds(slot, sources, stride=SLOTS), :] = dot(chosen, table)
    rows_ref[...] = wide_ref[...].astype(BF16)


def owned_kernel(asked_ref, owned_ref):
    slots = owned_ref.shape[1]
    source, line = iota((BLOCK, slots), 0), iota((BLOCK, slots), 1)
    spread = dot(asked_ref[...], jnp.where(source == line % SLOTS, 1.0, 0.0), EXACT)
    wanted = jnp.sum(jnp.where(source == line // SLOTS, spread, 0.0), axis=0, keepdims=True)
    owned_ref[...] = ones_where(iota_f(owned_ref.shape, 0) == wanted)


def masks_kernel(target_ref, hot_ref, cache_ref, table_ref, rows_ref, hot_in_ref, hot_put_ref, narrow_ref):
    square = (BLOCK, BLOCK)
    eye = iota(square, 0) == iota(square, 1)
    feats = hot_ref.shape[0]
    samples = hot_ref.shape[1]
    for k in range(feats):
        mine = target_ref[pl.ds(k, samples, stride=feats), :]
        for h in range(samples // BLOCK):
            at = k * samples + h * BLOCK
            row = jnp.sum(jnp.where(eye, mine[h * BLOCK : (h + 1) * BLOCK, :], 0.0), axis=0, keepdims=True)
            rows_ref[:, at : at + BLOCK] = jnp.broadcast_to(row, (8, BLOCK))
    cache = cache_ref[...].astype(BF16)
    hot = hot_ref[...].astype(F32)
    hot_count = cache.shape[0]
    hot_row = iota_f((hot_count, BLOCK), 0)
    hot_lane = iota_f((BLOCK, hot_count), 1)
    for k in range(feats):
        for h in range(samples // BLOCK):
            at = k * samples + h * BLOCK
            row = hot[k : k + 1, h * BLOCK : (h + 1) * BLOCK]
            hot_put_ref[:, at : at + BLOCK] = ones_where(hot_row == row)
            chosen = ones_where(column_of(row, eye) == hot_lane)
            hot_in_ref[h * BLOCK : (h + 1) * BLOCK, k * BLOCK : (k + 1) * BLOCK] = dot(chosen, cache).astype(BF16)
    narrow_ref[...] = table_ref[...].astype(BF16)


def layer_kernel(
    returned_ref, target_ref, rows_ref, hot_in_ref, weight_ref, out_weight_ref, labels_ref,
    outgoing_ref, inputs_ref, dhidden_ref, hot_dx_ref, head_ref,
):
    square = (BLOCK, BLOCK)
    eye = iota(square, 0) == iota(square, 1)
    samples = hot_in_ref.shape[0]
    width = BLOCK
    lane = iota_f((samples, BLOCK), 1)
    slots = returned_ref.shape[0]
    mine = [target_ref[pl.ds(k, samples, stride=2), :] for k in range(2)]
    take = [
        jnp.concatenate([ones_where(t == lane + float(b)) for b in range(0, slots, BLOCK)], axis=1) for t in mine
    ]
    cold = dot(jnp.concatenate(take, axis=0), returned_ref[...]).astype(BF16)
    inputs = jnp.concatenate([hot_in_ref[...], cold[:samples], cold[samples:]], axis=1)
    inputs_ref[...] = inputs
    weight = weight_ref[...]
    out_weight = out_weight_ref[...]
    preact = dot(inputs, weight)
    gates = jax.nn.sigmoid(preact)
    hidden = (preact * gates).astype(BF16).astype(F32)
    logits = jnp.sum(hidden * out_weight, axis=1, keepdims=True)
    labels = labels_ref[...].astype(F32)
    label = jnp.concatenate([column_of(labels[h : h + 1, :], eye) for h in range(samples // BLOCK)], axis=0)
    errors = jax.nn.sigmoid(logits) - label
    slope = gates * (1.0 + preact * (1.0 - gates))
    dhidden = (errors * out_weight * slope).astype(BF16)
    dhidden_ref[...] = dhidden
    dinputs = dot_t(dhidden, weight).astype(BF16)
    cold_dx = jnp.concatenate([dinputs[:, 2 * width : 3 * width], dinputs[:, 3 * width :]], axis=0)
    put = ones_where(iota_f((outgoing_ref.shape[0], rows_ref.shape[1]), 0) == rows_ref[:1, :])
    outgoing_ref[...] = dot(put, cold_dx).astype(BF16)
    hot_dx_ref[:samples, :] = dinputs[:, :width]
    hot_dx_ref[samples:, :] = dinputs[:, width : 2 * width]
    head = jnp.sum(errors * hidden, axis=0, keepdims=True)
    for b in range(head_ref.shape[0]):
        head_ref[b : b + 1, :] = head[:, b * BLOCK : (b + 1) * BLOCK]


def half_of_top(core, rep, inputs, dhidden):
    shape = (inputs.shape[1] // 2, inputs.shape[1])
    line = iota(shape, 0)
    row = (line & 15) * 32 + ((line >> 4) & 3) * 8 + core * 4 + ((line >> 6) ^ rep)
    ordered = dot_t(ones_where(row == iota(shape, 1)), inputs).astype(BF16)
    return dot(ordered, dhidden)


def hot_rows(picked_ref, core, rep, piece):
    count = picked_ref.shape[0] // 8
    return picked_ref[pl.ds(pl.multiple_of((core * 4 + (rep ^ piece)) * count, count), count), :]


def send_kernel(
    place_ref, refresh_ref, inputs_ref, dhidden_ref, hot_put_ref, hot_dx_ref, head_ref, pending_ref,
    send_ref, picked_ref, pending_new_ref,
):
    pending_new_ref[...] = pending_ref[...] + dot(hot_put_ref[...], hot_dx_ref[...])
    count = refresh_ref.shape[0]
    blocks = [pl.ds(pl.multiple_of(refresh_ref[i] * BLOCK, BLOCK), BLOCK) for i in range(count)]
    for i, at in enumerate(blocks):
        picked_ref[i * BLOCK : (i + 1) * BLOCK, :] = pending_new_ref[at, :]
    end = count * BLOCK
    picked_ref[end : end + 8, :] = head_ref[...]
    picked_ref[end + 8 :, :] = jnp.zeros((picked_ref.shape[0] - end - 8, BLOCK), F32)
    for at in blocks:
        pending_new_ref[at, :] = jnp.zeros((BLOCK, BLOCK), F32)
    core, rep = 1 - place_ref[0], place_ref[1]
    top = half_of_top(core, rep, inputs_ref[...], dhidden_ref[...])
    hot = jnp.concatenate([hot_rows(picked_ref, core, rep, d) for d in range(4)], axis=0)
    pack(jnp.concatenate([top, hot], axis=1), send_ref)


def pair_kernel(place_ref, inputs_ref, dhidden_ref, picked_ref, received_ref, own_ref, *pieces):
    core, rep = place_ref[0], place_ref[1]
    top = half_of_top(core, rep, inputs_ref[...], dhidden_ref[...])
    tall = own_ref.shape[0]
    for d, piece in enumerate((own_ref, *pieces)):
        rows = slice(d * tall, (d + 1) * tall)
        mine = jnp.concatenate([top[rows], hot_rows(picked_ref, core, rep, d)], axis=1)
        both = mine + unpack(received_ref[rows, :])
        if d:
            pack(both, piece)
        else:
            piece[...] = both


def four_kernel(own_ref, one_ref, two_ref, three_ref, sum_ref):
    total = (own_ref[...] + unpack(one_ref[...])) + (unpack(two_ref[...]) + unpack(three_ref[...]))
    pack(total, sum_ref)


def plane_kernel(parts_ref, out_ref):
    total = unpack(parts_ref[0])
    for i in range(1, parts_ref.shape[0]):
        total = total + unpack(parts_ref[i])
    wide = total.shape[1] - BLOCK
    tall = wide // BLOCK
    for b in range(tall):
        out_ref[:, b, :] = total[:, b * BLOCK : (b + 1) * BLOCK]
    for z in range(out_ref.shape[0]):
        out_ref[z, tall:, :] = total[:, wide:]


def column_kernel(parts_ref, top_ref, copies_ref):
    total = parts_ref[0]
    for i in range(1, parts_ref.shape[0]):
        total = total + parts_ref[i]
    tall = top_ref.shape[0]
    top_ref[...] = total[:tall]
    for i in range(copies_ref.shape[0]):
        copies_ref[i] = total[tall:]


def adagrad(table_rows, accum_rows, gradient):
    accum_next = accum_rows + gradient * gradient
    return (table_rows - step_size * gradient / (jnp.sqrt(accum_next) + epsilon), accum_next)


def hot_kernel(refresh_ref, clock_ref, sums_ref, cache_ref, accum_ref, cache_new_ref, accum_new_ref, out_grad_ref):
    cache_new_ref[...] = cache_ref[...]
    accum_new_ref[...] = accum_ref[...]
    count = refresh_ref.shape[0]
    for i in range(count):
        block = refresh_ref[i]
        at = pl.ds(pl.multiple_of(block * BLOCK, BLOCK), BLOCK)
        flush = sums_ref[i * BLOCK : (i + 1) * BLOCK, :] / (1.0 + clock_ref[block].astype(F32))
        cache_next, accum_next = adagrad(cache_ref[at, :], accum_ref[at, :], flush)
        cache_new_ref[at, :] = cache_next
        accum_new_ref[at, :] = accum_next
    out_grad_ref[...] = sums_ref[count * BLOCK : count * BLOCK + 8, :]


def cold_kernel(owned_ref, incoming_ref, grad_ref):
    grad_ref[...] = dot(owned_ref[...], incoming_ref[...])


def update_kernel(own_ref, one_ref, two_ref, three_ref, table_ref, accum_ref, table_new_ref, accum_new_ref):
    grad = (own_ref[...] + one_ref[...]) + (two_ref[...] + three_ref[...])
    table_next, accum_next = adagrad(table_ref[...], accum_ref[...], grad)
    table_new_ref[...] = table_next
    accum_new_ref[...] = accum_next


def swap(x, axis):
    return lax.all_to_all(x, axis, split_axis=0, concat_axis=0, tiled=True)


def from_others(pieces):
    return [lax.ppermute(p, "rep", [(i, i ^ d) for i in range(4)]) for d, p in enumerate(pieces, 1)]


def local(
    hot_ids,
    cold_owner,
    cold_offset,
    labels,
    top_weight,
    out_weight,
    cold_table,
    cold_accum,
    hot_cache,
    hot_accum,
    pending,
    refresh_blocks,
    block_clock,
):
    samples, feats = hot_ids.shape
    lookups = cold_offset.shape[0]
    own_rows, width = cold_table.shape
    hot_count = hot_cache.shape[0]
    inputs_width, hidden_width = top_weight.shape
    owners = lax.axis_size(DP)
    slots = owners * SLOTS
    groups = lookups // BLOCK
    place = jnp.stack([lax.axis_index("dp_2"), lax.axis_index("rep")]).astype(jnp.int32)

    request, target = call(
        requests_kernel,
        [((owners, BLOCK), F32), ((lookups, BLOCK), F32)],
        (cold_owner.reshape(groups, BLOCK), cold_offset.reshape(groups, BLOCK)),
    )
    asked = swap(request.reshape(owners, 1, BLOCK), DP).reshape(owners, BLOCK)
    target_rows, hot_in, hot_put, narrow = call(
        masks_kernel,
        [
            ((8, lookups), F32),
            ((samples, feats * width), BF16),
            ((hot_count, samples * feats), BF16),
            ((own_rows, width), BF16),
        ],
        (target, hot_ids.T, hot_cache, cold_table),
    )
    (found,) = call(rows_kernel, [((slots, width), BF16)], (asked, narrow), scratch=[((slots, width), F32)])
    returned = swap(found.reshape(owners, SLOTS, width), DP).reshape(slots, width)
    (owned,) = call(owned_kernel, [((own_rows, slots), BF16)], (asked,))
    outgoing, inputs, dhidden, hot_dx, head = call(
        layer_kernel,
        [
            ((slots, width), BF16),
            ((samples, inputs_width), BF16),
            ((samples, hidden_width), BF16),
            ((samples * feats, width), BF16),
            ((8, BLOCK), F32),
        ],
        (returned, target, target_rows, hot_in, top_weight, out_weight.reshape(1, hidden_width), labels.reshape(2, BLOCK)),
    )
    incoming = swap(outgoing.reshape(owners, SLOTS, width), DP).reshape(slots, width)

    half = inputs_width // 2
    broad = hidden_width + BLOCK
    packed = broad + 2 * BLOCK
    near = lax.axis_size("dp_1")
    far = lax.axis_size("dp_0")
    plane_size = lax.axis_size(PLANE)
    send, picked, pending_new = call(
        send_kernel,
        [((half, packed), I16), ((plane_size * far, BLOCK), F32), ((hot_count, width), F32)],
        (place, refresh_blocks, inputs, dhidden, hot_put, hot_dx, head, pending),
        smem=2,
    )
    received = lax.ppermute(send, "dp_2", [(0, 1), (1, 0)])
    pieces = call(
        pair_kernel,
        [((half // 4, broad), F32)] + [((half // 4, packed), I16)] * 3,
        (place, inputs, dhidden, picked, received),
        smem=1,
    )
    (paired,) = call(four_kernel, [((half // 4, packed), I16)], (pieces[0], *from_others(pieces[1:])))
    paired, incoming = lax.optimization_barrier((paired, incoming))
    plane = swap(paired.reshape(near, far, packed), "dp_1")
    tall = hidden_width // BLOCK
    (columns,) = call(plane_kernel, [((far, tall + far, BLOCK), F32)], (plane,))
    columns = swap(columns, "dp_0")
    top, copies = call(column_kernel, [((tall, BLOCK), F32), ((plane_size, far, BLOCK), F32)], (columns,))
    sums = swap(copies, PLANE).reshape(plane_size * far, BLOCK)

    (grad,) = call(cold_kernel, [((own_rows, width), F32)], (owned, incoming))
    others = from_others([grad] * 3)
    cold_table_new, cold_accum_new = call(
        update_kernel, [((own_rows, width), F32)] * 2, (grad, *others, cold_table, cold_accum)
    )
    hot_cache_new, hot_accum_new, out_grad = call(
        hot_kernel,
        [((hot_count, width), F32)] * 2 + [((8, BLOCK), F32)],
        (refresh_blocks, block_clock, sums, hot_cache, hot_accum),
        smem=2,
    )
    return (
        cold_table_new,
        cold_accum_new,
        hot_cache_new,
        hot_accum_new,
        pending_new,
        top.reshape(1, hidden_width),
        out_grad.reshape(hidden_width),
    )


def solution(mesh):
    split = Mesh(mesh.devices.reshape(16, 4, 2, mesh.shape["rep"]), ("dp_0", "dp_1", "dp_2", "rep"))
    in_specs = (
        P(DP_REP, None),
        P(DP_REP, None),
        P(DP_REP),
        P(DP_REP),
        P(),
        P(),
        P(DP, None),
        P(DP, None),
        P(),
        P(),
        P(DP_REP, None),
        P(),
        P(),
    )
    out_specs = (P(DP, None), P(DP, None), P(), P(), P(DP_REP, None), P(DP_REP, None), P())
    return jax.shard_map(local, mesh=split, in_specs=in_specs, out_specs=out_specs, check_vma=False)
```

```python
import jax
import jax.numpy as jnp
from jax import lax
from jax.experimental import pallas as pl
from jax.experimental.pallas import tpu as pltpu
from jax.sharding import Mesh
from jax.sharding import PartitionSpec as P

BLOCK = 128
SLOTS = 8
DP = ("dp_0", "dp_1", "dp_2")
DP_REP = ("dp_0", "dp_1", "dp_2", "rep")
PLANE = ("dp_2", "rep", "dp_1")

step_size = 0.5
epsilon = 1e-08

F32 = jnp.float32
BF16 = jnp.bfloat16
I16 = jnp.int16
LN2 = 0.6931471805599453
FINE = 65534.0
EXACT = lax.Precision.HIGHEST
VMEM = pl.BlockSpec(memory_space=pltpu.VMEM)
HBM = pl.BlockSpec(memory_space=pltpu.HBM)
SMEM = pl.BlockSpec(memory_space=pltpu.SMEM)


class Loaded:
    def __init__(self, source, held, sem):
        self.copy = pltpu.make_async_copy(source, held, sem)
        self.held = held
        self.copy.start()

    def wait(self):
        self.copy.wait()
        return self.held


def call(kernel, outs, args, smem=0, scratch=(), loads=(), held=(), kept=()):
    own = len(scratch)
    ins = len(args)

    def body(*refs):
        given = list(refs[:ins])
        rest = refs[ins + len(outs) :]
        for j, i in enumerate(loads):
            given[i] = Loaded(given[i], rest[own + j], rest[own + len(loads) + j])
        kernel(*given, *refs[ins : ins + len(outs)], *rest[:own])

    specs = [SMEM] * smem + [VMEM] * (ins - smem)
    args = list(args)
    for i in loads:
        specs[i] = HBM
        args[i] = pltpu.with_memory_space_constraint(args[i], pltpu.HBM)
    for i in held:
        args[i] = pltpu.with_memory_space_constraint(args[i], pltpu.VMEM)
    return pl.pallas_call(
        body,
        out_shape=[(pltpu.VMEM if i in kept else jax.ShapeDtypeStruct)(s, d) for i, (s, d) in enumerate(outs)],
        in_specs=specs,
        out_specs=[VMEM] * len(outs),
        scratch_shapes=[pltpu.VMEM(s, d) for s, d in scratch]
        + [pltpu.VMEM(args[i].shape, args[i].dtype) for i in loads]
        + [pltpu.SemaphoreType.DMA for _ in loads],
        compiler_params=pltpu.CompilerParams(vmem_limit_bytes=16 * 2**20),
        cost_estimate=pl.CostEstimate(flops=10**9, bytes_accessed=10**7, transcendentals=0),
    )(*args)


def iota(shape, dim):
    return lax.broadcasted_iota(jnp.int32, shape, dim)


def iota_f(shape, dim):
    return iota(shape, dim).astype(F32)


def ones_where(mask):
    return jnp.where(mask, 1.0, 0.0).astype(BF16)


def column_of(row, eye):
    return jnp.sum(jnp.where(eye, row, 0.0), axis=1, keepdims=True)


def dot(a, b, precision=None):
    return jnp.dot(a, b, preferred_element_type=F32, precision=precision)


def dot_t(a, b):
    return lax.dot_general(a, b, (((1,), (1,)), ((), ())), preferred_element_type=F32)


def power(exponent):
    return jnp.exp(exponent * LN2)


def exponent_of(top):
    return jnp.ceil(jnp.log(jnp.maximum(top, 1e-30)) * (1.0 / LN2) + 0.01) - 15.0


def pack(values, packed_ref):
    wide = values.shape[1] - BLOCK
    top, hot = values[:, :wide], values[:, wide:]
    top_exponent = exponent_of(jnp.max(jnp.abs(top), axis=1, keepdims=True))
    hot_exponent = exponent_of(jnp.max(jnp.abs(hot), axis=1, keepdims=True))
    lane = iota((values.shape[0], BLOCK), 1)
    hot = hot * power(-hot_exponent)
    coarse = jnp.round(hot)
    at = 0
    for part in (
        jnp.round(top * power(-top_exponent)),
        coarse,
        jnp.round((hot - coarse) * FINE),
        jnp.where(lane < BLOCK // 2, top_exponent, hot_exponent),
    ):
        packed_ref[:, at : at + part.shape[1]] = part.astype(jnp.int32).astype(I16)
        at += part.shape[1]


def unpack(packed):
    values = packed.astype(jnp.int32).astype(F32)
    wide = values.shape[1] - 3 * BLOCK
    coarse, fine, exponents = (values[:, wide + i * BLOCK : wide + (i + 1) * BLOCK] for i in range(3))
    top = values[:, :wide] * power(exponents[:, :1])
    hot = (coarse + fine * (1.0 / FINE)) * power(exponents[:, BLOCK - 1 :])
    return jnp.concatenate([top, hot], axis=1)


def requests_kernel(owner_ref, offset_ref, request_ref, target_ref):
    square = (BLOCK, BLOCK)
    eye = iota(square, 0) == iota(square, 1)
    owner = owner_ref.wait()[...].astype(F32)
    offset = offset_ref.wait()[...].astype(F32)
    groups = owner.shape[0]
    lookups = groups * BLOCK
    rows = [owner[s : s + 1, :] for s in range(groups)]
    owner_col = jnp.concatenate([column_of(row, eye) for row in rows], axis=0)
    offset_col = jnp.concatenate([column_of(offset[s : s + 1, :], eye) for s in range(groups)], axis=0)
    lane = iota_f((lookups, BLOCK), 1)
    named = owner_col == lane
    before = ones_where(iota((lookups, lookups), 0) > iota((lookups, lookups), 1))
    earlier = dot(before, ones_where(named))
    rank = jnp.sum(jnp.where(named, earlier, 0.0), axis=1, keepdims=True)
    target_ref[...] = jnp.broadcast_to(owner_col * SLOTS + rank, (lookups, BLOCK))
    placed = jnp.where(rank == lane, offset_col, 0.0)
    sublane = iota_f(square, 0)
    named_t = jnp.concatenate([jnp.where(sublane == row, 1.0, 0.0) for row in rows], axis=1)
    request_ref[...] = dot(named_t, placed, EXACT)


def rows_kernel(asked_ref, table_ref, rows_ref, wide_ref):
    asked = asked_ref[...]
    table = table_ref[...]
    sources = asked.shape[0]
    line = iota_f((sources, table.shape[0]), 1)
    for slot in range(SLOTS):
        chosen = ones_where(asked[:, slot : slot + 1] == line)
        wide_ref[pl.ds(slot, sources, stride=SLOTS), :] = dot(chosen, table)
    rows_ref[...] = wide_ref[...].astype(BF16)


def owned_kernel(asked_ref, owned_ref):
    slots = owned_ref.shape[1]
    source, line = iota((BLOCK, slots), 0), iota((BLOCK, slots), 1)
    spread = dot(asked_ref[...], jnp.where(source == line % SLOTS, 1.0, 0.0), EXACT)
    wanted = jnp.sum(jnp.where(source == line // SLOTS, spread, 0.0), axis=0, keepdims=True)
    owned_ref[...] = ones_where(iota_f(owned_ref.shape, 0) == wanted)


def masks_kernel(target_ref, hot_ref, cache_ref, table_ref, rows_ref, hot_in_ref, hot_put_ref, narrow_ref):
    square = (BLOCK, BLOCK)
    eye = iota(square, 0) == iota(square, 1)
    hot = hot_ref.wait()[...].astype(F32)
    feats, samples = hot.shape
    for k in range(feats):
        mine = target_ref[pl.ds(k, samples, stride=feats), :]
        for h in range(samples // BLOCK):
            at = k * samples + h * BLOCK
            row = jnp.sum(jnp.where(eye, mine[h * BLOCK : (h + 1) * BLOCK, :], 0.0), axis=0, keepdims=True)
            rows_ref[:, at : at + BLOCK] = jnp.broadcast_to(row, (8, BLOCK))
    cache = cache_ref.wait()[...].astype(BF16)
    hot_count = cache.shape[0]
    hot_row = iota_f((hot_count, BLOCK), 0)
    hot_lane = iota_f((BLOCK, hot_count), 1)
    for k in range(feats):
        for h in range(samples // BLOCK):
            at = k * samples + h * BLOCK
            row = hot[k : k + 1, h * BLOCK : (h + 1) * BLOCK]
            hot_put_ref[:, at : at + BLOCK] = ones_where(hot_row == row)
            chosen = ones_where(column_of(row, eye) == hot_lane)
            hot_in_ref[h * BLOCK : (h + 1) * BLOCK, k * BLOCK : (k + 1) * BLOCK] = dot(chosen, cache).astype(BF16)
    narrow_ref[...] = table_ref.wait()[...].astype(BF16)


def layer_kernel(
    returned_ref, target_ref, rows_ref, hot_in_ref, weight_ref, out_weight_ref, labels_ref,
    outgoing_ref, inputs_ref, dhidden_ref, hot_dx_ref, head_ref,
):
    square = (BLOCK, BLOCK)
    eye = iota(square, 0) == iota(square, 1)
    width = BLOCK
    samples = target_ref.shape[0] // 2
    lane = iota_f((samples, BLOCK), 1)
    slots = returned_ref.shape[0]
    mine = [target_ref[pl.ds(k, samples, stride=2), :] for k in range(2)]
    take = [
        jnp.concatenate([ones_where(t == lane + float(b)) for b in range(0, slots, BLOCK)], axis=1) for t in mine
    ]
    cold = dot(jnp.concatenate(take, axis=0), returned_ref[...]).astype(BF16)
    inputs = jnp.concatenate([hot_in_ref[...], cold[:samples], cold[samples:]], axis=1)
    inputs_ref[...] = inputs
    weight = weight_ref.wait()[...]
    out_weight = out_weight_ref.wait()[...]
    preact = dot(inputs, weight)
    gates = jax.nn.sigmoid(preact)
    hidden = (preact * gates).astype(BF16).astype(F32)
    logits = jnp.sum(hidden * out_weight, axis=1, keepdims=True)
    labels = labels_ref.wait()[...].astype(F32)
    label = jnp.concatenate([column_of(labels[h : h + 1, :], eye) for h in range(samples // BLOCK)], axis=0)
    errors = jax.nn.sigmoid(logits) - label
    slope = gates * (1.0 + preact * (1.0 - gates))
    dhidden = (errors * out_weight * slope).astype(BF16)
    dhidden_ref[...] = dhidden
    dinputs = dot_t(dhidden, weight).astype(BF16)
    cold_dx = jnp.concatenate([dinputs[:, 2 * width : 3 * width], dinputs[:, 3 * width :]], axis=0)
    put = ones_where(iota_f((outgoing_ref.shape[0], rows_ref.shape[1]), 0) == rows_ref[:1, :])
    outgoing_ref[...] = dot(put, cold_dx).astype(BF16)
    hot_dx_ref[:samples, :] = dinputs[:, :width]
    hot_dx_ref[samples:, :] = dinputs[:, width : 2 * width]
    head = jnp.sum(errors * hidden, axis=0, keepdims=True)
    for b in range(head_ref.shape[0]):
        head_ref[b : b + 1, :] = head[:, b * BLOCK : (b + 1) * BLOCK]


def half_of_top(core, rep, inputs, dhidden):
    shape = (inputs.shape[1] // 2, inputs.shape[1])
    line = iota(shape, 0)
    row = (line & 15) * 32 + ((line >> 4) & 3) * 8 + core * 4 + ((line >> 6) ^ rep)
    ordered = dot_t(ones_where(row == iota(shape, 1)), inputs).astype(BF16)
    return dot(ordered, dhidden)


def hot_rows(picked_ref, core, rep, piece):
    count = picked_ref.shape[0] // 8
    return picked_ref[pl.ds(pl.multiple_of((core * 4 + (rep ^ piece)) * count, count), count), :]


def send_kernel(
    place_ref, refresh_ref, inputs_ref, dhidden_ref, hot_put_ref, hot_dx_ref, head_ref, pending_ref,
    send_ref, picked_ref, pending_new_ref,
):
    pending_new_ref[...] = dot(hot_put_ref[...], hot_dx_ref[...]) + pending_ref.wait()[...]
    count = refresh_ref.shape[0]
    blocks = [pl.ds(pl.multiple_of(refresh_ref[i] * BLOCK, BLOCK), BLOCK) for i in range(count)]
    for i, at in enumerate(blocks):
        picked_ref[i * BLOCK : (i + 1) * BLOCK, :] = pending_new_ref[at, :]
    end = count * BLOCK
    picked_ref[end : end + 8, :] = head_ref[...]
    picked_ref[end + 8 :, :] = jnp.zeros((picked_ref.shape[0] - end - 8, BLOCK), F32)
    for at in blocks:
        pending_new_ref[at, :] = jnp.zeros((BLOCK, BLOCK), F32)
    core, rep = 1 - place_ref[0], place_ref[1]
    top = half_of_top(core, rep, inputs_ref[...], dhidden_ref[...])
    hot = jnp.concatenate([hot_rows(picked_ref, core, rep, d) for d in range(4)], axis=0)
    pack(jnp.concatenate([top, hot], axis=1), send_ref)


def pair_kernel(place_ref, inputs_ref, dhidden_ref, picked_ref, received_ref, own_ref, *pieces):
    core, rep = place_ref[0], place_ref[1]
    top = half_of_top(core, rep, inputs_ref[...], dhidden_ref[...])
    tall = own_ref.shape[0]
    for d, piece in enumerate((own_ref, *pieces)):
        rows = slice(d * tall, (d + 1) * tall)
        mine = jnp.concatenate([top[rows], hot_rows(picked_ref, core, rep, d)], axis=1)
        both = mine + unpack(received_ref[rows, :])
        if d:
            pack(both, piece)
        else:
            piece[...] = both


def four_kernel(own_ref, one_ref, two_ref, three_ref, sum_ref):
    total = (own_ref[...] + unpack(one_ref[...])) + (unpack(two_ref[...]) + unpack(three_ref[...]))
    pack(total, sum_ref)


def plane_kernel(parts_ref, out_ref):
    total = unpack(parts_ref[0])
    for i in range(1, parts_ref.shape[0]):
        total = total + unpack(parts_ref[i])
    wide = total.shape[1] - BLOCK
    tall = wide // BLOCK
    for b in range(tall):
        out_ref[:, b, :] = total[:, b * BLOCK : (b + 1) * BLOCK]
    for z in range(out_ref.shape[0]):
        out_ref[z, tall:, :] = total[:, wide:]


def column_kernel(parts_ref, top_ref, copies_ref):
    total = parts_ref[0]
    for i in range(1, parts_ref.shape[0]):
        total = total + parts_ref[i]
    tall = top_ref.shape[0]
    top_ref[...] = total[:tall]
    for i in range(copies_ref.shape[0]):
        copies_ref[i] = total[tall:]


def adagrad(table_rows, accum_rows, gradient):
    accum_next = accum_rows + gradient * gradient
    return (table_rows - step_size * gradient / (jnp.sqrt(accum_next) + epsilon), accum_next)


def hot_kernel(refresh_ref, clock_ref, sums_ref, cache_ref, accum_ref, cache_new_ref, accum_new_ref, out_grad_ref):
    cache_new_ref[...] = cache_ref[...]
    accum_new_ref[...] = accum_ref[...]
    count = refresh_ref.shape[0]
    for i in range(count):
        block = refresh_ref[i]
        at = pl.ds(pl.multiple_of(block * BLOCK, BLOCK), BLOCK)
        flush = sums_ref[i * BLOCK : (i + 1) * BLOCK, :] / (1.0 + clock_ref[block].astype(F32))
        cache_next, accum_next = adagrad(cache_ref[at, :], accum_ref[at, :], flush)
        cache_new_ref[at, :] = cache_next
        accum_new_ref[at, :] = accum_next
    out_grad_ref[...] = sums_ref[count * BLOCK : count * BLOCK + 8, :]


def cold_kernel(owned_ref, incoming_ref, grad_ref):
    grad_ref[...] = dot(owned_ref[...], incoming_ref[...])


def two_kernel(own_ref, other_ref, sum_ref):
    sum_ref[...] = own_ref[...] + other_ref[...]


def update_kernel(own_ref, other_ref, table_ref, accum_ref, table_new_ref, accum_new_ref):
    table_next, accum_next = adagrad(table_ref[...], accum_ref[...], own_ref[...] + other_ref[...])
    table_new_ref[...] = table_next
    accum_new_ref[...] = accum_next


def swap(x, axis):
    return lax.all_to_all(x, axis, split_axis=0, concat_axis=0, tiled=True)


def from_rep(piece, distance):
    return lax.ppermute(piece, "rep", [(i, i ^ distance) for i in range(4)])


def local(
    hot_ids,
    cold_owner,
    cold_offset,
    labels,
    top_weight,
    out_weight,
    cold_table,
    cold_accum,
    hot_cache,
    hot_accum,
    pending,
    refresh_blocks,
    block_clock,
):
    samples, feats = hot_ids.shape
    lookups = cold_offset.shape[0]
    own_rows, width = cold_table.shape
    hot_count = hot_cache.shape[0]
    inputs_width, hidden_width = top_weight.shape
    owners = lax.axis_size(DP)
    slots = owners * SLOTS
    groups = lookups // BLOCK
    place = jnp.stack([lax.axis_index("dp_2"), lax.axis_index("rep")]).astype(jnp.int32)

    request, target = call(
        requests_kernel,
        [((owners, BLOCK), F32), ((lookups, BLOCK), F32)],
        (cold_owner.reshape(groups, BLOCK), cold_offset.reshape(groups, BLOCK)),
        loads=(0, 1),
        kept=(1,),
    )
    asked = swap(request.reshape(owners, 1, BLOCK), DP).reshape(owners, BLOCK)
    target_rows, hot_in, hot_put, narrow = call(
        masks_kernel,
        [
            ((8, lookups), F32),
            ((samples, feats * width), BF16),
            ((hot_count, samples * feats), BF16),
            ((own_rows, width), BF16),
        ],
        (target, hot_ids.T, hot_cache, cold_table),
        loads=(1, 2, 3),
        held=(0,),
        kept=(0, 1, 2, 3),
    )
    (found,) = call(rows_kernel, [((slots, width), BF16)], (asked, narrow), held=(1,), scratch=[((slots, width), F32)])
    returned = swap(found.reshape(owners, SLOTS, width), DP).reshape(slots, width)
    (owned,) = call(owned_kernel, [((own_rows, slots), BF16)], (asked,))
    outgoing, inputs, dhidden, hot_dx, head = call(
        layer_kernel,
        [
            ((slots, width), BF16),
            ((samples, inputs_width), BF16),
            ((samples, hidden_width), BF16),
            ((samples * feats, width), BF16),
            ((8, BLOCK), F32),
        ],
        (returned, target, target_rows, hot_in, top_weight, out_weight.reshape(1, hidden_width), labels.reshape(2, BLOCK)),
        loads=(4, 5, 6),
        held=(1, 2, 3),
        kept=(1, 2, 3, 4),
    )
    half = inputs_width // 2
    broad = hidden_width + BLOCK
    packed = broad + 2 * BLOCK
    near = lax.axis_size("dp_1")
    far = lax.axis_size("dp_0")
    plane_size = lax.axis_size(PLANE)
    send, picked, pending_new = call(
        send_kernel,
        [((half, packed), I16), ((plane_size * far, BLOCK), F32), ((hot_count, width), F32)],
        (place, refresh_blocks, inputs, dhidden, hot_put, hot_dx, head, pending),
        smem=2,
        loads=(7,),
        held=(2, 3, 4, 5, 6),
        kept=(1,),
    )
    send, outgoing = lax.optimization_barrier((send, outgoing))
    received = lax.ppermute(send, "dp_2", [(0, 1), (1, 0)])
    incoming = swap(outgoing.reshape(owners, SLOTS, width), DP).reshape(slots, width)
    pieces = call(
        pair_kernel,
        [((half // 4, broad), F32)] + [((half // 4, packed), I16)] * 3,
        (place, inputs, dhidden, picked, received),
        smem=1,
        held=(1, 2, 3),
    )
    two, one, three = (from_rep(pieces[d], d) for d in (2, 1, 3))
    (paired,) = call(four_kernel, [((half // 4, packed), I16)], (pieces[0], one, two, three))
    paired, incoming = lax.optimization_barrier((paired, incoming))
    plane = swap(paired.reshape(near, far, packed), "dp_1")
    tall = hidden_width // BLOCK
    (columns,) = call(plane_kernel, [((far, tall + far, BLOCK), F32)], (plane,))
    columns = swap(columns, "dp_0")
    top, copies = call(column_kernel, [((tall, BLOCK), F32), ((plane_size, far, BLOCK), F32)], (columns,))
    sums = swap(copies, PLANE).reshape(plane_size * far, BLOCK)

    (grad,) = call(cold_kernel, [((own_rows, width), F32)], (owned, incoming))
    (grad,) = call(two_kernel, [((own_rows, width), F32)], (grad, from_rep(grad, 1)))
    cold_table_new, cold_accum_new = call(
        update_kernel, [((own_rows, width), F32)] * 2, (grad, from_rep(grad, 3), cold_table, cold_accum)
    )
    hot_cache_new, hot_accum_new, out_grad = call(
        hot_kernel,
        [((hot_count, width), F32)] * 2 + [((8, BLOCK), F32)],
        (refresh_blocks, block_clock, sums, hot_cache, hot_accum),
        smem=2,
    )
    return (
        cold_table_new,
        cold_accum_new,
        hot_cache_new,
        hot_accum_new,
        pending_new,
        top.reshape(1, hidden_width),
        out_grad.reshape(hidden_width),
    )


def solution(mesh):
    split = Mesh(mesh.devices.reshape(16, 4, 2, mesh.shape["rep"]), ("dp_0", "dp_1", "dp_2", "rep"))
    in_specs = (
        P(DP_REP, None),
        P(DP_REP, None),
        P(DP_REP),
        P(DP_REP),
        P(),
        P(),
        P(DP, None),
        P(DP, None),
        P(),
        P(),
        P(DP_REP, None),
        P(),
        P(),
    )
    out_specs = (P(DP, None), P(DP, None), P(), P(), P(DP_REP, None), P(DP_REP, None), P())
    return jax.shard_map(local, mesh=split, in_specs=in_specs, out_specs=out_specs, check_vma=False)
```

```python
import jax
import jax.numpy as jnp
from jax import lax
from jax.experimental import pallas as pl
from jax.experimental.pallas import tpu as pltpu
from jax.sharding import Mesh
from jax.sharding import PartitionSpec as P

BLOCK = 128
SLOTS = 8
REFRESHED = 3
DP = ("dp_0", "dp_1", "dp_2")
DP_REP = ("dp_0", "dp_1", "dp_2", "rep")
PLANE = ("dp_2", "rep", "dp_1")

step_size = 0.5
epsilon = 1e-08

F32 = jnp.float32
BF16 = jnp.bfloat16
I16 = jnp.int16
LN2 = 0.6931471805599453
FINE = 65534.0
EXACT = lax.Precision.HIGHEST
VMEM = pl.BlockSpec(memory_space=pltpu.VMEM)
HBM = pl.BlockSpec(memory_space=pltpu.HBM)
SMEM = pl.BlockSpec(memory_space=pltpu.SMEM)


class Loaded:
    def __init__(self, source, held, sem):
        self.copy = pltpu.make_async_copy(source, held, sem)
        self.held = held
        self.copy.start()

    def wait(self):
        self.copy.wait()
        return self.held


def call(kernel, outs, args, smem=0, scratch=(), loads=(), held=(), kept=(), flops=10**9):
    own = len(scratch)
    ins = len(args)

    def body(*refs):
        given = list(refs[:ins])
        rest = refs[ins + len(outs) :]
        for j, i in enumerate(loads):
            given[i] = Loaded(given[i], rest[own + j], rest[own + len(loads) + j])
        kernel(*given, *refs[ins : ins + len(outs)], *rest[:own])

    specs = [SMEM] * smem + [VMEM] * (ins - smem)
    args = list(args)
    for i in loads:
        specs[i] = HBM
        args[i] = pltpu.with_memory_space_constraint(args[i], pltpu.HBM)
    for i in held:
        args[i] = pltpu.with_memory_space_constraint(args[i], pltpu.VMEM)
    return pl.pallas_call(
        body,
        out_shape=[(pltpu.VMEM if i in kept else jax.ShapeDtypeStruct)(s, d) for i, (s, d) in enumerate(outs)],
        in_specs=specs,
        out_specs=[VMEM] * len(outs),
        scratch_shapes=[pltpu.VMEM(s, d) for s, d in scratch]
        + [pltpu.VMEM(args[i].shape, args[i].dtype) for i in loads]
        + [pltpu.SemaphoreType.DMA for _ in loads],
        compiler_params=pltpu.CompilerParams(vmem_limit_bytes=16 * 2**20),
        cost_estimate=pl.CostEstimate(flops=flops, bytes_accessed=flops // 100, transcendentals=0),
    )(*args)


def iota(shape, dim):
    return lax.broadcasted_iota(jnp.int32, shape, dim)


def iota_f(shape, dim):
    return iota(shape, dim).astype(F32)


def ones_where(mask):
    return jnp.where(mask, 1.0, 0.0).astype(BF16)


def column_of(row, eye):
    return jnp.sum(jnp.where(eye, row, 0.0), axis=1, keepdims=True)


def dot(a, b, precision=None):
    return jnp.dot(a, b, preferred_element_type=F32, precision=precision)


def dot_t(a, b):
    return lax.dot_general(a, b, (((1,), (1,)), ((), ())), preferred_element_type=F32)


def power(exponent):
    return jnp.exp(exponent * LN2)


def exponent_of(top):
    return jnp.ceil(jnp.log(jnp.maximum(top, 1e-30)) * (1.0 / LN2) + 0.01) - 15.0


def pack(values, packed_ref):
    wide = values.shape[1] - BLOCK
    top, hot = values[:, :wide], values[:, wide:]
    top_exponent = exponent_of(jnp.max(jnp.abs(top), axis=1, keepdims=True))
    hot_exponent = exponent_of(jnp.max(jnp.abs(hot), axis=1, keepdims=True))
    lane = iota((values.shape[0], BLOCK), 1)
    hot = hot * power(-hot_exponent)
    coarse = jnp.round(hot)
    at = 0
    for part in (
        jnp.round(top * power(-top_exponent)),
        coarse,
        jnp.round((hot - coarse) * FINE),
        jnp.where(lane < BLOCK // 2, top_exponent, hot_exponent),
    ):
        packed_ref[:, at : at + part.shape[1]] = part.astype(jnp.int32).astype(I16)
        at += part.shape[1]


def unpack(packed):
    values = packed.astype(jnp.int32).astype(F32)
    wide = values.shape[1] - 3 * BLOCK
    coarse, fine, exponents = (values[:, wide + i * BLOCK : wide + (i + 1) * BLOCK] for i in range(3))
    top = values[:, :wide] * power(exponents[:, :1])
    hot = (coarse + fine * (1.0 / FINE)) * power(exponents[:, BLOCK - 1 :])
    return jnp.concatenate([top, hot], axis=1)


def requests_kernel(owner_ref, offset_ref, request_ref, target_ref):
    square = (BLOCK, BLOCK)
    eye = iota(square, 0) == iota(square, 1)
    owner = owner_ref.wait()[...].astype(F32)
    offset = offset_ref.wait()[...].astype(F32)
    groups = owner.shape[0]
    lookups = groups * BLOCK
    rows = [owner[s : s + 1, :] for s in range(groups)]
    owner_col = jnp.concatenate([column_of(row, eye) for row in rows], axis=0)
    offset_col = jnp.concatenate([column_of(offset[s : s + 1, :], eye) for s in range(groups)], axis=0)
    lane = iota_f((lookups, BLOCK), 1)
    named = owner_col == lane
    before = ones_where(iota((lookups, lookups), 0) > iota((lookups, lookups), 1))
    earlier = dot(before, ones_where(named))
    rank = jnp.sum(jnp.where(named, earlier, 0.0), axis=1, keepdims=True)
    target_ref[...] = jnp.broadcast_to(owner_col * SLOTS + rank, (lookups, BLOCK))
    placed = jnp.where(rank == lane, offset_col, 0.0)
    sublane = iota_f(square, 0)
    named_t = jnp.concatenate([jnp.where(sublane == row, 1.0, 0.0) for row in rows], axis=1)
    request_ref[...] = dot(named_t, placed, EXACT)


def rows_kernel(asked_ref, table_ref, rows_ref, wide_ref):
    asked = asked_ref[...]
    table = table_ref[...]
    sources = asked.shape[0]
    line = iota_f((sources, table.shape[0]), 1)
    for slot in range(SLOTS):
        chosen = ones_where(asked[:, slot : slot + 1] == line)
        wide_ref[pl.ds(slot, sources, stride=SLOTS), :] = dot(chosen, table)
    rows_ref[...] = wide_ref[...].astype(BF16)


def owned_kernel(asked_ref, owned_ref):
    slots = owned_ref.shape[1]
    source, line = iota((BLOCK, slots), 0), iota((BLOCK, slots), 1)
    spread = dot(asked_ref[...], jnp.where(source == line % SLOTS, 1.0, 0.0), EXACT)
    wanted = jnp.sum(jnp.where(source == line // SLOTS, spread, 0.0), axis=0, keepdims=True)
    owned_ref[...] = ones_where(iota_f(owned_ref.shape, 0) == wanted)


def masks_kernel(target_ref, hot_ref, cache_ref, table_ref, rows_ref, hot_in_ref, hot_rows_ref, narrow_ref):
    square = (BLOCK, BLOCK)
    eye = iota(square, 0) == iota(square, 1)
    hot = hot_ref.wait()[...].astype(F32)
    feats, samples = hot.shape
    for k in range(feats):
        mine = target_ref[pl.ds(k, samples, stride=feats), :]
        for h in range(samples // BLOCK):
            at = k * samples + h * BLOCK
            row = jnp.sum(jnp.where(eye, mine[h * BLOCK : (h + 1) * BLOCK, :], 0.0), axis=0, keepdims=True)
            rows_ref[:, at : at + BLOCK] = jnp.broadcast_to(row, (8, BLOCK))
    cache = cache_ref.wait()[...].astype(BF16)
    hot_count = cache.shape[0]
    hot_lane = iota_f((BLOCK, hot_count), 1)
    for k in range(feats):
        for h in range(samples // BLOCK):
            at = k * samples + h * BLOCK
            row = hot[k : k + 1, h * BLOCK : (h + 1) * BLOCK]
            hot_rows_ref[:, at : at + BLOCK] = jnp.broadcast_to(row, (8, BLOCK))
            chosen = ones_where(column_of(row, eye) == hot_lane)
            hot_in_ref[h * BLOCK : (h + 1) * BLOCK, k * BLOCK : (k + 1) * BLOCK] = dot(chosen, cache).astype(BF16)
    narrow_ref[...] = table_ref.wait()[...].astype(BF16)


def layer_kernel(
    returned_ref, target_ref, rows_ref, hot_in_ref, weight_ref, out_weight_ref, labels_ref,
    outgoing_ref, inputs_ref, dhidden_ref, hot_dx_ref, head_ref,
):
    square = (BLOCK, BLOCK)
    eye = iota(square, 0) == iota(square, 1)
    width = BLOCK
    samples = target_ref.shape[0] // 2
    lane = iota_f((samples, BLOCK), 1)
    slots = returned_ref.shape[0]
    mine = [target_ref[pl.ds(k, samples, stride=2), :] for k in range(2)]
    take = [
        jnp.concatenate([ones_where(t == lane + float(b)) for b in range(0, slots, BLOCK)], axis=1) for t in mine
    ]
    cold = dot(jnp.concatenate(take, axis=0), returned_ref[...]).astype(BF16)
    inputs = jnp.concatenate([hot_in_ref[...], cold[:samples], cold[samples:]], axis=1)
    inputs_ref[...] = inputs
    weight = weight_ref[...]
    out_weight = out_weight_ref.wait()[...]
    preact = dot(inputs, weight)
    gates = jax.nn.sigmoid(preact)
    hidden = (preact * gates).astype(BF16).astype(F32)
    logits = jnp.sum(hidden * out_weight, axis=1, keepdims=True)
    labels = labels_ref.wait()[...].astype(F32)
    label = jnp.concatenate([column_of(labels[h : h + 1, :], eye) for h in range(samples // BLOCK)], axis=0)
    errors = jax.nn.sigmoid(logits) - label
    slope = gates * (1.0 + preact * (1.0 - gates))
    dhidden = (errors * out_weight * slope).astype(BF16)
    dhidden_ref[...] = dhidden
    dinputs = dot_t(dhidden, weight).astype(BF16)
    cold_dx = jnp.concatenate([dinputs[:, 2 * width : 3 * width], dinputs[:, 3 * width :]], axis=0)
    put = ones_where(iota_f((outgoing_ref.shape[0], rows_ref.shape[1]), 0) == rows_ref[:1, :])
    outgoing_ref[...] = dot(put, cold_dx).astype(BF16)
    hot_dx_ref[:samples, :] = dinputs[:, :width]
    hot_dx_ref[samples:, :] = dinputs[:, width : 2 * width]
    head = jnp.sum(errors * hidden, axis=0, keepdims=True)
    for b in range(head_ref.shape[0]):
        head_ref[b : b + 1, :] = head[:, b * BLOCK : (b + 1) * BLOCK]


def half_of_top(core, rep, inputs, dhidden):
    shape = (inputs.shape[1] // 2, inputs.shape[1])
    line = iota(shape, 0)
    row = (line & 15) * 32 + ((line >> 4) & 3) * 8 + core * 4 + ((line >> 6) ^ rep)
    ordered = dot_t(ones_where(row == iota(shape, 1)), inputs).astype(BF16)
    return dot(ordered, dhidden)


def hot_rows(picked_ref, core, rep, piece):
    count = picked_ref.shape[0] // 8
    return picked_ref[pl.ds(pl.multiple_of((core * 4 + (rep ^ piece)) * count, count), count), :]


def send_kernel(
    control_ref, inputs_ref, dhidden_ref, hot_rows_ref, hot_dx_ref, head_ref, pending_ref,
    send_ref, picked_ref, pending_new_ref,
):
    put = ones_where(iota_f((pending_ref.shape[0], hot_rows_ref.shape[1]), 0) == hot_rows_ref[:1, :])
    pending_new_ref[...] = dot(put, hot_dx_ref[...]) + pending_ref[...]
    count = REFRESHED
    blocks = [pl.ds(pl.multiple_of(control_ref[2 + i] * BLOCK, BLOCK), BLOCK) for i in range(count)]
    for i, at in enumerate(blocks):
        picked_ref[i * BLOCK : (i + 1) * BLOCK, :] = pending_new_ref[at, :]
    end = count * BLOCK
    picked_ref[end : end + 8, :] = head_ref[...]
    picked_ref[end + 8 :, :] = jnp.zeros((picked_ref.shape[0] - end - 8, BLOCK), F32)
    for at in blocks:
        pending_new_ref[at, :] = jnp.zeros((BLOCK, BLOCK), F32)
    core, rep = 1 - control_ref[0], control_ref[1]
    top = half_of_top(core, rep, inputs_ref[...], dhidden_ref[...])
    hot = jnp.concatenate([hot_rows(picked_ref, core, rep, d) for d in range(4)], axis=0)
    pack(jnp.concatenate([top, hot], axis=1), send_ref)


def pair_kernel(control_ref, inputs_ref, dhidden_ref, picked_ref, received_ref, own_ref, *pieces):
    core, rep = control_ref[0], control_ref[1]
    top = half_of_top(core, rep, inputs_ref[...], dhidden_ref[...])
    tall = own_ref.shape[0]
    for d, piece in enumerate((own_ref, *pieces)):
        rows = slice(d * tall, (d + 1) * tall)
        mine = jnp.concatenate([top[rows], hot_rows(picked_ref, core, rep, d)], axis=1)
        both = mine + unpack(received_ref[rows, :])
        if d:
            pack(both, piece)
        else:
            piece[...] = both


def four_kernel(own_ref, one_ref, two_ref, three_ref, sum_ref):
    total = (own_ref[...] + unpack(one_ref[...])) + (unpack(two_ref[...]) + unpack(three_ref[...]))
    pack(total, sum_ref)


def plane_kernel(parts_ref, out_ref):
    total = unpack(parts_ref[0])
    for i in range(1, parts_ref.shape[0]):
        total = total + unpack(parts_ref[i])
    wide = total.shape[1] - BLOCK
    tall = wide // BLOCK
    for b in range(tall):
        out_ref[:, b, :] = total[:, b * BLOCK : (b + 1) * BLOCK]
    for z in range(out_ref.shape[0]):
        out_ref[z, tall:, :] = total[:, wide:]


def column_kernel(parts_ref, top_ref, copies_ref):
    total = parts_ref[0]
    for i in range(1, parts_ref.shape[0]):
        total = total + parts_ref[i]
    tall = top_ref.shape[0]
    top_ref[...] = total[:tall]
    for i in range(copies_ref.shape[0]):
        copies_ref[i] = total[tall:]


def adagrad(table_rows, accum_rows, gradient):
    accum_next = accum_rows + gradient * gradient
    return (table_rows - step_size * gradient / (jnp.sqrt(accum_next) + epsilon), accum_next)


def hot_kernel(control_ref, sums_ref, cache_ref, accum_ref, cache_new_ref, accum_new_ref, out_grad_ref):
    cache_new_ref[...] = cache_ref[...]
    accum_new_ref[...] = accum_ref[...]
    count = REFRESHED
    for i in range(count):
        block = control_ref[2 + i]
        at = pl.ds(pl.multiple_of(block * BLOCK, BLOCK), BLOCK)
        flush = sums_ref[i * BLOCK : (i + 1) * BLOCK, :] / (1.0 + control_ref[2 + count + block].astype(F32))
        cache_next, accum_next = adagrad(cache_ref[at, :], accum_ref[at, :], flush)
        cache_new_ref[at, :] = cache_next
        accum_new_ref[at, :] = accum_next
    out_grad_ref[...] = sums_ref[count * BLOCK : count * BLOCK + 8, :]


def cold_kernel(owned_ref, incoming_ref, grad_ref):
    grad_ref[...] = dot(owned_ref[...], incoming_ref[...])


def two_kernel(own_ref, other_ref, sum_ref):
    sum_ref[...] = own_ref[...] + other_ref[...]


def update_kernel(own_ref, other_ref, table_ref, accum_ref, table_new_ref, accum_new_ref):
    table_next, accum_next = adagrad(table_ref[...], accum_ref[...], own_ref[...] + other_ref[...])
    table_new_ref[...] = table_next
    accum_new_ref[...] = accum_next


def swap(x, axis):
    return lax.all_to_all(x, axis, split_axis=0, concat_axis=0, tiled=True)


def from_rep(piece, distance):
    return lax.ppermute(piece, "rep", [(i, i ^ distance) for i in range(4)])


def local(
    hot_ids,
    cold_owner,
    cold_offset,
    labels,
    top_weight,
    out_weight,
    cold_table,
    cold_accum,
    hot_cache,
    hot_accum,
    pending,
    refresh_blocks,
    block_clock,
):
    samples, feats = hot_ids.shape
    lookups = cold_offset.shape[0]
    own_rows, width = cold_table.shape
    hot_count = hot_cache.shape[0]
    inputs_width, hidden_width = top_weight.shape
    owners = lax.axis_size(DP)
    slots = owners * SLOTS
    groups = lookups // BLOCK
    place = jnp.stack([lax.axis_index("dp_2"), lax.axis_index("rep")]).astype(jnp.int32)
    control = jnp.concatenate([place, refresh_blocks, block_clock])

    request, target = call(
        requests_kernel,
        [((owners, BLOCK), F32), ((lookups, BLOCK), F32)],
        (cold_owner.reshape(groups, BLOCK), cold_offset.reshape(groups, BLOCK)),
        loads=(0, 1),
        kept=(1,),
    )
    asked = swap(request.reshape(owners, 1, BLOCK), DP).reshape(owners, BLOCK)
    target_rows, hot_in, hot_id_rows, narrow = call(
        masks_kernel,
        [
            ((8, lookups), F32),
            ((samples, feats * width), BF16),
            ((8, samples * feats), F32),
            ((own_rows, width), BF16),
        ],
        (target, hot_ids.T, hot_cache, cold_table),
        loads=(1, 2, 3),
        held=(0,),
        kept=(0, 1, 2, 3),
    )
    (found,) = call(rows_kernel, [((slots, width), BF16)], (asked, narrow), held=(1,), scratch=[((slots, width), F32)])
    returned = swap(found.reshape(owners, SLOTS, width), DP).reshape(slots, width)
    (owned,) = call(owned_kernel, [((own_rows, slots), BF16)], (asked,))
    outgoing, inputs, dhidden, hot_dx, head = call(
        layer_kernel,
        [
            ((slots, width), BF16),
            ((samples, inputs_width), BF16),
            ((samples, hidden_width), BF16),
            ((samples * feats, width), BF16),
            ((8, BLOCK), F32),
        ],
        (returned, target, target_rows, hot_in, top_weight, out_weight.reshape(1, hidden_width), labels.reshape(2, BLOCK)),
        loads=(5, 6),
        held=(1, 2, 3),
        kept=(1, 2, 3, 4),
    )
    half = inputs_width // 2
    broad = hidden_width + BLOCK
    packed = broad + 2 * BLOCK
    near = lax.axis_size("dp_1")
    far = lax.axis_size("dp_0")
    plane_size = lax.axis_size(PLANE)
    send, picked, pending_new = call(
        send_kernel,
        [((half, packed), I16), ((plane_size * far, BLOCK), F32), ((hot_count, width), F32)],
        (control, inputs, dhidden, hot_id_rows, hot_dx, head, pending),
        smem=1,
        held=(1, 2, 3, 4, 5),
        kept=(1,),
        flops=10**9,
    )
    send, outgoing = lax.optimization_barrier((send, outgoing))
    received = lax.ppermute(send, "dp_2", [(0, 1), (1, 0)])
    incoming = swap(outgoing.reshape(owners, SLOTS, width), DP).reshape(slots, width)
    pieces = call(
        pair_kernel,
        [((half // 4, broad), F32)] + [((half // 4, packed), I16)] * 3,
        (control, inputs, dhidden, picked, received),
        smem=1,
        held=(1, 2, 3),
    )
    two, one, three = (from_rep(pieces[d], d) for d in (2, 1, 3))
    (paired,) = call(four_kernel, [((half // 4, packed), I16)], (pieces[0], one, two, three))
    paired, incoming = lax.optimization_barrier((paired, incoming))
    plane = swap(paired.reshape(near, far, packed), "dp_1")
    tall = hidden_width // BLOCK
    (columns,) = call(plane_kernel, [((far, tall + far, BLOCK), F32)], (plane,))
    columns = swap(columns, "dp_0")
    top, copies = call(column_kernel, [((tall, BLOCK), F32), ((plane_size, far, BLOCK), F32)], (columns,))
    sums = swap(copies, PLANE).reshape(plane_size * far, BLOCK)

    (grad,) = call(cold_kernel, [((own_rows, width), F32)], (owned, incoming))
    (grad,) = call(two_kernel, [((own_rows, width), F32)], (grad, from_rep(grad, 1)))
    cold_table_new, cold_accum_new = call(
        update_kernel, [((own_rows, width), F32)] * 2, (grad, from_rep(grad, 3), cold_table, cold_accum)
    )
    hot_cache_new, hot_accum_new, out_grad = call(
        hot_kernel,
        [((hot_count, width), F32)] * 2 + [((8, BLOCK), F32)],
        (control, sums, hot_cache, hot_accum),
        smem=1,
    )
    return (
        cold_table_new,
        cold_accum_new,
        hot_cache_new,
        hot_accum_new,
        pending_new,
        top.reshape(1, hidden_width),
        out_grad.reshape(hidden_width),
    )


def solution(mesh):
    split = Mesh(mesh.devices.reshape(16, 4, 2, mesh.shape["rep"]), ("dp_0", "dp_1", "dp_2", "rep"))
    in_specs = (
        P(DP_REP, None),
        P(DP_REP, None),
        P(DP_REP),
        P(DP_REP),
        P(),
        P(),
        P(DP, None),
        P(DP, None),
        P(),
        P(),
        P(DP_REP, None),
        P(),
        P(),
    )
    out_specs = (P(DP, None), P(DP, None), P(), P(), P(DP_REP, None), P(DP_REP, None), P())
    return jax.shard_map(local, mesh=split, in_specs=in_specs, out_specs=out_specs, check_vma=False)
```

```python
import jax
import jax.numpy as jnp
from jax import lax
from jax.experimental import pallas as pl
from jax.experimental.pallas import tpu as pltpu
from jax.sharding import Mesh
from jax.sharding import PartitionSpec as P

BLOCK = 128
SLOTS = 8
REFRESHED = 3
DP = ("dp_0", "dp_1", "dp_2")
DP_REP = ("dp_0", "dp_1", "dp_2", "rep")
PLANE = ("dp_2", "rep", "dp_1")

step_size = 0.5
epsilon = 1e-08

F32 = jnp.float32
BF16 = jnp.bfloat16
I16 = jnp.int16
LN2 = 0.6931471805599453
FINE = 65534.0
SENT = 18
HELD = 13
EXACT = lax.Precision.HIGHEST
VMEM = pl.BlockSpec(memory_space=pltpu.VMEM)
HBM = pl.BlockSpec(memory_space=pltpu.HBM)
SMEM = pl.BlockSpec(memory_space=pltpu.SMEM)


class Loaded:
    def __init__(self, source, held, sem):
        self.copy = pltpu.make_async_copy(source, held, sem)
        self.held = held
        self.copy.start()

    def wait(self):
        self.copy.wait()
        return self.held


def call(kernel, outs, args, smem=0, scratch=(), loads=(), held=(), kept=(), flops=10**9):
    own = len(scratch)
    ins = len(args)

    def body(*refs):
        given = list(refs[:ins])
        rest = refs[ins + len(outs) :]
        for j, i in enumerate(loads):
            given[i] = Loaded(given[i], rest[own + j], rest[own + len(loads) + j])
        kernel(*given, *refs[ins : ins + len(outs)], *rest[:own])

    specs = [SMEM] * smem + [VMEM] * (ins - smem)
    args = list(args)
    for i in loads:
        specs[i] = HBM
        args[i] = pltpu.with_memory_space_constraint(args[i], pltpu.HBM)
    for i in held:
        args[i] = pltpu.with_memory_space_constraint(args[i], pltpu.VMEM)
    return pl.pallas_call(
        body,
        out_shape=[(pltpu.VMEM if i in kept else jax.ShapeDtypeStruct)(s, d) for i, (s, d) in enumerate(outs)],
        in_specs=specs,
        out_specs=[VMEM] * len(outs),
        scratch_shapes=[pltpu.VMEM(s, d) for s, d in scratch]
        + [pltpu.VMEM(args[i].shape, args[i].dtype) for i in loads]
        + [pltpu.SemaphoreType.DMA for _ in loads],
        compiler_params=pltpu.CompilerParams(vmem_limit_bytes=16 * 2**20),
        cost_estimate=pl.CostEstimate(flops=flops, bytes_accessed=flops // 100, transcendentals=0),
    )(*args)


def iota(shape, dim):
    return lax.broadcasted_iota(jnp.int32, shape, dim)


def iota_f(shape, dim):
    return iota(shape, dim).astype(F32)


def ones_where(mask):
    return jnp.where(mask, 1.0, 0.0).astype(BF16)


def column_of(row, eye):
    return jnp.sum(jnp.where(eye, row, 0.0), axis=1, keepdims=True)


def dot(a, b, precision=None):
    return jnp.dot(a, b, preferred_element_type=F32, precision=precision)


def dot_t(a, b):
    return lax.dot_general(a, b, (((1,), (1,)), ((), ())), preferred_element_type=F32)


def power(exponent):
    return jnp.exp(exponent * LN2)


def exponent_of(top):
    return jnp.ceil(jnp.log(jnp.maximum(top, 1e-30)) * (1.0 / LN2) + 0.01) - 15.0


def pack(values, packed_ref):
    wide = values.shape[1] - BLOCK
    top, hot = values[:, :wide], values[:, wide:]
    top_exponent = exponent_of(jnp.max(jnp.abs(top), axis=1, keepdims=True))
    hot_exponent = exponent_of(jnp.max(jnp.abs(hot), axis=1, keepdims=True))
    lane = iota((values.shape[0], BLOCK), 1)
    hot = hot * power(-hot_exponent)
    coarse = jnp.round(hot)
    at = 0
    for part in (
        jnp.round(top * power(-top_exponent)),
        coarse,
        jnp.round((hot - coarse) * FINE),
        jnp.where(lane < BLOCK // 2, top_exponent, hot_exponent),
    ):
        packed_ref[:, at : at + part.shape[1]] = part.astype(jnp.int32).astype(I16)
        at += part.shape[1]


def unpack(packed):
    values = packed.astype(jnp.int32).astype(F32)
    wide = values.shape[1] - 3 * BLOCK
    coarse, fine, exponents = (values[:, wide + i * BLOCK : wide + (i + 1) * BLOCK] for i in range(3))
    top = values[:, :wide] * power(exponents[:, :1])
    hot = (coarse + fine * (1.0 / FINE)) * power(exponents[:, BLOCK - 1 :])
    return jnp.concatenate([top, hot], axis=1)


def requests_kernel(owner_ref, offset_ref, request_ref, target_ref):
    square = (BLOCK, BLOCK)
    eye = iota(square, 0) == iota(square, 1)
    owner = owner_ref.wait()[...].astype(F32)
    offset = offset_ref.wait()[...].astype(F32)
    groups = owner.shape[0]
    lookups = groups * BLOCK
    rows = [owner[s : s + 1, :] for s in range(groups)]
    owner_col = jnp.concatenate([column_of(row, eye) for row in rows], axis=0)
    offset_col = jnp.concatenate([column_of(offset[s : s + 1, :], eye) for s in range(groups)], axis=0)
    lane = iota_f((lookups, BLOCK), 1)
    named = owner_col == lane
    before = ones_where(iota((lookups, lookups), 0) > iota((lookups, lookups), 1))
    earlier = dot(before, ones_where(named))
    rank = jnp.sum(jnp.where(named, earlier, 0.0), axis=1, keepdims=True)
    target_ref[...] = jnp.broadcast_to(owner_col * SLOTS + rank, (lookups, BLOCK))
    placed = jnp.where(rank == lane, offset_col, 0.0)
    sublane = iota_f(square, 0)
    named_t = jnp.concatenate([jnp.where(sublane == row, 1.0, 0.0) for row in rows], axis=1)
    request_ref[...] = dot(named_t, placed, EXACT)


def rows_kernel(asked_ref, table_ref, rows_ref, wide_ref):
    asked = asked_ref[...]
    table = table_ref[...]
    sources = asked.shape[0]
    line = iota_f((sources, table.shape[0]), 1)
    for slot in range(SLOTS):
        chosen = ones_where(asked[:, slot : slot + 1] == line)
        wide_ref[pl.ds(slot, sources, stride=SLOTS), :] = dot(chosen, table)
    rows_ref[...] = wide_ref[...].astype(BF16)


def owned_kernel(asked_ref, owned_ref):
    slots = owned_ref.shape[1]
    source, line = iota((BLOCK, slots), 0), iota((BLOCK, slots), 1)
    spread = dot(asked_ref[...], jnp.where(source == line % SLOTS, 1.0, 0.0), EXACT)
    wanted = jnp.sum(jnp.where(source == line // SLOTS, spread, 0.0), axis=0, keepdims=True)
    owned_ref[...] = ones_where(iota_f(owned_ref.shape, 0) == wanted)


def masks_kernel(
    target_ref, hot_ref, cache_ref, table_ref, labels_ref, out_weight_ref,
    rows_ref, hot_in_ref, hot_rows_ref, narrow_ref, label_ref, out_held_ref,
):
    square = (BLOCK, BLOCK)
    eye = iota(square, 0) == iota(square, 1)
    hot = hot_ref.wait()[...].astype(F32)
    feats, samples = hot.shape
    for k in range(feats):
        mine = target_ref[pl.ds(k, samples, stride=feats), :]
        for h in range(samples // BLOCK):
            at = k * samples + h * BLOCK
            row = jnp.sum(jnp.where(eye, mine[h * BLOCK : (h + 1) * BLOCK, :], 0.0), axis=0, keepdims=True)
            rows_ref[:, at : at + BLOCK] = jnp.broadcast_to(row, (8, BLOCK))
    cache = cache_ref.wait()[...].astype(BF16)
    hot_count = cache.shape[0]
    hot_lane = iota_f((BLOCK, hot_count), 1)
    for k in range(feats):
        for h in range(samples // BLOCK):
            at = k * samples + h * BLOCK
            row = hot[k : k + 1, h * BLOCK : (h + 1) * BLOCK]
            hot_rows_ref[:, at : at + BLOCK] = jnp.broadcast_to(row, (8, BLOCK))
            chosen = ones_where(column_of(row, eye) == hot_lane)
            hot_in_ref[h * BLOCK : (h + 1) * BLOCK, k * BLOCK : (k + 1) * BLOCK] = dot(chosen, cache).astype(BF16)
    narrow_ref[...] = table_ref.wait()[...].astype(BF16)
    labels = labels_ref.wait()[...].astype(F32)
    for h in range(labels.shape[0]):
        column = column_of(labels[h : h + 1, :], eye)
        label_ref[h * BLOCK : (h + 1) * BLOCK, :] = jnp.broadcast_to(column, (BLOCK, BLOCK))
    out_held_ref[...] = out_weight_ref.wait()[...]


def layer_kernel(
    returned_ref, target_ref, rows_ref, hot_in_ref, weight_ref, out_weight_ref, label_ref,
    outgoing_ref, inputs_ref, dhidden_ref, hot_dx_ref, head_ref,
):
    width = BLOCK
    samples = target_ref.shape[0] // 2
    lane = iota_f((samples, BLOCK), 1)
    slots = returned_ref.shape[0]
    mine = [target_ref[pl.ds(k, samples, stride=2), :] for k in range(2)]
    take = [
        jnp.concatenate([ones_where(t == lane + float(b)) for b in range(0, slots, BLOCK)], axis=1) for t in mine
    ]
    cold = dot(jnp.concatenate(take, axis=0), returned_ref[...]).astype(BF16)
    inputs = jnp.concatenate([hot_in_ref[...], cold[:samples], cold[samples:]], axis=1)
    inputs_ref[...] = inputs
    weight = weight_ref[...]
    out_weight = out_weight_ref[...]
    preact = dot(inputs, weight)
    gates = jax.nn.sigmoid(preact)
    hidden = (preact * gates).astype(BF16).astype(F32)
    logits = jnp.sum(hidden * out_weight, axis=1, keepdims=True)
    label = label_ref[:, :1]
    errors = jax.nn.sigmoid(logits) - label
    slope = gates * (1.0 + preact * (1.0 - gates))
    dhidden = (errors * out_weight * slope).astype(BF16)
    dhidden_ref[...] = dhidden
    dinputs = dot_t(dhidden, weight).astype(BF16)
    cold_dx = jnp.concatenate([dinputs[:, 2 * width : 3 * width], dinputs[:, 3 * width :]], axis=0)
    put = ones_where(iota_f((outgoing_ref.shape[0], rows_ref.shape[1]), 0) == rows_ref[:1, :])
    outgoing_ref[...] = dot(put, cold_dx).astype(BF16)
    hot_dx_ref[:samples, :] = dinputs[:, :width]
    hot_dx_ref[samples:, :] = dinputs[:, width : 2 * width]
    head = jnp.sum(errors * hidden, axis=0, keepdims=True)
    for b in range(head_ref.shape[0]):
        head_ref[b : b + 1, :] = head[:, b * BLOCK : (b + 1) * BLOCK]


def half_of_top(core, rep, inputs, dhidden):
    shape = (inputs.shape[1] // 2, inputs.shape[1])
    line = iota(shape, 0)
    row = (line & 15) * 32 + ((line >> 4) & 3) * 8 + core * 4 + ((line >> 6) ^ rep)
    ordered = dot_t(ones_where(row == iota(shape, 1)), inputs).astype(BF16)
    return dot(ordered, dhidden)


def hot_rows(picked_ref, core, rep, piece):
    count = picked_ref.shape[0] // 8
    return picked_ref[pl.ds(pl.multiple_of((core * 4 + (rep ^ piece)) * count, count), count), :]


def send_kernel(
    control_ref, inputs_ref, dhidden_ref, hot_rows_ref, hot_dx_ref, head_ref, pending_ref,
    send_ref, picked_ref, pending_new_ref, flat_ref,
):
    put = ones_where(iota_f((pending_ref.shape[0], hot_rows_ref.shape[1]), 0) == hot_rows_ref[:1, :])
    pending_new_ref[...] = dot(put, hot_dx_ref[...]) + pending_ref[...]
    count = REFRESHED
    blocks = [pl.ds(pl.multiple_of(control_ref[2 + i] * BLOCK, BLOCK), BLOCK) for i in range(count)]
    for i, at in enumerate(blocks):
        flat_ref[i * BLOCK : (i + 1) * BLOCK, :] = pending_new_ref[at, :]
    rows = HELD - 1
    count = picked_ref.shape[0] // 16
    part = iota((1, BLOCK), 1) // (8 * BLOCK // count)
    for i in range(count):
        at = i * 16
        q, p = divmod(i, count // 8)
        picked_ref[at : at + rows, :] = flat_ref[i * rows : (i + 1) * rows, :]
        picked_ref[at + rows : at + HELD, :] = jnp.where(part == p, head_ref[q : q + 1, :], 0.0)
        picked_ref[at + HELD : at + 16, :] = jnp.zeros((16 - HELD, BLOCK), F32)
    for at in blocks:
        pending_new_ref[at, :] = jnp.zeros((BLOCK, BLOCK), F32)
    core, rep = 1 - control_ref[0], control_ref[1]
    top = half_of_top(core, rep, inputs_ref[...], dhidden_ref[...])
    hot = jnp.concatenate([hot_rows(picked_ref, core, rep, d) for d in range(4)], axis=0)
    pack(jnp.concatenate([top, hot], axis=1), send_ref)


def pair_kernel(control_ref, inputs_ref, dhidden_ref, picked_ref, received_ref, own_ref, *pieces):
    core, rep = control_ref[0], control_ref[1]
    top = half_of_top(core, rep, inputs_ref[...], dhidden_ref[...])
    tall = own_ref.shape[0]
    for d, piece in enumerate((own_ref, *pieces)):
        rows = slice(d * tall, (d + 1) * tall)
        mine = jnp.concatenate([top[rows], hot_rows(picked_ref, core, rep, d)], axis=1)
        both = mine + unpack(received_ref[rows, :])
        if d:
            pack(both, piece)
        else:
            piece[...] = both


def four_kernel(own_ref, one_ref, two_ref, three_ref, sum_ref):
    total = (own_ref[...] + unpack(one_ref[...])) + (unpack(two_ref[...]) + unpack(three_ref[...]))
    pack(total, sum_ref)


def plane_kernel(parts_ref, out_ref):
    total = unpack(parts_ref[0])
    for i in range(1, parts_ref.shape[0]):
        total = total + unpack(parts_ref[i])
    count = total.shape[0]
    wide = total.shape[1] - BLOCK
    top, hot = total[:, :wide], total[:, wide:]
    top_exponent = exponent_of(jnp.max(jnp.abs(top), axis=1, keepdims=True))
    top = jnp.round(top * power(-top_exponent)).astype(jnp.int32)
    pairs = (top[:, : wide // 2] & 65535) | (top[:, wide // 2 :] << 16)
    most = jnp.max(jnp.max(jnp.abs(hot), axis=1, keepdims=True), axis=0, keepdims=True)
    hot_exponent = exponent_of(jnp.maximum(most, 1e-20)) - 15.0
    hot = jnp.round(hot * power(-hot_exponent)).astype(jnp.int32)
    lane = iota((count, BLOCK), 1)
    rows = [pairs[:, b : b + BLOCK] for b in range(0, wide // 2, BLOCK)]
    rows += [jnp.broadcast_to(hot[r : r + 1], (count, BLOCK)) for r in range(HELD)]
    rows += [jnp.where(lane < BLOCK // 2, top_exponent, hot_exponent).astype(jnp.int32)]
    for r, row in enumerate(rows):
        out_ref[pl.ds(r, count, stride=SENT), :] = row


def column_kernel(parts_ref, top_ref, copies_ref):
    tall = top_ref.shape[0] // 2
    low, high = jnp.zeros((tall, BLOCK), F32), jnp.zeros((tall, BLOCK), F32)
    hot = jnp.zeros((HELD, BLOCK), F32)
    for i in range(parts_ref.shape[0] // SENT):
        at = i * SENT
        scale = power(parts_ref[at + SENT - 1 : at + SENT, :].astype(F32))
        pairs = parts_ref[at : at + tall, :]
        low = low + ((pairs << 16) >> 16).astype(F32) * scale[:, :1]
        high = high + (pairs >> 16).astype(F32) * scale[:, :1]
        hot = hot + parts_ref[at + tall : at + tall + HELD, :].astype(F32) * scale[:, BLOCK - 1 :]
    top_ref[:tall, :] = low
    top_ref[tall:, :] = high
    for i in range(copies_ref.shape[0] // HELD):
        copies_ref[i * HELD : (i + 1) * HELD, :] = hot


def adagrad(table_rows, accum_rows, gradient):
    accum_next = accum_rows + gradient * gradient
    return (table_rows - step_size * gradient / (jnp.sqrt(accum_next) + epsilon), accum_next)


def hot_kernel(control_ref, sums_ref, cache_ref, accum_ref, cache_new_ref, accum_new_ref, out_grad_ref, flat_ref):
    cache_new_ref[...] = cache_ref[...]
    accum_new_ref[...] = accum_ref[...]
    rows = HELD - 1
    pieces = sums_ref.shape[0] // HELD
    for i in range(pieces):
        flat_ref[i * rows : (i + 1) * rows, :] = sums_ref[i * HELD : i * HELD + rows, :]
    for q in range(8):
        parts = [sums_ref[i * HELD + rows : (i + 1) * HELD, :] for i in range(q * pieces // 8, (q + 1) * pieces // 8)]
        out_grad_ref[q : q + 1, :] = sum(parts[1:], parts[0])
    count = REFRESHED
    for i in range(count):
        block = control_ref[2 + i]
        at = pl.ds(pl.multiple_of(block * BLOCK, BLOCK), BLOCK)
        flush = flat_ref[i * BLOCK : (i + 1) * BLOCK, :] / (1.0 + control_ref[2 + count + block].astype(F32))
        cache_next, accum_next = adagrad(cache_ref[at, :], accum_ref[at, :], flush)
        cache_new_ref[at, :] = cache_next
        accum_new_ref[at, :] = accum_next


def cold_kernel(owned_ref, incoming_ref, grad_ref):
    grad_ref[...] = dot(owned_ref[...], incoming_ref[...])


def two_kernel(own_ref, other_ref, sum_ref):
    sum_ref[...] = own_ref[...] + other_ref[...]


def update_kernel(own_ref, other_ref, table_ref, accum_ref, table_new_ref, accum_new_ref):
    table_next, accum_next = adagrad(table_ref[...], accum_ref[...], own_ref[...] + other_ref[...])
    table_new_ref[...] = table_next
    accum_new_ref[...] = accum_next


def swap(x, axis):
    return lax.all_to_all(x, axis, split_axis=0, concat_axis=0, tiled=True)


def from_rep(piece, distance):
    return lax.ppermute(piece, "rep", [(i, i ^ distance) for i in range(4)])


def local(
    hot_ids,
    cold_owner,
    cold_offset,
    labels,
    top_weight,
    out_weight,
    cold_table,
    cold_accum,
    hot_cache,
    hot_accum,
    pending,
    refresh_blocks,
    block_clock,
):
    samples, feats = hot_ids.shape
    lookups = cold_offset.shape[0]
    own_rows, width = cold_table.shape
    hot_count = hot_cache.shape[0]
    inputs_width, hidden_width = top_weight.shape
    owners = lax.axis_size(DP)
    slots = owners * SLOTS
    groups = lookups // BLOCK
    place = jnp.stack([lax.axis_index("dp_2"), lax.axis_index("rep")]).astype(jnp.int32)
    control = jnp.concatenate([place, refresh_blocks, block_clock])

    request, target = call(
        requests_kernel,
        [((owners, BLOCK), F32), ((lookups, BLOCK), F32)],
        (cold_owner.reshape(groups, BLOCK), cold_offset.reshape(groups, BLOCK)),
        loads=(0, 1),
        kept=(1,),
    )
    asked = swap(request.reshape(owners, 1, BLOCK), DP).reshape(owners, BLOCK)
    target_rows, hot_in, hot_id_rows, narrow, label, out_held = call(
        masks_kernel,
        [
            ((8, lookups), F32),
            ((samples, feats * width), BF16),
            ((8, samples * feats), F32),
            ((own_rows, width), BF16),
            ((samples, BLOCK), F32),
            ((1, hidden_width), F32),
        ],
        (target, hot_ids.T, hot_cache, cold_table, labels.reshape(2, BLOCK), out_weight.reshape(1, hidden_width)),
        loads=(1, 2, 3, 4, 5),
        held=(0,),
        kept=(0, 1, 2, 3, 4, 5),
    )
    (found,) = call(rows_kernel, [((slots, width), BF16)], (asked, narrow), held=(1,), scratch=[((slots, width), F32)])
    returned = swap(found.reshape(owners, SLOTS, width), DP).reshape(slots, width)
    (owned,) = call(owned_kernel, [((own_rows, slots), BF16)], (asked,))
    outgoing, inputs, dhidden, hot_dx, head = call(
        layer_kernel,
        [
            ((slots, width), BF16),
            ((samples, inputs_width), BF16),
            ((samples, hidden_width), BF16),
            ((samples * feats, width), BF16),
            ((8, BLOCK), F32),
        ],
        (returned, target, target_rows, hot_in, top_weight, out_held, label),
        held=(1, 2, 3, 5, 6),
        kept=(1, 2, 3, 4),
    )
    half = inputs_width // 2
    broad = hidden_width + BLOCK
    packed = broad + 2 * BLOCK
    near = lax.axis_size("dp_1")
    far = lax.axis_size("dp_0")
    plane_size = lax.axis_size(PLANE)
    send, picked, pending_new = call(
        send_kernel,
        [((half, packed), I16), ((plane_size * far, BLOCK), F32), ((hot_count, width), F32)],
        (control, inputs, dhidden, hot_id_rows, hot_dx, head, pending),
        smem=1,
        held=(1, 2, 3, 4, 5),
        kept=(1,),
        scratch=[((REFRESHED * BLOCK, BLOCK), F32)],
        flops=10**9,
    )
    send, outgoing = lax.optimization_barrier((send, outgoing))
    received = lax.ppermute(send, "dp_2", [(0, 1), (1, 0)])
    incoming = swap(outgoing.reshape(owners, SLOTS, width), DP).reshape(slots, width)
    pieces = call(
        pair_kernel,
        [((half // 4, broad), F32)] + [((half // 4, packed), I16)] * 3,
        (control, inputs, dhidden, picked, received),
        smem=1,
        held=(1, 2, 3),
    )
    two, one, three = (from_rep(pieces[d], d) for d in (2, 1, 3))
    (paired,) = call(four_kernel, [((half // 4, packed), I16)], (pieces[0], one, two, three))
    paired, incoming = lax.optimization_barrier((paired, incoming))
    plane = swap(paired.reshape(near, far, packed), "dp_1")
    tall = hidden_width // BLOCK
    (columns,) = call(plane_kernel, [((far * SENT, BLOCK), jnp.int32)], (plane,))
    columns = swap(columns.reshape(far, 1, SENT * BLOCK), "dp_0").reshape(far * SENT, BLOCK)
    top, copies = call(column_kernel, [((tall, BLOCK), F32), ((plane_size * HELD, BLOCK), F32)], (columns,))
    sums = swap(copies.reshape(plane_size, 1, HELD * BLOCK), PLANE).reshape(plane_size * HELD, BLOCK)

    (grad,) = call(cold_kernel, [((own_rows, width), F32)], (owned, incoming))
    (grad,) = call(two_kernel, [((own_rows, width), F32)], (grad, from_rep(grad, 1)))
    cold_table_new, cold_accum_new = call(
        update_kernel, [((own_rows, width), F32)] * 2, (grad, from_rep(grad, 3), cold_table, cold_accum)
    )
    hot_cache_new, hot_accum_new, out_grad = call(
        hot_kernel,
        [((hot_count, width), F32)] * 2 + [((8, BLOCK), F32)],
        (control, sums, hot_cache, hot_accum),
        smem=1,
        scratch=[((REFRESHED * BLOCK, BLOCK), F32)],
    )
    return (
        cold_table_new,
        cold_accum_new,
        hot_cache_new,
        hot_accum_new,
        pending_new,
        top.reshape(1, hidden_width),
        out_grad.reshape(hidden_width),
    )


def solution(mesh):
    split = Mesh(mesh.devices.reshape(16, 4, 2, mesh.shape["rep"]), ("dp_0", "dp_1", "dp_2", "rep"))
    in_specs = (
        P(DP_REP, None),
        P(DP_REP, None),
        P(DP_REP),
        P(DP_REP),
        P(),
        P(),
        P(DP, None),
        P(DP, None),
        P(),
        P(),
        P(DP_REP, None),
        P(),
        P(),
    )
    out_specs = (P(DP, None), P(DP, None), P(), P(), P(DP_REP, None), P(DP_REP, None), P())
    return jax.shard_map(local, mesh=split, in_specs=in_specs, out_specs=out_specs, check_vma=False)
```

```python
import jax
import jax.numpy as jnp
from jax import lax
from jax.experimental import pallas as pl
from jax.experimental.pallas import tpu as pltpu
from jax.sharding import Mesh
from jax.sharding import PartitionSpec as P

BLOCK = 128
SLOTS = 8
REFRESHED = 3
DP = ("dp_0", "dp_1", "dp_2")
DP_REP = ("dp_0", "dp_1", "dp_2", "rep")
PLANE = ("dp_2", "rep", "dp_1")

step_size = 0.5
epsilon = 1e-08

F32 = jnp.float32
BF16 = jnp.bfloat16
I16 = jnp.int16
LN2 = 0.6931471805599453
FINE = 65534.0
SENT = 18
HELD = 13
EXACT = lax.Precision.HIGHEST
VMEM = pl.BlockSpec(memory_space=pltpu.VMEM)
HBM = pl.BlockSpec(memory_space=pltpu.HBM)
SMEM = pl.BlockSpec(memory_space=pltpu.SMEM)


class Loaded:
    def __init__(self, source, held, sem):
        self.copy = pltpu.make_async_copy(source, held, sem)
        self.held = held
        self.copy.start()

    def wait(self):
        self.copy.wait()
        return self.held


def call(kernel, outs, args, smem=0, scratch=(), loads=(), held=(), kept=(), flops=10**9):
    own = len(scratch)
    ins = len(args)

    def body(*refs):
        given = list(refs[:ins])
        rest = refs[ins + len(outs) :]
        for j, i in enumerate(loads):
            given[i] = Loaded(given[i], rest[own + j], rest[own + len(loads) + j])
        kernel(*given, *refs[ins : ins + len(outs)], *rest[:own])

    specs = [SMEM] * smem + [VMEM] * (ins - smem)
    args = list(args)
    for i in loads:
        specs[i] = HBM
        args[i] = pltpu.with_memory_space_constraint(args[i], pltpu.HBM)
    for i in held:
        args[i] = pltpu.with_memory_space_constraint(args[i], pltpu.VMEM)
    return pl.pallas_call(
        body,
        out_shape=[(pltpu.VMEM if i in kept else jax.ShapeDtypeStruct)(s, d) for i, (s, d) in enumerate(outs)],
        in_specs=specs,
        out_specs=[VMEM] * len(outs),
        scratch_shapes=[pltpu.VMEM(s, d) for s, d in scratch]
        + [pltpu.VMEM(args[i].shape, args[i].dtype) for i in loads]
        + [pltpu.SemaphoreType.DMA for _ in loads],
        compiler_params=pltpu.CompilerParams(vmem_limit_bytes=16 * 2**20),
        cost_estimate=pl.CostEstimate(flops=flops, bytes_accessed=flops // 100, transcendentals=0),
    )(*args)


def iota(shape, dim):
    return lax.broadcasted_iota(jnp.int32, shape, dim)


def iota_f(shape, dim):
    return iota(shape, dim).astype(F32)


def ones_where(mask):
    return jnp.where(mask, 1.0, 0.0).astype(BF16)


def column_of(row, eye):
    return jnp.sum(jnp.where(eye, row, 0.0), axis=1, keepdims=True)


def dot(a, b, precision=None):
    return jnp.dot(a, b, preferred_element_type=F32, precision=precision)


def dot_t(a, b):
    return lax.dot_general(a, b, (((1,), (1,)), ((), ())), preferred_element_type=F32)


def power(exponent):
    return jnp.exp(exponent * LN2)


def exponent_of(top):
    return jnp.ceil(jnp.log(jnp.maximum(top, 1e-30)) * (1.0 / LN2) + 0.01) - 15.0


def pack(values, packed_ref):
    wide = values.shape[1] - BLOCK
    top, hot = values[:, :wide], values[:, wide:]
    top_exponent = exponent_of(jnp.max(jnp.abs(top), axis=1, keepdims=True))
    hot_exponent = exponent_of(jnp.max(jnp.abs(hot), axis=1, keepdims=True))
    lane = iota((values.shape[0], BLOCK), 1)
    hot = hot * power(-hot_exponent)
    coarse = jnp.round(hot)
    at = 0
    for part in (
        jnp.round(top * power(-top_exponent)),
        coarse,
        jnp.round((hot - coarse) * FINE),
        jnp.where(lane < BLOCK // 2, top_exponent, hot_exponent),
    ):
        packed_ref[:, at : at + part.shape[1]] = part.astype(jnp.int32).astype(I16)
        at += part.shape[1]


def unpack(packed):
    values = packed.astype(jnp.int32).astype(F32)
    wide = values.shape[1] - 3 * BLOCK
    coarse, fine, exponents = (values[:, wide + i * BLOCK : wide + (i + 1) * BLOCK] for i in range(3))
    top = values[:, :wide] * power(exponents[:, :1])
    hot = (coarse + fine * (1.0 / FINE)) * power(exponents[:, BLOCK - 1 :])
    return jnp.concatenate([top, hot], axis=1)


def requests_kernel(owner_ref, offset_ref, request_ref, target_ref):
    square = (BLOCK, BLOCK)
    owner = owner_ref.wait()[...].astype(F32)
    offset = offset_ref.wait()[...].astype(F32)
    groups = owner.shape[0]
    lookups = groups * BLOCK
    columns = jnp.transpose(jnp.concatenate([owner, offset], axis=0))
    owner_col = jnp.concatenate([columns[:, s : s + 1] for s in range(groups)], axis=0)
    offset_col = jnp.concatenate([columns[:, groups + s : groups + s + 1] for s in range(groups)], axis=0)
    lane = iota_f((lookups, BLOCK), 1)
    named = owner_col == lane
    before = ones_where(iota(square, 0) > iota(square, 1))
    counts = jnp.where(named, 1.0, 0.0)
    earlier = []
    so_far = jnp.zeros((1, BLOCK), F32)
    for s in range(groups):
        block = counts[s * BLOCK : (s + 1) * BLOCK]
        earlier.append(dot(before, block.astype(BF16)) + so_far)
        so_far = so_far + jnp.sum(block, axis=0, keepdims=True)
    rank = jnp.sum(jnp.where(named, jnp.concatenate(earlier, axis=0), 0.0), axis=1, keepdims=True)
    target_ref[...] = jnp.broadcast_to(owner_col * SLOTS + rank, (lookups, BLOCK))
    high = jnp.where(offset_col >= 256.0, 1.0, 0.0)
    placed = jnp.where(rank == lane, offset_col - 256.0 * high, jnp.where(rank == lane - SLOTS, high, 0.0))
    sublane = iota_f(square, 0)
    named_t = jnp.concatenate([ones_where(sublane == owner[s : s + 1, :]) for s in range(groups)], axis=1)
    request_ref[...] = dot(named_t, placed.astype(BF16))


def rows_kernel(asked_ref, table_ref, rows_ref, wide_ref):
    asked = asked_ref[:, :SLOTS] + 256.0 * asked_ref[:, SLOTS : 2 * SLOTS]
    table = table_ref[...]
    sources = asked.shape[0]
    line = iota_f((sources, table.shape[0]), 1)
    for slot in range(SLOTS):
        chosen = ones_where(asked[:, slot : slot + 1] == line)
        wide_ref[pl.ds(slot, sources, stride=SLOTS), :] = dot(chosen, table)
    rows_ref[...] = wide_ref[...].astype(BF16)


def owned_kernel(asked_ref, owned_ref):
    slots = owned_ref.shape[1]
    source, line = iota((BLOCK, slots), 0), iota((BLOCK, slots), 1)
    slot = line % SLOTS
    worth = jnp.where(source == slot, 1.0, jnp.where(source == slot + SLOTS, 256.0, 0.0))
    spread = dot(asked_ref[...], worth, EXACT)
    wanted = jnp.sum(jnp.where(source == line // SLOTS, spread, 0.0), axis=0, keepdims=True)
    owned_ref[...] = ones_where(iota_f(owned_ref.shape, 0) == wanted)


def masks_kernel(
    target_ref, hot_ref, cache_ref, table_ref, labels_ref, out_weight_ref,
    rows_ref, hot_in_ref, hot_rows_ref, narrow_ref, label_ref, out_held_ref,
):
    square = (BLOCK, BLOCK)
    eye = iota(square, 0) == iota(square, 1)
    hot = hot_ref.wait()[...].astype(F32)
    feats, samples = hot.shape
    for k in range(feats):
        mine = target_ref[pl.ds(k, samples, stride=feats), :]
        for h in range(samples // BLOCK):
            at = k * samples + h * BLOCK
            row = jnp.sum(jnp.where(eye, mine[h * BLOCK : (h + 1) * BLOCK, :], 0.0), axis=0, keepdims=True)
            rows_ref[:, at : at + BLOCK] = jnp.broadcast_to(row, (8, BLOCK))
    cache = cache_ref.wait()[...].astype(BF16)
    hot_count = cache.shape[0]
    hot_lane = iota_f((BLOCK, hot_count), 1)
    for k in range(feats):
        for h in range(samples // BLOCK):
            at = k * samples + h * BLOCK
            row = hot[k : k + 1, h * BLOCK : (h + 1) * BLOCK]
            hot_rows_ref[:, at : at + BLOCK] = jnp.broadcast_to(row, (8, BLOCK))
            chosen = ones_where(column_of(row, eye) == hot_lane)
            hot_in_ref[h * BLOCK : (h + 1) * BLOCK, k * BLOCK : (k + 1) * BLOCK] = dot(chosen, cache).astype(BF16)
    narrow_ref[...] = table_ref.wait()[...].astype(BF16)
    labels = labels_ref.wait()[...].astype(F32)
    for h in range(labels.shape[0]):
        column = column_of(labels[h : h + 1, :], eye)
        label_ref[h * BLOCK : (h + 1) * BLOCK, :] = jnp.broadcast_to(column, (BLOCK, BLOCK))
    out_held_ref[...] = out_weight_ref.wait()[...]


def layer_kernel(
    returned_ref, target_ref, rows_ref, hot_in_ref, weight_ref, out_weight_ref, label_ref,
    outgoing_ref, inputs_ref, dhidden_ref, hot_dx_ref, head_ref,
):
    width = BLOCK
    samples = target_ref.shape[0] // 2
    lane = iota_f((samples, BLOCK), 1)
    slots = returned_ref.shape[0]
    mine = [target_ref[pl.ds(k, samples, stride=2), :] for k in range(2)]
    take = [
        jnp.concatenate([ones_where(t == lane + float(b)) for b in range(0, slots, BLOCK)], axis=1) for t in mine
    ]
    cold = dot(jnp.concatenate(take, axis=0), returned_ref[...]).astype(BF16)
    inputs = jnp.concatenate([hot_in_ref[...], cold[:samples], cold[samples:]], axis=1)
    inputs_ref[...] = inputs
    weight = weight_ref[...]
    out_weight = out_weight_ref[...]
    preact = dot(inputs, weight)
    gates = jax.nn.sigmoid(preact)
    hidden = (preact * gates).astype(BF16).astype(F32)
    logits = jnp.sum(hidden * out_weight, axis=1, keepdims=True)
    label = label_ref[:, :1]
    errors = jax.nn.sigmoid(logits) - label
    slope = gates * (1.0 + preact * (1.0 - gates))
    dhidden = (errors * out_weight * slope).astype(BF16)
    dhidden_ref[...] = dhidden
    dinputs = dot_t(dhidden, weight).astype(BF16)
    cold_dx = jnp.concatenate([dinputs[:, 2 * width : 3 * width], dinputs[:, 3 * width :]], axis=0)
    put = ones_where(iota_f((outgoing_ref.shape[0], rows_ref.shape[1]), 0) == rows_ref[:1, :])
    outgoing_ref[...] = dot(put, cold_dx).astype(BF16)
    hot_dx_ref[:samples, :] = dinputs[:, :width]
    hot_dx_ref[samples:, :] = dinputs[:, width : 2 * width]
    head = jnp.sum(errors * hidden, axis=0, keepdims=True)
    for b in range(head_ref.shape[0]):
        head_ref[b : b + 1, :] = head[:, b * BLOCK : (b + 1) * BLOCK]


def half_of_top(core, rep, inputs, dhidden):
    shape = (inputs.shape[1] // 2, inputs.shape[1])
    line = iota(shape, 0)
    row = (line & 15) * 32 + ((line >> 4) & 3) * 8 + core * 4 + ((line >> 6) ^ rep)
    ordered = dot_t(ones_where(row == iota(shape, 1)), inputs).astype(BF16)
    return dot(ordered, dhidden)


def hot_rows(picked_ref, core, rep, piece):
    count = picked_ref.shape[0] // 8
    return picked_ref[pl.ds(pl.multiple_of((core * 4 + (rep ^ piece)) * count, count), count), :]


def send_kernel(
    control_ref, inputs_ref, dhidden_ref, hot_rows_ref, hot_dx_ref, head_ref, pending_ref,
    send_ref, picked_ref, pending_new_ref, flat_ref,
):
    put = ones_where(iota_f((pending_ref.shape[0], hot_rows_ref.shape[1]), 0) == hot_rows_ref[:1, :])
    pending_new_ref[...] = dot(put, hot_dx_ref[...]) + pending_ref[...]
    count = REFRESHED
    blocks = [pl.ds(pl.multiple_of(control_ref[2 + i] * BLOCK, BLOCK), BLOCK) for i in range(count)]
    for i, at in enumerate(blocks):
        flat_ref[i * BLOCK : (i + 1) * BLOCK, :] = pending_new_ref[at, :]
    rows = HELD - 1
    count = picked_ref.shape[0] // 16
    part = iota((1, BLOCK), 1) // (8 * BLOCK // count)
    for i in range(count):
        at = i * 16
        q, p = divmod(i, count // 8)
        picked_ref[at : at + rows, :] = flat_ref[i * rows : (i + 1) * rows, :]
        picked_ref[at + rows : at + HELD, :] = jnp.where(part == p, head_ref[q : q + 1, :], 0.0)
        picked_ref[at + HELD : at + 16, :] = jnp.zeros((16 - HELD, BLOCK), F32)
    for at in blocks:
        pending_new_ref[at, :] = jnp.zeros((BLOCK, BLOCK), F32)
    core, rep = 1 - control_ref[0], control_ref[1]
    top = half_of_top(core, rep, inputs_ref[...], dhidden_ref[...])
    hot = jnp.concatenate([hot_rows(picked_ref, core, rep, d) for d in range(4)], axis=0)
    pack(jnp.concatenate([top, hot], axis=1), send_ref)


def pair_kernel(control_ref, inputs_ref, dhidden_ref, picked_ref, received_ref, own_ref, *pieces):
    core, rep = control_ref[0], control_ref[1]
    top = half_of_top(core, rep, inputs_ref[...], dhidden_ref[...])
    tall = own_ref.shape[0]
    for d, piece in enumerate((own_ref, *pieces)):
        rows = slice(d * tall, (d + 1) * tall)
        mine = jnp.concatenate([top[rows], hot_rows(picked_ref, core, rep, d)], axis=1)
        both = mine + unpack(received_ref[rows, :])
        if d:
            pack(both, piece)
        else:
            piece[...] = both


def four_kernel(own_ref, two_ref, one_ref, three_ref, sum_ref):
    total = (own_ref[...] + unpack(one_ref[...])) + (unpack(two_ref[...]) + unpack(three_ref[...]))
    pack(total, sum_ref)


def plane_kernel(parts_ref, out_ref):
    total = unpack(parts_ref[0])
    for i in range(1, parts_ref.shape[0]):
        total = total + unpack(parts_ref[i])
    count = total.shape[0]
    wide = total.shape[1] - BLOCK
    top, hot = total[:, :wide], total[:, wide:]
    top_exponent = exponent_of(jnp.max(jnp.abs(top), axis=1, keepdims=True))
    top = jnp.round(top * power(-top_exponent)).astype(jnp.int32)
    pairs = (top[:, : wide // 2] & 65535) | (top[:, wide // 2 :] << 16)
    most = jnp.max(jnp.max(jnp.abs(hot), axis=1, keepdims=True), axis=0, keepdims=True)
    hot_exponent = exponent_of(jnp.maximum(most, 1e-20)) - 15.0
    hot = jnp.round(hot * power(-hot_exponent)).astype(jnp.int32)
    lane = iota((count, BLOCK), 1)
    rows = [pairs[:, b : b + BLOCK] for b in range(0, wide // 2, BLOCK)]
    rows += [jnp.broadcast_to(hot[r : r + 1], (count, BLOCK)) for r in range(HELD)]
    rows += [jnp.where(lane < BLOCK // 2, top_exponent, hot_exponent).astype(jnp.int32)]
    for r, row in enumerate(rows):
        out_ref[pl.ds(r, count, stride=SENT), :] = row


def column_kernel(parts_ref, top_ref, copies_ref):
    tall = top_ref.shape[0] // 2
    low, high = jnp.zeros((tall, BLOCK), F32), jnp.zeros((tall, BLOCK), F32)
    hot = jnp.zeros((HELD, BLOCK), F32)
    for i in range(parts_ref.shape[0] // SENT):
        at = i * SENT
        scale = power(parts_ref[at + SENT - 1 : at + SENT, :].astype(F32))
        pairs = parts_ref[at : at + tall, :]
        low = low + ((pairs << 16) >> 16).astype(F32) * scale[:, :1]
        high = high + (pairs >> 16).astype(F32) * scale[:, :1]
        hot = hot + parts_ref[at + tall : at + tall + HELD, :].astype(F32) * scale[:, BLOCK - 1 :]
    top_ref[:tall, :] = low
    top_ref[tall:, :] = high
    for i in range(copies_ref.shape[0] // HELD):
        copies_ref[i * HELD : (i + 1) * HELD, :] = hot


def adagrad(table_rows, accum_rows, gradient):
    accum_next = accum_rows + gradient * gradient
    return (table_rows - step_size * gradient / (jnp.sqrt(accum_next) + epsilon), accum_next)


def hot_kernel(control_ref, sums_ref, cache_ref, accum_ref, cache_new_ref, accum_new_ref, out_grad_ref, flat_ref):
    cache_new_ref[...] = cache_ref[...]
    accum_new_ref[...] = accum_ref[...]
    rows = HELD - 1
    pieces = sums_ref.shape[0] // HELD
    for i in range(pieces):
        flat_ref[i * rows : (i + 1) * rows, :] = sums_ref[i * HELD : i * HELD + rows, :]
    for q in range(8):
        parts = [sums_ref[i * HELD + rows : (i + 1) * HELD, :] for i in range(q * pieces // 8, (q + 1) * pieces // 8)]
        out_grad_ref[q : q + 1, :] = sum(parts[1:], parts[0])
    count = REFRESHED
    for i in range(count):
        block = control_ref[2 + i]
        at = pl.ds(pl.multiple_of(block * BLOCK, BLOCK), BLOCK)
        flush = flat_ref[i * BLOCK : (i + 1) * BLOCK, :] / (1.0 + control_ref[2 + count + block].astype(F32))
        cache_next, accum_next = adagrad(cache_ref[at, :], accum_ref[at, :], flush)
        cache_new_ref[at, :] = cache_next
        accum_new_ref[at, :] = accum_next


def cold_kernel(owned_ref, incoming_ref, grad_ref):
    grad_ref[...] = dot(owned_ref[...], incoming_ref[...])


def two_kernel(own_ref, other_ref, sum_ref):
    sum_ref[...] = own_ref[...] + other_ref[...]


def update_kernel(own_ref, other_ref, table_ref, accum_ref, table_new_ref, accum_new_ref):
    table_next, accum_next = adagrad(table_ref[...], accum_ref[...], own_ref[...] + other_ref[...])
    table_new_ref[...] = table_next
    accum_new_ref[...] = accum_next


def swap(x, axis):
    return lax.all_to_all(x, axis, split_axis=0, concat_axis=0, tiled=True)


def from_rep(piece, distance):
    return lax.ppermute(piece, "rep", [(i, i ^ distance) for i in range(4)])


def local(
    hot_ids,
    cold_owner,
    cold_offset,
    labels,
    top_weight,
    out_weight,
    cold_table,
    cold_accum,
    hot_cache,
    hot_accum,
    pending,
    refresh_blocks,
    block_clock,
):
    samples, feats = hot_ids.shape
    lookups = cold_offset.shape[0]
    own_rows, width = cold_table.shape
    hot_count = hot_cache.shape[0]
    inputs_width, hidden_width = top_weight.shape
    owners = lax.axis_size(DP)
    slots = owners * SLOTS
    groups = lookups // BLOCK
    place = jnp.stack([lax.axis_index("dp_2"), lax.axis_index("rep")]).astype(jnp.int32)
    control = jnp.concatenate([place, refresh_blocks, block_clock])

    request, target = call(
        requests_kernel,
        [((owners, BLOCK), F32), ((lookups, BLOCK), F32)],
        (cold_owner.reshape(groups, BLOCK), cold_offset.reshape(groups, BLOCK)),
        loads=(0, 1),
        kept=(1,),
    )
    asked = swap(request.reshape(owners, 1, BLOCK), DP).reshape(owners, BLOCK)
    target_rows, hot_in, hot_id_rows, narrow, label, out_held = call(
        masks_kernel,
        [
            ((8, lookups), F32),
            ((samples, feats * width), BF16),
            ((8, samples * feats), F32),
            ((own_rows, width), BF16),
            ((samples, BLOCK), F32),
            ((1, hidden_width), F32),
        ],
        (target, hot_ids.T, hot_cache, cold_table, labels.reshape(2, BLOCK), out_weight.reshape(1, hidden_width)),
        loads=(1, 2, 3, 4, 5),
        held=(0,),
        kept=(0, 1, 2, 3, 4, 5),
    )
    (found,) = call(rows_kernel, [((slots, width), BF16)], (asked, narrow), held=(1,), scratch=[((slots, width), F32)])
    returned = swap(found.reshape(owners, SLOTS, width), DP).reshape(slots, width)
    (owned,) = call(owned_kernel, [((own_rows, slots), BF16)], (asked,))
    outgoing, inputs, dhidden, hot_dx, head = call(
        layer_kernel,
        [
            ((slots, width), BF16),
            ((samples, inputs_width), BF16),
            ((samples, hidden_width), BF16),
            ((samples * feats, width), BF16),
            ((8, BLOCK), F32),
        ],
        (returned, target, target_rows, hot_in, top_weight, out_held, label),
        held=(1, 2, 3, 5, 6),
        kept=(1, 2, 3, 4),
    )
    half = inputs_width // 2
    broad = hidden_width + BLOCK
    packed = broad + 2 * BLOCK
    near = lax.axis_size("dp_1")
    far = lax.axis_size("dp_0")
    plane_size = lax.axis_size(PLANE)
    send, picked, pending_new = call(
        send_kernel,
        [((half, packed), I16), ((plane_size * far, BLOCK), F32), ((hot_count, width), F32)],
        (control, inputs, dhidden, hot_id_rows, hot_dx, head, pending),
        smem=1,
        held=(1, 2, 3, 4, 5),
        kept=(1,),
        scratch=[((REFRESHED * BLOCK, BLOCK), F32)],
        flops=10**9,
    )
    send, outgoing = lax.optimization_barrier((send, outgoing))
    received = lax.ppermute(send, "dp_2", [(0, 1), (1, 0)])
    incoming = swap(outgoing.reshape(owners, SLOTS, width), DP).reshape(slots, width)
    pieces = call(
        pair_kernel,
        [((half // 4, broad), F32)] + [((half // 4, packed), I16)] * 3,
        (control, inputs, dhidden, picked, received),
        smem=1,
        held=(1, 2, 3),
    )
    two, one, three = (from_rep(pieces[d], d) for d in (2, 1, 3))
    (paired,) = call(four_kernel, [((half // 4, packed), I16)], (pieces[0], two, one, three))
    paired, incoming = lax.optimization_barrier((paired, incoming))
    plane = swap(paired.reshape(near, far, packed), "dp_1")
    tall = hidden_width // BLOCK
    (columns,) = call(plane_kernel, [((far * SENT, BLOCK), jnp.int32)], (plane,))
    columns = swap(columns.reshape(far, 1, SENT * BLOCK), "dp_0").reshape(far * SENT, BLOCK)
    top, copies = call(column_kernel, [((tall, BLOCK), F32), ((plane_size * HELD, BLOCK), F32)], (columns,))
    sums = swap(copies.reshape(plane_size, 1, HELD * BLOCK), PLANE).reshape(plane_size * HELD, BLOCK)

    (grad,) = call(cold_kernel, [((own_rows, width), F32)], (owned, incoming))
    (grad,) = call(two_kernel, [((own_rows, width), F32)], (grad, from_rep(grad, 1)))
    cold_table_new, cold_accum_new = call(
        update_kernel, [((own_rows, width), F32)] * 2, (grad, from_rep(grad, 3), cold_table, cold_accum)
    )
    hot_cache_new, hot_accum_new, out_grad = call(
        hot_kernel,
        [((hot_count, width), F32)] * 2 + [((8, BLOCK), F32)],
        (control, sums, hot_cache, hot_accum),
        smem=1,
        scratch=[((REFRESHED * BLOCK, BLOCK), F32)],
    )
    return (
        cold_table_new,
        cold_accum_new,
        hot_cache_new,
        hot_accum_new,
        pending_new,
        top.reshape(1, hidden_width),
        out_grad.reshape(hidden_width),
    )


def solution(mesh):
    split = Mesh(mesh.devices.reshape(16, 4, 2, mesh.shape["rep"]), ("dp_0", "dp_1", "dp_2", "rep"))
    in_specs = (
        P(DP_REP, None),
        P(DP_REP, None),
        P(DP_REP),
        P(DP_REP),
        P(),
        P(),
        P(DP, None),
        P(DP, None),
        P(),
        P(),
        P(DP_REP, None),
        P(),
        P(),
    )
    out_specs = (P(DP, None), P(DP, None), P(), P(), P(DP_REP, None), P(DP_REP, None), P())
    return jax.shard_map(local, mesh=split, in_specs=in_specs, out_specs=out_specs, check_vma=False)
```

```python
import jax
import jax.numpy as jnp
from jax import lax
from jax.experimental import pallas as pl
from jax.experimental.pallas import tpu as pltpu
from jax.sharding import Mesh
from jax.sharding import PartitionSpec as P

BLOCK = 128
SLOTS = 8
REFRESHED = 3
DP = ("dp_0", "dp_1", "dp_2")
DP_REP = ("dp_0", "dp_1", "dp_2", "rep")
PLANE = ("dp_2", "rep", "dp_1")

step_size = 0.5
epsilon = 1e-08

F32 = jnp.float32
BF16 = jnp.bfloat16
I16 = jnp.int16
LN2 = 0.6931471805599453
FINE = 65534.0
SENT = 18
HELD = 13
EXACT = lax.Precision.HIGHEST
VMEM = pl.BlockSpec(memory_space=pltpu.VMEM)
HBM = pl.BlockSpec(memory_space=pltpu.HBM)
SMEM = pl.BlockSpec(memory_space=pltpu.SMEM)


class Loaded:
    def __init__(self, source, held, sem):
        self.copy = pltpu.make_async_copy(source, held, sem)
        self.held = held
        self.copy.start()

    def wait(self):
        self.copy.wait()
        return self.held


def call(kernel, outs, args, smem=0, scratch=(), loads=(), held=(), kept=(), flops=10**9):
    own = len(scratch)
    ins = len(args)

    def body(*refs):
        given = list(refs[:ins])
        rest = refs[ins + len(outs) :]
        for j, i in enumerate(loads):
            given[i] = Loaded(given[i], rest[own + j], rest[own + len(loads) + j])
        kernel(*given, *refs[ins : ins + len(outs)], *rest[:own])

    specs = [SMEM] * smem + [VMEM] * (ins - smem)
    args = list(args)
    for i in loads:
        specs[i] = HBM
        args[i] = pltpu.with_memory_space_constraint(args[i], pltpu.HBM)
    for i in held:
        args[i] = pltpu.with_memory_space_constraint(args[i], pltpu.VMEM)
    return pl.pallas_call(
        body,
        out_shape=[(pltpu.VMEM if i in kept else jax.ShapeDtypeStruct)(s, d) for i, (s, d) in enumerate(outs)],
        in_specs=specs,
        out_specs=[VMEM] * len(outs),
        scratch_shapes=[pltpu.VMEM(s, d) for s, d in scratch]
        + [pltpu.VMEM(args[i].shape, args[i].dtype) for i in loads]
        + [pltpu.SemaphoreType.DMA for _ in loads],
        compiler_params=pltpu.CompilerParams(vmem_limit_bytes=16 * 2**20),
        cost_estimate=pl.CostEstimate(flops=flops, bytes_accessed=flops // 100, transcendentals=0),
    )(*args)


def iota(shape, dim):
    return lax.broadcasted_iota(jnp.int32, shape, dim)


def iota_f(shape, dim):
    return iota(shape, dim).astype(F32)


def ones_where(mask):
    return jnp.where(mask, 1.0, 0.0).astype(BF16)


def column_of(row, eye):
    return jnp.sum(jnp.where(eye, row, 0.0), axis=1, keepdims=True)


def dot(a, b, precision=None):
    return jnp.dot(a, b, preferred_element_type=F32, precision=precision)


def dot_t(a, b):
    return lax.dot_general(a, b, (((1,), (1,)), ((), ())), preferred_element_type=F32)


def power(exponent):
    return jnp.exp(exponent * LN2)


def exponent_of(top):
    return jnp.ceil(jnp.log(jnp.maximum(top, 1e-30)) * (1.0 / LN2) + 0.01) - 15.0


def pack(values, packed_ref):
    wide = values.shape[1] - BLOCK
    top, hot = values[:, :wide], values[:, wide:]
    top_exponent = exponent_of(jnp.max(jnp.abs(top), axis=1, keepdims=True))
    hot_exponent = exponent_of(jnp.max(jnp.abs(hot), axis=1, keepdims=True))
    lane = iota((values.shape[0], BLOCK), 1)
    hot = hot * power(-hot_exponent)
    coarse = jnp.round(hot)
    at = 0
    for part in (
        jnp.round(top * power(-top_exponent)),
        coarse,
        jnp.round((hot - coarse) * FINE),
        jnp.where(lane < BLOCK // 2, top_exponent, hot_exponent),
    ):
        packed_ref[:, at : at + part.shape[1]] = part.astype(jnp.int32).astype(I16)
        at += part.shape[1]


def unpack(packed):
    values = packed.astype(jnp.int32).astype(F32)
    wide = values.shape[1] - 3 * BLOCK
    coarse, fine, exponents = (values[:, wide + i * BLOCK : wide + (i + 1) * BLOCK] for i in range(3))
    top = values[:, :wide] * power(exponents[:, :1])
    hot = (coarse + fine * (1.0 / FINE)) * power(exponents[:, BLOCK - 1 :])
    return jnp.concatenate([top, hot], axis=1)


def requests_kernel(owner_ref, offset_ref, request_ref, target_ref):
    square = (BLOCK, BLOCK)
    owner = owner_ref.wait()[...].astype(F32)
    offset = offset_ref.wait()[...].astype(F32)
    groups = owner.shape[0]
    lookups = groups * BLOCK
    columns = jnp.transpose(jnp.concatenate([owner, offset], axis=0))
    owner_col = jnp.concatenate([columns[:, s : s + 1] for s in range(groups)], axis=0)
    offset_col = jnp.concatenate([columns[:, groups + s : groups + s + 1] for s in range(groups)], axis=0)
    lane = iota_f((lookups, BLOCK), 1)
    named = owner_col == lane
    before = ones_where(iota(square, 0) > iota(square, 1))
    counts = jnp.where(named, 1.0, 0.0)
    earlier = []
    so_far = jnp.zeros((1, BLOCK), F32)
    for s in range(groups):
        block = counts[s * BLOCK : (s + 1) * BLOCK]
        earlier.append(dot(before, block.astype(BF16)) + so_far)
        so_far = so_far + jnp.sum(block, axis=0, keepdims=True)
    rank = jnp.sum(jnp.where(named, jnp.concatenate(earlier, axis=0), 0.0), axis=1, keepdims=True)
    target_ref[...] = jnp.broadcast_to(owner_col * SLOTS + rank, (lookups, BLOCK))
    high = jnp.where(offset_col >= 256.0, 1.0, 0.0)
    placed = jnp.where(rank == lane, offset_col - 256.0 * high, jnp.where(rank == lane - SLOTS, high, 0.0))
    sublane = iota_f(square, 0)
    named_t = jnp.concatenate([ones_where(sublane == owner[s : s + 1, :]) for s in range(groups)], axis=1)
    request_ref[...] = dot(named_t, placed.astype(BF16))


def rows_kernel(asked_ref, table_ref, rows_ref, wide_ref):
    asked = asked_ref[:, :SLOTS] + 256.0 * asked_ref[:, SLOTS : 2 * SLOTS]
    table = table_ref[...]
    sources = asked.shape[0]
    line = iota_f((sources, table.shape[0]), 1)
    for slot in range(SLOTS):
        chosen = ones_where(asked[:, slot : slot + 1] == line)
        wide_ref[pl.ds(slot, sources, stride=SLOTS), :] = dot(chosen, table)
    rows_ref[...] = wide_ref[...].astype(BF16)


def owned_kernel(asked_ref, owned_ref):
    slots = owned_ref.shape[1]
    source, line = iota((BLOCK, slots), 0), iota((BLOCK, slots), 1)
    slot = line % SLOTS
    worth = jnp.where(source == slot, 1.0, jnp.where(source == slot + SLOTS, 256.0, 0.0))
    spread = dot(asked_ref[...], worth, EXACT)
    wanted = jnp.sum(jnp.where(source == line // SLOTS, spread, 0.0), axis=0, keepdims=True)
    owned_ref[...] = ones_where(iota_f(owned_ref.shape, 0) == wanted)


def masks_kernel(
    target_ref, hot_ref, cache_ref, table_ref, labels_ref, out_weight_ref,
    rows_ref, hot_in_ref, hot_rows_ref, narrow_ref, label_ref, out_held_ref,
):
    square = (BLOCK, BLOCK)
    eye = iota(square, 0) == iota(square, 1)
    hot = hot_ref.wait()[...].astype(F32)
    feats, samples = hot.shape
    for k in range(feats):
        mine = target_ref[pl.ds(k, samples, stride=feats), :]
        for h in range(samples // BLOCK):
            at = k * samples + h * BLOCK
            row = jnp.sum(jnp.where(eye, mine[h * BLOCK : (h + 1) * BLOCK, :], 0.0), axis=0, keepdims=True)
            rows_ref[:, at : at + BLOCK] = jnp.broadcast_to(row, (8, BLOCK))
    cache = cache_ref.wait()[...].astype(BF16)
    hot_count = cache.shape[0]
    hot_lane = iota_f((BLOCK, hot_count), 1)
    for k in range(feats):
        for h in range(samples // BLOCK):
            at = k * samples + h * BLOCK
            row = hot[k : k + 1, h * BLOCK : (h + 1) * BLOCK]
            hot_rows_ref[:, at : at + BLOCK] = jnp.broadcast_to(row, (8, BLOCK))
            chosen = ones_where(column_of(row, eye) == hot_lane)
            hot_in_ref[h * BLOCK : (h + 1) * BLOCK, k * BLOCK : (k + 1) * BLOCK] = dot(chosen, cache).astype(BF16)
    narrow_ref[...] = table_ref.wait()[...].astype(BF16)
    labels = labels_ref.wait()[...].astype(F32)
    for h in range(labels.shape[0]):
        column = column_of(labels[h : h + 1, :], eye)
        label_ref[h * BLOCK : (h + 1) * BLOCK, :] = jnp.broadcast_to(column, (BLOCK, BLOCK))
    out_held_ref[...] = out_weight_ref.wait()[...]


def layer_kernel(
    returned_ref, target_ref, rows_ref, hot_in_ref, weight_ref, out_weight_ref, label_ref,
    outgoing_ref, inputs_ref, dhidden_ref, hot_dx_ref, head_ref,
):
    width = BLOCK
    samples = target_ref.shape[0] // 2
    lane = iota_f((samples, BLOCK), 1)
    slots = returned_ref.shape[0]
    mine = [target_ref[pl.ds(k, samples, stride=2), :] for k in range(2)]
    take = [
        jnp.concatenate([ones_where(t == lane + float(b)) for b in range(0, slots, BLOCK)], axis=1) for t in mine
    ]
    cold = dot(jnp.concatenate(take, axis=0), returned_ref[...]).astype(BF16)
    inputs = jnp.concatenate([hot_in_ref[...], cold[:samples], cold[samples:]], axis=1)
    inputs_ref[...] = inputs
    weight = weight_ref[...]
    out_weight = out_weight_ref[...]
    preact = dot(inputs, weight)
    gates = jax.nn.sigmoid(preact)
    hidden = (preact * gates).astype(BF16).astype(F32)
    logits = jnp.sum(hidden * out_weight, axis=1, keepdims=True)
    label = label_ref[:, :1]
    errors = jax.nn.sigmoid(logits) - label
    slope = gates * (1.0 + preact * (1.0 - gates))
    dhidden = (errors * out_weight * slope).astype(BF16)
    dhidden_ref[...] = dhidden
    dinputs = dot_t(dhidden, weight).astype(BF16)
    cold_dx = jnp.concatenate([dinputs[:, 2 * width : 3 * width], dinputs[:, 3 * width :]], axis=0)
    put = ones_where(iota_f((outgoing_ref.shape[0], rows_ref.shape[1]), 0) == rows_ref[:1, :])
    outgoing_ref[...] = dot(put, cold_dx).astype(BF16)
    hot_dx_ref[:samples, :] = dinputs[:, :width]
    hot_dx_ref[samples:, :] = dinputs[:, width : 2 * width]
    head = jnp.sum(errors * hidden, axis=0, keepdims=True)
    for b in range(head_ref.shape[0]):
        head_ref[b : b + 1, :] = head[:, b * BLOCK : (b + 1) * BLOCK]


def half_of_top(core, rep, inputs, dhidden):
    wide = inputs.shape[1]
    shape = (wide // 2, BLOCK)
    line = iota(shape, 0)
    row = (line & 15) * 32 + ((line >> 4) & 3) * 8 + core * 4 + ((line >> 6) ^ rep)
    lane = iota(shape, 1)
    order = jnp.concatenate([ones_where(row == lane + b) for b in range(0, wide, BLOCK)], axis=1)
    ordered = dot_t(order, inputs).astype(BF16)
    return dot(ordered, dhidden)


def hot_rows(picked_ref, core, rep, piece):
    count = picked_ref.shape[0] // 8
    return picked_ref[pl.ds(pl.multiple_of((core * 4 + (rep ^ piece)) * count, count), count), :]


def send_kernel(
    control_ref, inputs_ref, dhidden_ref, hot_rows_ref, hot_dx_ref, head_ref, pending_ref,
    send_ref, picked_ref, pending_new_ref, flat_ref,
):
    put = ones_where(iota_f((pending_ref.shape[0], hot_rows_ref.shape[1]), 0) == hot_rows_ref[:1, :])
    pending_new_ref[...] = dot(put, hot_dx_ref[...]) + pending_ref[...]
    count = REFRESHED
    blocks = [pl.ds(pl.multiple_of(control_ref[2 + i] * BLOCK, BLOCK), BLOCK) for i in range(count)]
    for i, at in enumerate(blocks):
        flat_ref[i * BLOCK : (i + 1) * BLOCK, :] = pending_new_ref[at, :]
    rows = HELD - 1
    count = picked_ref.shape[0] // 16
    part = iota((1, BLOCK), 1) // (8 * BLOCK // count)
    for i in range(count):
        at = i * 16
        q, p = divmod(i, count // 8)
        picked_ref[at : at + rows, :] = flat_ref[i * rows : (i + 1) * rows, :]
        picked_ref[at + rows : at + HELD, :] = jnp.where(part == p, head_ref[q : q + 1, :], 0.0)
        picked_ref[at + HELD : at + 16, :] = jnp.zeros((16 - HELD, BLOCK), F32)
    for at in blocks:
        pending_new_ref[at, :] = jnp.zeros((BLOCK, BLOCK), F32)
    core, rep = 1 - control_ref[0], control_ref[1]
    top = half_of_top(core, rep, inputs_ref[...], dhidden_ref[...])
    hot = jnp.concatenate([hot_rows(picked_ref, core, rep, d) for d in range(4)], axis=0)
    pack(jnp.concatenate([top, hot], axis=1), send_ref)


def pair_kernel(control_ref, inputs_ref, dhidden_ref, picked_ref, received_ref, own_ref, *pieces):
    core, rep = control_ref[0], control_ref[1]
    top = half_of_top(core, rep, inputs_ref[...], dhidden_ref[...])
    tall = own_ref.shape[0]
    for d, piece in enumerate((own_ref, *pieces)):
        rows = slice(d * tall, (d + 1) * tall)
        mine = jnp.concatenate([top[rows], hot_rows(picked_ref, core, rep, d)], axis=1)
        both = mine + unpack(received_ref[rows, :])
        if d:
            pack(both, piece)
        else:
            piece[...] = both


def four_kernel(own_ref, two_ref, one_ref, three_ref, sum_ref):
    total = (own_ref[...] + unpack(one_ref[...])) + (unpack(two_ref[...]) + unpack(three_ref[...]))
    pack(total, sum_ref)


def plane_kernel(parts_ref, out_ref):
    total = unpack(parts_ref[0])
    for i in range(1, parts_ref.shape[0]):
        total = total + unpack(parts_ref[i])
    count = total.shape[0]
    wide = total.shape[1] - BLOCK
    top, hot = total[:, :wide], total[:, wide:]
    top_exponent = exponent_of(jnp.max(jnp.abs(top), axis=1, keepdims=True))
    top = jnp.round(top * power(-top_exponent)).astype(jnp.int32)
    pairs = (top[:, : wide // 2] & 65535) | (top[:, wide // 2 :] << 16)
    most = jnp.max(jnp.max(jnp.abs(hot), axis=1, keepdims=True), axis=0, keepdims=True)
    hot_exponent = exponent_of(jnp.maximum(most, 1e-20)) - 15.0
    hot = jnp.round(hot * power(-hot_exponent)).astype(jnp.int32)
    lane = iota((count, BLOCK), 1)
    rows = [pairs[:, b : b + BLOCK] for b in range(0, wide // 2, BLOCK)]
    rows += [jnp.broadcast_to(hot[r : r + 1], (count, BLOCK)) for r in range(HELD)]
    rows += [jnp.where(lane < BLOCK // 2, top_exponent, hot_exponent).astype(jnp.int32)]
    for r, row in enumerate(rows):
        out_ref[pl.ds(r, count, stride=SENT), :] = row


def column_kernel(parts_ref, top_ref, copies_ref):
    tall = top_ref.shape[0] // 2
    low, high = jnp.zeros((tall, BLOCK), F32), jnp.zeros((tall, BLOCK), F32)
    hot = jnp.zeros((HELD, BLOCK), F32)
    for i in range(parts_ref.shape[0] // SENT):
        at = i * SENT
        scale = power(parts_ref[at + SENT - 1 : at + SENT, :].astype(F32))
        pairs = parts_ref[at : at + tall, :]
        low = low + ((pairs << 16) >> 16).astype(F32) * scale[:, :1]
        high = high + (pairs >> 16).astype(F32) * scale[:, :1]
        hot = hot + parts_ref[at + tall : at + tall + HELD, :].astype(F32) * scale[:, BLOCK - 1 :]
    top_ref[:tall, :] = low
    top_ref[tall:, :] = high
    for i in range(copies_ref.shape[0] // HELD):
        copies_ref[i * HELD : (i + 1) * HELD, :] = hot


def adagrad(table_rows, accum_rows, gradient):
    accum_next = accum_rows + gradient * gradient
    return (table_rows - step_size * gradient / (jnp.sqrt(accum_next) + epsilon), accum_next)


def hot_kernel(control_ref, sums_ref, cache_ref, accum_ref, cache_new_ref, accum_new_ref, out_grad_ref, flat_ref):
    cache_new_ref[...] = cache_ref[...]
    accum_new_ref[...] = accum_ref[...]
    rows = HELD - 1
    pieces = sums_ref.shape[0] // HELD
    for i in range(pieces):
        flat_ref[i * rows : (i + 1) * rows, :] = sums_ref[i * HELD : i * HELD + rows, :]
    for q in range(8):
        parts = [sums_ref[i * HELD + rows : (i + 1) * HELD, :] for i in range(q * pieces // 8, (q + 1) * pieces // 8)]
        out_grad_ref[q : q + 1, :] = sum(parts[1:], parts[0])
    count = REFRESHED
    for i in range(count):
        block = control_ref[2 + i]
        at = pl.ds(pl.multiple_of(block * BLOCK, BLOCK), BLOCK)
        flush = flat_ref[i * BLOCK : (i + 1) * BLOCK, :] / (1.0 + control_ref[2 + count + block].astype(F32))
        cache_next, accum_next = adagrad(cache_ref[at, :], accum_ref[at, :], flush)
        cache_new_ref[at, :] = cache_next
        accum_new_ref[at, :] = accum_next


def cold_kernel(owned_ref, incoming_ref, grad_ref):
    grad_ref[...] = dot(owned_ref[...], incoming_ref[...])


def two_kernel(own_ref, other_ref, sum_ref):
    sum_ref[...] = own_ref[...] + other_ref[...]


def update_kernel(own_ref, other_ref, table_ref, accum_ref, table_new_ref, accum_new_ref):
    table_next, accum_next = adagrad(table_ref[...], accum_ref[...], own_ref[...] + other_ref[...])
    table_new_ref[...] = table_next
    accum_new_ref[...] = accum_next


def swap(x, axis):
    return lax.all_to_all(x, axis, split_axis=0, concat_axis=0, tiled=True)


def from_rep(piece, distance):
    return lax.ppermute(piece, "rep", [(i, i ^ distance) for i in range(4)])


def local(
    hot_ids,
    cold_owner,
    cold_offset,
    labels,
    top_weight,
    out_weight,
    cold_table,
    cold_accum,
    hot_cache,
    hot_accum,
    pending,
    refresh_blocks,
    block_clock,
):
    samples, feats = hot_ids.shape
    lookups = cold_offset.shape[0]
    own_rows, width = cold_table.shape
    hot_count = hot_cache.shape[0]
    inputs_width, hidden_width = top_weight.shape
    owners = lax.axis_size(DP)
    slots = owners * SLOTS
    groups = lookups // BLOCK
    place = jnp.stack([lax.axis_index("dp_2"), lax.axis_index("rep")]).astype(jnp.int32)
    control = jnp.concatenate([place, refresh_blocks, block_clock])

    request, target = call(
        requests_kernel,
        [((owners, BLOCK), F32), ((lookups, BLOCK), F32)],
        (cold_owner.reshape(groups, BLOCK), cold_offset.reshape(groups, BLOCK)),
        loads=(0, 1),
        kept=(1,),
    )
    asked = swap(request.reshape(owners, 1, BLOCK), DP).reshape(owners, BLOCK)
    target_rows, hot_in, hot_id_rows, narrow, label, out_held = call(
        masks_kernel,
        [
            ((8, lookups), F32),
            ((samples, feats * width), BF16),
            ((8, samples * feats), F32),
            ((own_rows, width), BF16),
            ((samples, BLOCK), F32),
            ((1, hidden_width), F32),
        ],
        (target, hot_ids.T, hot_cache, cold_table, labels.reshape(2, BLOCK), out_weight.reshape(1, hidden_width)),
        loads=(1, 2, 3, 4, 5),
        held=(0,),
        kept=(0, 1, 2, 3, 4, 5),
    )
    (found,) = call(rows_kernel, [((slots, width), BF16)], (asked, narrow), held=(1,), scratch=[((slots, width), F32)])
    returned = swap(found.reshape(owners, SLOTS, width), DP).reshape(slots, width)
    (owned,) = call(owned_kernel, [((own_rows, slots), BF16)], (asked,))
    outgoing, inputs, dhidden, hot_dx, head = call(
        layer_kernel,
        [
            ((slots, width), BF16),
            ((samples, inputs_width), BF16),
            ((samples, hidden_width), BF16),
            ((samples * feats, width), BF16),
            ((8, BLOCK), F32),
        ],
        (returned, target, target_rows, hot_in, top_weight, out_held, label),
        held=(1, 2, 3, 5, 6),
        kept=(1, 2, 3, 4),
    )
    half = inputs_width // 2
    broad = hidden_width + BLOCK
    packed = broad + 2 * BLOCK
    near = lax.axis_size("dp_1")
    far = lax.axis_size("dp_0")
    plane_size = lax.axis_size(PLANE)
    send, picked, pending_new = call(
        send_kernel,
        [((half, packed), I16), ((plane_size * far, BLOCK), F32), ((hot_count, width), F32)],
        (control, inputs, dhidden, hot_id_rows, hot_dx, head, pending),
        smem=1,
        held=(1, 2, 3, 4, 5),
        kept=(1, 2),
        scratch=[((REFRESHED * BLOCK, BLOCK), F32)],
        flops=10**9,
    )
    send, outgoing = lax.optimization_barrier((send, outgoing))
    received = lax.ppermute(send, "dp_2", [(0, 1), (1, 0)])
    incoming = swap(outgoing.reshape(owners, SLOTS, width), DP).reshape(slots, width)
    pieces = call(
        pair_kernel,
        [((half // 4, broad), F32)] + [((half // 4, packed), I16)] * 3,
        (control, inputs, dhidden, picked, received),
        smem=1,
        held=(1, 2, 3),
    )
    two, one, three = (from_rep(pieces[d], d) for d in (2, 1, 3))
    (paired,) = call(four_kernel, [((half // 4, packed), I16)], (pieces[0], two, one, three))
    paired, incoming = lax.optimization_barrier((paired, incoming))
    plane = swap(paired.reshape(near, far, packed), "dp_1")
    tall = hidden_width // BLOCK
    (columns,) = call(plane_kernel, [((far * SENT, BLOCK), jnp.int32)], (plane,))
    columns = swap(columns.reshape(far, 1, SENT * BLOCK), "dp_0").reshape(far * SENT, BLOCK)
    top, copies = call(column_kernel, [((tall, BLOCK), F32), ((plane_size * HELD, BLOCK), F32)], (columns,))
    sums = swap(copies.reshape(plane_size, 1, HELD * BLOCK), PLANE).reshape(plane_size * HELD, BLOCK)

    (grad,) = call(cold_kernel, [((own_rows, width), F32)], (owned, incoming))
    (grad,) = call(two_kernel, [((own_rows, width), F32)], (grad, from_rep(grad, 1)))
    cold_table_new, cold_accum_new = call(
        update_kernel, [((own_rows, width), F32)] * 2, (grad, from_rep(grad, 3), cold_table, cold_accum)
    )
    hot_cache_new, hot_accum_new, out_grad = call(
        hot_kernel,
        [((hot_count, width), F32)] * 2 + [((8, BLOCK), F32)],
        (control, sums, hot_cache, hot_accum),
        smem=1,
        scratch=[((REFRESHED * BLOCK, BLOCK), F32)],
    )
    return (
        cold_table_new,
        cold_accum_new,
        hot_cache_new,
        hot_accum_new,
        pending_new,
        top.reshape(1, hidden_width),
        out_grad.reshape(hidden_width),
    )


def solution(mesh):
    split = Mesh(mesh.devices.reshape(16, 4, 2, mesh.shape["rep"]), ("dp_0", "dp_1", "dp_2", "rep"))
    in_specs = (
        P(DP_REP, None),
        P(DP_REP, None),
        P(DP_REP),
        P(DP_REP),
        P(),
        P(),
        P(DP, None),
        P(DP, None),
        P(),
        P(),
        P(DP_REP, None),
        P(),
        P(),
    )
    out_specs = (P(DP, None), P(DP, None), P(), P(), P(DP_REP, None), P(DP_REP, None), P())
    return jax.shard_map(local, mesh=split, in_specs=in_specs, out_specs=out_specs, check_vma=False)
```

```python
import jax
import jax.numpy as jnp
from jax import lax
from jax.experimental import pallas as pl
from jax.experimental.pallas import tpu as pltpu
from jax.sharding import Mesh
from jax.sharding import PartitionSpec as P

BLOCK = 128
SLOTS = 8
REFRESHED = 3
DP = ("dp_0", "dp_1", "dp_2")
DP_REP = ("dp_0", "dp_1", "dp_2", "rep")
PLANE = ("dp_2", "rep", "dp_1")

step_size = 0.5
epsilon = 1e-08

F32 = jnp.float32
BF16 = jnp.bfloat16
I16 = jnp.int16
LN2 = 0.6931471805599453
FINE = 65534.0
SENT = 18
HELD = 13
EXACT = lax.Precision.HIGHEST
VMEM = pl.BlockSpec(memory_space=pltpu.VMEM)
HBM = pl.BlockSpec(memory_space=pltpu.HBM)
SMEM = pl.BlockSpec(memory_space=pltpu.SMEM)


class Loaded:
    def __init__(self, source, held, sem):
        self.copy = pltpu.make_async_copy(source, held, sem)
        self.held = held
        self.copy.start()

    def wait(self):
        self.copy.wait()
        return self.held


def call(kernel, outs, args, smem=0, scratch=(), loads=(), held=(), kept=(), flops=10**9):
    own = len(scratch)
    ins = len(args)

    def body(*refs):
        given = list(refs[:ins])
        rest = refs[ins + len(outs) :]
        for j, i in enumerate(loads):
            given[i] = Loaded(given[i], rest[own + j], rest[own + len(loads) + j])
        kernel(*given, *refs[ins : ins + len(outs)], *rest[:own])

    specs = [SMEM] * smem + [VMEM] * (ins - smem)
    args = list(args)
    for i in loads:
        specs[i] = HBM
        args[i] = pltpu.with_memory_space_constraint(args[i], pltpu.HBM)
    for i in held:
        args[i] = pltpu.with_memory_space_constraint(args[i], pltpu.VMEM)
    return pl.pallas_call(
        body,
        out_shape=[(pltpu.VMEM if i in kept else jax.ShapeDtypeStruct)(s, d) for i, (s, d) in enumerate(outs)],
        in_specs=specs,
        out_specs=[VMEM] * len(outs),
        scratch_shapes=[pltpu.VMEM(s, d) for s, d in scratch]
        + [pltpu.VMEM(args[i].shape, args[i].dtype) for i in loads]
        + [pltpu.SemaphoreType.DMA for _ in loads],
        compiler_params=pltpu.CompilerParams(vmem_limit_bytes=16 * 2**20),
        cost_estimate=pl.CostEstimate(flops=flops, bytes_accessed=flops // 100, transcendentals=0),
    )(*args)


def iota(shape, dim):
    return lax.broadcasted_iota(jnp.int32, shape, dim)


def iota_f(shape, dim):
    return iota(shape, dim).astype(F32)


def ones_where(mask):
    return jnp.where(mask, 1.0, 0.0).astype(BF16)


def column_of(row, eye):
    return jnp.sum(jnp.where(eye, row, 0.0), axis=1, keepdims=True)


def dot(a, b, precision=None):
    return jnp.dot(a, b, preferred_element_type=F32, precision=precision)


def dot_t(a, b):
    return lax.dot_general(a, b, (((1,), (1,)), ((), ())), preferred_element_type=F32)


def power(exponent):
    return jnp.exp(exponent * LN2)


def exponent_of(top):
    return jnp.ceil(jnp.log(jnp.maximum(top, 1e-30)) * (1.0 / LN2) + 0.01) - 15.0


def pack(values, packed_ref):
    wide = values.shape[1] - BLOCK
    top, hot = values[:, :wide], values[:, wide:]
    top_exponent = exponent_of(jnp.max(jnp.abs(top), axis=1, keepdims=True))
    hot_exponent = exponent_of(jnp.max(jnp.abs(hot), axis=1, keepdims=True))
    lane = iota((values.shape[0], BLOCK), 1)
    hot = hot * power(-hot_exponent)
    coarse = jnp.round(hot)
    at = 0
    for part in (
        jnp.round(top * power(-top_exponent)),
        coarse,
        jnp.round((hot - coarse) * FINE),
        jnp.where(lane < BLOCK // 2, top_exponent, hot_exponent),
    ):
        packed_ref[:, at : at + part.shape[1]] = part.astype(jnp.int32).astype(I16)
        at += part.shape[1]


def unpack(packed):
    values = packed.astype(jnp.int32).astype(F32)
    wide = values.shape[1] - 3 * BLOCK
    coarse, fine, exponents = (values[:, wide + i * BLOCK : wide + (i + 1) * BLOCK] for i in range(3))
    top = values[:, :wide] * power(exponents[:, :1])
    hot = (coarse + fine * (1.0 / FINE)) * power(exponents[:, BLOCK - 1 :])
    return jnp.concatenate([top, hot], axis=1)


def requests_kernel(owner_ref, offset_ref, request_ref, target_ref):
    square = (BLOCK, BLOCK)
    owner = owner_ref.wait()[...].astype(F32)
    offset = offset_ref.wait()[...].astype(F32)
    groups = owner.shape[0]
    lookups = groups * BLOCK
    columns = jnp.transpose(jnp.concatenate([owner, offset], axis=0))
    owner_col = jnp.concatenate([columns[:, s : s + 1] for s in range(groups)], axis=0)
    offset_col = jnp.concatenate([columns[:, groups + s : groups + s + 1] for s in range(groups)], axis=0)
    lane = iota_f((lookups, BLOCK), 1)
    named = owner_col == lane
    before = ones_where(iota(square, 0) > iota(square, 1))
    counts = jnp.where(named, 1.0, 0.0)
    earlier = []
    so_far = jnp.zeros((1, BLOCK), F32)
    for s in range(groups):
        block = counts[s * BLOCK : (s + 1) * BLOCK]
        earlier.append(dot(before, block.astype(BF16)) + so_far)
        so_far = so_far + jnp.sum(block, axis=0, keepdims=True)
    rank = jnp.sum(jnp.where(named, jnp.concatenate(earlier, axis=0), 0.0), axis=1, keepdims=True)
    target_ref[...] = jnp.broadcast_to(owner_col * SLOTS + rank, (lookups, BLOCK))
    high = jnp.where(offset_col >= 256.0, 1.0, 0.0)
    placed = jnp.where(rank == lane, offset_col - 256.0 * high, jnp.where(rank == lane - SLOTS, high, 0.0))
    sublane = iota_f(square, 0)
    named_t = jnp.concatenate([ones_where(sublane == owner[s : s + 1, :]) for s in range(groups)], axis=1)
    request_ref[...] = dot(named_t, placed.astype(BF16))


def rows_kernel(asked_ref, table_ref, rows_ref, wide_ref):
    asked = asked_ref[:, :SLOTS] + 256.0 * asked_ref[:, SLOTS : 2 * SLOTS]
    table = table_ref[...]
    sources = asked.shape[0]
    line = iota_f((sources, table.shape[0]), 1)
    for slot in range(SLOTS):
        chosen = ones_where(asked[:, slot : slot + 1] == line)
        wide_ref[pl.ds(slot, sources, stride=SLOTS), :] = dot(chosen, table)
    rows_ref[...] = wide_ref[...].astype(BF16)


def owned_kernel(asked_ref, owned_ref):
    slots = owned_ref.shape[1]
    source, line = iota((BLOCK, slots), 0), iota((BLOCK, slots), 1)
    slot = line % SLOTS
    worth = jnp.where(source == slot, 1.0, jnp.where(source == slot + SLOTS, 256.0, 0.0))
    spread = dot(asked_ref[...], worth, EXACT)
    wanted = jnp.sum(jnp.where(source == line // SLOTS, spread, 0.0), axis=0, keepdims=True)
    owned_ref[...] = ones_where(iota_f(owned_ref.shape, 0) == wanted)


def masks_kernel(
    target_ref, hot_ref, cache_ref, table_ref, labels_ref, out_weight_ref,
    rows_ref, hot_in_ref, hot_rows_ref, narrow_ref, label_ref, out_held_ref,
):
    square = (BLOCK, BLOCK)
    eye = iota(square, 0) == iota(square, 1)
    hot = hot_ref.wait()[...].astype(F32)
    feats, samples = hot.shape
    for k in range(feats):
        mine = target_ref[pl.ds(k, samples, stride=feats), :]
        for h in range(samples // BLOCK):
            at = k * samples + h * BLOCK
            row = jnp.sum(jnp.where(eye, mine[h * BLOCK : (h + 1) * BLOCK, :], 0.0), axis=0, keepdims=True)
            rows_ref[:, at : at + BLOCK] = jnp.broadcast_to(row, (8, BLOCK))
    cache = cache_ref.wait()[...].astype(BF16)
    hot_count = cache.shape[0]
    hot_lane = iota_f((BLOCK, hot_count), 1)
    for k in range(feats):
        for h in range(samples // BLOCK):
            at = k * samples + h * BLOCK
            row = hot[k : k + 1, h * BLOCK : (h + 1) * BLOCK]
            hot_rows_ref[:, at : at + BLOCK] = jnp.broadcast_to(row, (8, BLOCK))
            chosen = ones_where(column_of(row, eye) == hot_lane)
            hot_in_ref[h * BLOCK : (h + 1) * BLOCK, k * BLOCK : (k + 1) * BLOCK] = dot(chosen, cache).astype(BF16)
    narrow_ref[...] = table_ref.wait()[...].astype(BF16)
    labels = labels_ref.wait()[...].astype(F32)
    for h in range(labels.shape[0]):
        column = column_of(labels[h : h + 1, :], eye)
        label_ref[h * BLOCK : (h + 1) * BLOCK, :] = jnp.broadcast_to(column, (BLOCK, BLOCK))
    out_held_ref[...] = out_weight_ref.wait()[...]


def layer_kernel(
    returned_ref, target_ref, rows_ref, hot_in_ref, weight_ref, out_weight_ref, label_ref,
    outgoing_ref, inputs_ref, dhidden_ref, hot_dx_ref, head_ref,
):
    width = BLOCK
    samples = target_ref.shape[0] // 2
    lane = iota_f((samples, BLOCK), 1)
    slots = returned_ref.shape[0]
    mine = [target_ref[pl.ds(k, samples, stride=2), :] for k in range(2)]
    take = [
        jnp.concatenate([ones_where(t == lane + float(b)) for b in range(0, slots, BLOCK)], axis=1) for t in mine
    ]
    cold = dot(jnp.concatenate(take, axis=0), returned_ref[...]).astype(BF16)
    inputs = jnp.concatenate([hot_in_ref[...], cold[:samples], cold[samples:]], axis=1)
    inputs_ref[...] = inputs
    weight = weight_ref[...]
    out_weight = out_weight_ref[...]
    preact = dot(inputs, weight)
    gates = jax.nn.sigmoid(preact)
    hidden = (preact * gates).astype(BF16).astype(F32)
    logits = jnp.sum(hidden * out_weight, axis=1, keepdims=True)
    label = label_ref[:, :1]
    errors = jax.nn.sigmoid(logits) - label
    slope = gates * (1.0 + preact * (1.0 - gates))
    dhidden = (errors * out_weight * slope).astype(BF16)
    dhidden_ref[...] = dhidden
    dinputs = dot_t(dhidden, weight).astype(BF16)
    cold_dx = jnp.concatenate([dinputs[:, 2 * width : 3 * width], dinputs[:, 3 * width :]], axis=0)
    put = ones_where(iota_f((outgoing_ref.shape[0], rows_ref.shape[1]), 0) == rows_ref[:1, :])
    outgoing_ref[...] = dot(put, cold_dx).astype(BF16)
    hot_dx_ref[:samples, :] = dinputs[:, :width]
    hot_dx_ref[samples:, :] = dinputs[:, width : 2 * width]
    head = jnp.sum(errors * hidden, axis=0, keepdims=True)
    for b in range(head_ref.shape[0]):
        head_ref[b : b + 1, :] = head[:, b * BLOCK : (b + 1) * BLOCK]


def half_of_top(core, rep, inputs, dhidden):
    wide = inputs.shape[1]
    shape = (wide // 2, BLOCK)
    line = iota(shape, 0)
    row = (line & 15) * 32 + ((line >> 4) & 3) * 8 + core * 4 + ((line >> 6) ^ rep)
    lane = iota(shape, 1)
    order = jnp.concatenate([ones_where(row == lane + b) for b in range(0, wide, BLOCK)], axis=1)
    ordered = dot_t(order, inputs).astype(BF16)
    return dot(ordered, dhidden)


def hot_rows(picked_ref, core, rep, piece):
    count = picked_ref.shape[0] // 8
    return picked_ref[pl.ds(pl.multiple_of((core * 4 + (rep ^ piece)) * count, count), count), :]


def send_kernel(
    control_ref, inputs_ref, dhidden_ref, hot_rows_ref, hot_dx_ref, head_ref, pending_ref,
    send_ref, picked_ref, pending_new_ref, flat_ref,
):
    put = ones_where(iota_f((pending_ref.shape[0], hot_rows_ref.shape[1]), 0) == hot_rows_ref[:1, :])
    pending_new_ref[...] = dot(put, hot_dx_ref[...]) + pending_ref[...]
    count = REFRESHED
    blocks = [pl.ds(pl.multiple_of(control_ref[2 + i] * BLOCK, BLOCK), BLOCK) for i in range(count)]
    for i, at in enumerate(blocks):
        flat_ref[i * BLOCK : (i + 1) * BLOCK, :] = pending_new_ref[at, :]
    rows = HELD - 1
    count = picked_ref.shape[0] // 16
    part = iota((1, BLOCK), 1) // (8 * BLOCK // count)
    for i in range(count):
        at = i * 16
        q, p = divmod(i, count // 8)
        picked_ref[at : at + rows, :] = flat_ref[i * rows : (i + 1) * rows, :]
        picked_ref[at + rows : at + HELD, :] = jnp.where(part == p, head_ref[q : q + 1, :], 0.0)
        picked_ref[at + HELD : at + 16, :] = jnp.zeros((16 - HELD, BLOCK), F32)
    for at in blocks:
        pending_new_ref[at, :] = jnp.zeros((BLOCK, BLOCK), F32)
    core, rep = 1 - control_ref[0], control_ref[1]
    top = half_of_top(core, rep, inputs_ref[...], dhidden_ref[...])
    hot = jnp.concatenate([hot_rows(picked_ref, core, rep, d) for d in range(4)], axis=0)
    pack(jnp.concatenate([top, hot], axis=1), send_ref)


def pair_kernel(control_ref, inputs_ref, dhidden_ref, picked_ref, received_ref, own_ref, *pieces):
    core, rep = control_ref[0], control_ref[1]
    top = half_of_top(core, rep, inputs_ref[...], dhidden_ref[...])
    tall = own_ref.shape[0]
    for d, piece in enumerate((own_ref, *pieces)):
        rows = slice(d * tall, (d + 1) * tall)
        mine = jnp.concatenate([top[rows], hot_rows(picked_ref, core, rep, d)], axis=1)
        both = mine + unpack(received_ref[rows, :])
        if d:
            pack(both, piece)
        else:
            piece[...] = both


def four_kernel(own_ref, two_ref, one_ref, three_ref, sum_ref):
    total = (own_ref[...] + unpack(one_ref[...])) + (unpack(two_ref[...]) + unpack(three_ref[...]))
    pack(total, sum_ref)


def plane_kernel(parts_ref, out_ref):
    total = unpack(parts_ref[0])
    for i in range(1, parts_ref.shape[0]):
        total = total + unpack(parts_ref[i])
    count = total.shape[0]
    wide = total.shape[1] - BLOCK
    top, hot = total[:, :wide], total[:, wide:]
    top_exponent = exponent_of(jnp.max(jnp.abs(top), axis=1, keepdims=True))
    top = jnp.round(top * power(-top_exponent)).astype(jnp.int32)
    pairs = (top[:, : wide // 2] & 65535) | (top[:, wide // 2 :] << 16)
    most = jnp.max(jnp.max(jnp.abs(hot), axis=1, keepdims=True), axis=0, keepdims=True)
    hot_exponent = exponent_of(jnp.maximum(most, 1e-20)) - 15.0
    hot = jnp.round(hot * power(-hot_exponent)).astype(jnp.int32)
    lane = iota((count, BLOCK), 1)
    rows = [pairs[:, b : b + BLOCK] for b in range(0, wide // 2, BLOCK)]
    rows += [jnp.broadcast_to(hot[r : r + 1], (count, BLOCK)) for r in range(HELD)]
    rows += [jnp.where(lane < BLOCK // 2, top_exponent, hot_exponent).astype(jnp.int32)]
    for r, row in enumerate(rows):
        out_ref[pl.ds(r, count, stride=SENT), :] = row


def column_kernel(parts_ref, top_ref, copies_ref):
    tall = top_ref.shape[0] // 2
    low, high = jnp.zeros((tall, BLOCK), F32), jnp.zeros((tall, BLOCK), F32)
    hot = jnp.zeros((HELD, BLOCK), F32)
    for i in range(parts_ref.shape[0] // SENT):
        at = i * SENT
        scale = power(parts_ref[at + SENT - 1 : at + SENT, :].astype(F32))
        pairs = parts_ref[at : at + tall, :]
        low = low + ((pairs << 16) >> 16).astype(F32) * scale[:, :1]
        high = high + (pairs >> 16).astype(F32) * scale[:, :1]
        hot = hot + parts_ref[at + tall : at + tall + HELD, :].astype(F32) * scale[:, BLOCK - 1 :]
    top_ref[:tall, :] = low
    top_ref[tall:, :] = high
    for i in range(copies_ref.shape[0] // HELD):
        copies_ref[i * HELD : (i + 1) * HELD, :] = hot


def adagrad(table_rows, accum_rows, gradient):
    accum_next = accum_rows + gradient * gradient
    return (table_rows - step_size * gradient / (jnp.sqrt(accum_next) + epsilon), accum_next)


def hot_kernel(control_ref, sums_ref, cache_ref, accum_ref, cache_new_ref, accum_new_ref, out_grad_ref, flat_ref):
    cache_new_ref[...] = cache_ref[...]
    accum_new_ref[...] = accum_ref[...]
    rows = HELD - 1
    pieces = sums_ref.shape[0] // HELD
    for i in range(pieces):
        flat_ref[i * rows : (i + 1) * rows, :] = sums_ref[i * HELD : i * HELD + rows, :]
    for q in range(8):
        parts = [sums_ref[i * HELD + rows : (i + 1) * HELD, :] for i in range(q * pieces // 8, (q + 1) * pieces // 8)]
        out_grad_ref[q : q + 1, :] = sum(parts[1:], parts[0])
    count = REFRESHED
    for i in range(count):
        block = control_ref[2 + i]
        at = pl.ds(pl.multiple_of(block * BLOCK, BLOCK), BLOCK)
        flush = flat_ref[i * BLOCK : (i + 1) * BLOCK, :] / (1.0 + control_ref[2 + count + block].astype(F32))
        cache_next, accum_next = adagrad(cache_ref[at, :], accum_ref[at, :], flush)
        cache_new_ref[at, :] = cache_next
        accum_new_ref[at, :] = accum_next


def cold_kernel(owned_ref, incoming_ref, grad_ref):
    grad_ref[...] = dot(owned_ref[...], incoming_ref[...])


def two_kernel(own_ref, other_ref, sum_ref):
    sum_ref[...] = own_ref[...] + other_ref[...]


def update_kernel(own_ref, other_ref, table_ref, accum_ref, table_new_ref, accum_new_ref):
    table_next, accum_next = adagrad(table_ref[...], accum_ref[...], own_ref[...] + other_ref[...])
    table_new_ref[...] = table_next
    accum_new_ref[...] = accum_next


def swap(x, axis):
    return lax.all_to_all(x, axis, split_axis=0, concat_axis=0, tiled=True)


def from_rep(piece, distance):
    return lax.ppermute(piece, "rep", [(i, i ^ distance) for i in range(4)])


def local(
    hot_ids,
    cold_owner,
    cold_offset,
    labels,
    top_weight,
    out_weight,
    cold_table,
    cold_accum,
    hot_cache,
    hot_accum,
    pending,
    refresh_blocks,
    block_clock,
):
    samples, feats = hot_ids.shape
    lookups = cold_offset.shape[0]
    own_rows, width = cold_table.shape
    hot_count = hot_cache.shape[0]
    inputs_width, hidden_width = top_weight.shape
    owners = lax.axis_size(DP)
    slots = owners * SLOTS
    groups = lookups // BLOCK
    place = jnp.stack([lax.axis_index("dp_2"), lax.axis_index("rep")]).astype(jnp.int32)
    control = jnp.concatenate([place, refresh_blocks, block_clock])

    request, target = call(
        requests_kernel,
        [((owners, BLOCK), F32), ((lookups, BLOCK), F32)],
        (cold_owner.reshape(groups, BLOCK), cold_offset.reshape(groups, BLOCK)),
        loads=(0, 1),
        kept=(1,),
    )
    asked = swap(request.reshape(owners, 1, BLOCK), DP).reshape(owners, BLOCK)
    target_rows, hot_in, hot_id_rows, narrow, label, out_held = call(
        masks_kernel,
        [
            ((8, lookups), F32),
            ((samples, feats * width), BF16),
            ((8, samples * feats), F32),
            ((own_rows, width), BF16),
            ((samples, BLOCK), F32),
            ((1, hidden_width), F32),
        ],
        (target, hot_ids.T, hot_cache, cold_table, labels.reshape(2, BLOCK), out_weight.reshape(1, hidden_width)),
        loads=(1, 2, 3, 4, 5),
        held=(0,),
        kept=(0, 1, 2, 3, 4, 5),
    )
    (found,) = call(rows_kernel, [((slots, width), BF16)], (asked, narrow), held=(1,), scratch=[((slots, width), F32)])
    returned = swap(found.reshape(owners, SLOTS, width), DP).reshape(slots, width)
    (owned,) = call(owned_kernel, [((own_rows, slots), BF16)], (asked,))
    outgoing, inputs, dhidden, hot_dx, head = call(
        layer_kernel,
        [
            ((slots, width), BF16),
            ((samples, inputs_width), BF16),
            ((samples, hidden_width), BF16),
            ((samples * feats, width), BF16),
            ((8, BLOCK), F32),
        ],
        (returned, target, target_rows, hot_in, top_weight, out_held, label),
        held=(1, 2, 3, 5, 6),
        kept=(1, 2, 3, 4),
    )
    half = inputs_width // 2
    broad = hidden_width + BLOCK
    packed = broad + 2 * BLOCK
    near = lax.axis_size("dp_1")
    far = lax.axis_size("dp_0")
    plane_size = lax.axis_size(PLANE)
    send, picked, pending_new = call(
        send_kernel,
        [((half, packed), I16), ((plane_size * far, BLOCK), F32), ((hot_count, width), F32)],
        (control, inputs, dhidden, hot_id_rows, hot_dx, head, pending),
        smem=1,
        held=(1, 2, 3, 4, 5),
        kept=(1, 2),
        scratch=[((REFRESHED * BLOCK, BLOCK), F32)],
        flops=10**9,
    )
    send, outgoing = lax.optimization_barrier((send, outgoing))
    received = lax.ppermute(send, "dp_2", [(0, 1), (1, 0)])
    incoming = swap(outgoing.reshape(owners, SLOTS, width), DP).reshape(slots, width)
    pieces = call(
        pair_kernel,
        [((half // 4, broad), F32)] + [((half // 4, packed), I16)] * 3,
        (control, inputs, dhidden, picked, received),
        smem=1,
        held=(1, 2, 3),
    )
    two, one, three = (from_rep(pieces[d], d) for d in (2, 1, 3))
    (paired,) = call(four_kernel, [((half // 4, packed), I16)], (pieces[0], two, one, three))
    paired, incoming = lax.optimization_barrier((paired, incoming))
    plane = swap(paired.reshape(near, far, packed), "dp_1")
    tall = hidden_width // BLOCK
    (grad,) = call(cold_kernel, [((own_rows, width), F32)], (owned, incoming))
    plane, grad = lax.optimization_barrier((plane, grad))
    (columns,) = call(plane_kernel, [((far * SENT, BLOCK), jnp.int32)], (plane,))
    columns = swap(columns.reshape(far, 1, SENT * BLOCK), "dp_0").reshape(far * SENT, BLOCK)
    top, copies = call(column_kernel, [((tall, BLOCK), F32), ((plane_size * HELD, BLOCK), F32)], (columns,))
    sums = swap(copies.reshape(plane_size, 1, HELD * BLOCK), PLANE).reshape(plane_size * HELD, BLOCK)

    (grad,) = call(two_kernel, [((own_rows, width), F32)], (grad, from_rep(grad, 1)))
    cold_table_new, cold_accum_new = call(
        update_kernel, [((own_rows, width), F32)] * 2, (grad, from_rep(grad, 3), cold_table, cold_accum)
    )
    hot_cache_new, hot_accum_new, out_grad = call(
        hot_kernel,
        [((hot_count, width), F32)] * 2 + [((8, BLOCK), F32)],
        (control, sums, hot_cache, hot_accum),
        smem=1,
        scratch=[((REFRESHED * BLOCK, BLOCK), F32)],
    )
    return (
        cold_table_new,
        cold_accum_new,
        hot_cache_new,
        hot_accum_new,
        pending_new,
        top.reshape(1, hidden_width),
        out_grad.reshape(hidden_width),
    )


def solution(mesh):
    split = Mesh(mesh.devices.reshape(16, 4, 2, mesh.shape["rep"]), ("dp_0", "dp_1", "dp_2", "rep"))
    in_specs = (
        P(DP_REP, None),
        P(DP_REP, None),
        P(DP_REP),
        P(DP_REP),
        P(),
        P(),
        P(DP, None),
        P(DP, None),
        P(),
        P(),
        P(DP_REP, None),
        P(),
        P(),
    )
    out_specs = (P(DP, None), P(DP, None), P(), P(), P(DP_REP, None), P(DP_REP, None), P())
    return jax.shard_map(local, mesh=split, in_specs=in_specs, out_specs=out_specs, check_vma=False)
```
